256 devices in a mesh: heads: 4 (over x), seq: 64 (over z, y, core).
Axes of the slice: x: 4, y: 4, z: 8, core: 2. Of those that a mesh axis runs over, the one named last changes fastest.
Arguments:
- queries: bfloat16 [49152, 2048], P('seq', 'heads'), may hold values from -6 to 6
- key_vectors: bfloat16 [49152, 2048], P('seq', 'heads'), may hold values from -10 to 10
- value_vectors: bfloat16 [49152, 2048], P('seq', 'heads'), may hold values from -6 to 6
- random_blocks: int32 [16, 768, 3], P('heads', 'seq'), may hold values from 0 to 767, as said below
- global_blocks: int32 [2], replicated, may hold values from 0 to 767, as said below
- out_weight: bfloat16 [2048, 4096], P('heads'), may hold values from -0.1875 to 0.1875
Outputs:
- layer_out: bfloat16 [49152, 4096], P('seq', 'heads')
The draws below stay inside these ranges and needn't reach their ends.
Inputs may be any that keep to these rules, and one draw needn't show every extreme that they name: `random_blocks`: entries are block numbers. Of the entries with heads of one group of 4 and query blocks of one run of 12 blocks, at most 4 lie in any one run of key blocks s * 12 to (s + 1) * 12 - 1, and exactly 4 lie in one such run. Entries may repeat. `global_blocks`: Distinct; the last entry is the last block, 767.
All inputs are finite; a program needn't handle non-finite values.
Results may differ from the reference program's by a relative error of at most 0.0095.
Values may be sent and summed in bfloat16 or wider, within the bound.
No kernel may reach another device: no remote copies, remote signals or barrier semaphores. Data moves between devices by JAX's collectives and lax.ppermute only.
A program may use at most 128 MiB of HBM per device.

```python
import jax
import jax.numpy as jnp
from jax import lax

D = 4096
HEADS = 16
DH = 128
BLOCK = 64
RANDOM = 3
GLOBAL = 2
HEAD_GROUPS = 4
SHARDS = 64
HEADS_DEV = 4
BLOCKS_DEV = 12
BLOCKS_ALL = 768
TOKENS = 49152
REQUESTS = 144
CAPACITY = 4
N_HEADS = 4


def global_pick(key):
    ordering = jax.random.permutation(jax.random.fold_in(key, 7), BLOCKS_ALL - 1)
    chosen = ordering[:GLOBAL - 1].astype(jnp.int32)
    last_block = jnp.full((1,), BLOCKS_ALL - 1, jnp.int32)
    return jnp.concatenate([chosen, last_block]).astype(jnp.int32)


def draw_global_blocks(key, part):
    return global_pick(key)


def draw_queries(key, part):
    drawn = jnp.clip(jax.random.normal(jax.random.fold_in(key, 21), (TOKENS, HEADS * DH), jnp.float32), -6.0, 6.0)
    return drawn.astype(jnp.bfloat16)


def draw_key_vectors(key, part):
    drawn = jax.random.normal(jax.random.fold_in(key, 22), (TOKENS, HEADS * DH), jnp.float32)
    drawn = jnp.clip(2.0 * drawn, -10.0, 10.0)
    return drawn.astype(jnp.bfloat16)


def device_lists(key):
    tickets = jnp.arange(SHARDS * CAPACITY, dtype=jnp.int32) // CAPACITY
    busiest = jax.random.randint(jax.random.fold_in(key, 1), (), 0, SHARDS).astype(jnp.int32)
    shuffled = jax.random.permutation(jax.random.fold_in(key, 2), SHARDS * CAPACITY).astype(jnp.int32)
    ranking = shuffled - jnp.where(tickets == busiest, SHARDS * CAPACITY, 0).astype(jnp.int32)
    ordering = jnp.argsort(ranking)
    owners = tickets[ordering[:REQUESTS]]
    owners = owners[jax.random.permutation(jax.random.fold_in(key, 3), REQUESTS)]
    local_ids = jax.random.randint(jax.random.fold_in(key, 4), (REQUESTS,), 0, BLOCKS_DEV).astype(jnp.int32)
    return (owners * BLOCKS_DEV + local_ids).reshape(HEADS_DEV, BLOCKS_DEV, RANDOM)


def draw_random_blocks(key, part):
    devices = HEAD_GROUPS * SHARDS
    device_keys = jax.vmap(lambda number: jax.random.fold_in(key, number))(jnp.arange(devices))
    tables = jax.vmap(device_lists)(device_keys)
    tables = tables.reshape(HEAD_GROUPS, SHARDS, HEADS_DEV, BLOCKS_DEV, RANDOM).transpose(0, 2, 1, 3, 4)
    return tables.reshape(HEADS, BLOCKS_ALL, RANDOM).astype(jnp.int32)


def with_spikes(values, stream_key, source, target, blocks, factor):
    owner, partner = [(jnp.arange(values.shape[dim]) // (values.shape[dim] // blocks)).reshape([-1 if axis == dim else 1 for axis in range(values.ndim)]) for dim in (source, target)]
    chosen = jax.random.permutation(stream_key, blocks)[partner]
    strong = (owner == chosen) | (owner == (partner + blocks // 2) % blocks)
    return jnp.where(strong, factor * values, values)


def level_of(own_key, dims, split, smallest, high):
    level = 1.0
    for axis_at, parts in split:
        steps = jax.random.uniform(jax.random.fold_in(jax.random.fold_in(own_key, 6), axis_at), (parts,), jnp.float32, smallest / len(split), high / len(split))
        level = level * jnp.repeat(jnp.exp(steps), dims[axis_at] // parts).reshape((-1,) + (1,) * (len(dims) - 1 - axis_at))
    return level


def scatter_about(stream_key, dims, deviation, bound, shards=(), kind=jnp.bfloat16):
    loudness = level_of(stream_key, dims, shards, -0.22, 0.18) if shards else 1.0
    values = jax.random.normal(stream_key, dims, jnp.float32) * deviation * loudness
    return jnp.minimum(jnp.maximum(values, -bound), bound).astype(kind)


def noise_with(own_key, extent, deviation, limit, cuts, heavy, kind=jnp.bfloat16):
    values = deviation * jax.random.normal(own_key, extent, jnp.float32)
    if cuts:
        values = values * level_of(own_key, extent, cuts, -0.22, 0.18)
    return jnp.clip(with_spikes(values, jax.random.fold_in(own_key, 3), *heavy), -limit, limit).astype(kind)


def setup_inputs(seed: int = 0) -> dict:
    splits = jax.random.split(jax.random.key(seed), 7)
    return {
        "queries": draw_queries(jax.random.fold_in(splits[6], 71), 0),
        "key_vectors": draw_key_vectors(jax.random.fold_in(splits[6], 71), 0),
        "value_vectors": scatter_about(splits[2], (TOKENS, HEADS * DH), 1.0, 6.0, ((0, 64), (1, 4))),
        "random_blocks": draw_random_blocks(jax.random.fold_in(splits[6], 71), 0),
        "global_blocks": draw_global_blocks(jax.random.fold_in(splits[6], 71), 0),
        "out_weight": noise_with(splits[5], (HEADS * DH, D), (HEADS * DH) ** -0.5, 0.1875, ((0, 4),), (0, 1, 4, 2.0)),
    }


def head_attention(operands, global_blocks):
    q_head, k_head, v_head, rand_head = operands
    block_count = q_head.shape[0] // BLOCK
    score_multiplier = DH ** -0.5
    query_block_tiles = q_head.reshape(block_count, BLOCK, DH)
    k_tiles = k_head.reshape(block_count, BLOCK, DH)
    v_tiles = v_head.reshape(block_count, BLOCK, DH)

    def gather_keys(tiles):
        zero_tile = jnp.zeros((1, BLOCK, DH), tiles.dtype)
        padded = jnp.concatenate([zero_tile, tiles, zero_tile], axis=0)
        window = jnp.stack([padded[:-2], padded[1:-1], padded[2:]], axis=1)
        random_part = tiles[rand_head]
        global_part = jnp.broadcast_to(tiles[global_blocks][None], (block_count, GLOBAL, BLOCK, DH))
        joined = jnp.concatenate([window, random_part, global_part], axis=1)
        return joined.reshape(block_count, -1, DH)

    window_key_rows = gather_keys(k_tiles)
    window_value_rows = gather_keys(v_tiles)
    logit_scores = jnp.einsum("hmo,hzo->hmz", query_block_tiles.astype(jnp.float32), window_key_rows.astype(jnp.float32)) * score_multiplier
    column_block = jnp.arange(window_key_rows.shape[1]) // BLOCK
    row_block = jnp.arange(block_count)
    valid_keys = jnp.where(column_block[None, :] == 0, row_block[:, None] > 0,
                           jnp.where(column_block[None, :] == 2, row_block[:, None] < block_count - 1, True))
    logit_scores = jnp.where(valid_keys[:, None, :], logit_scores, -jnp.inf)
    row_peak = jnp.max(logit_scores, axis=-1, keepdims=True)
    exponent = jnp.exp(logit_scores - row_peak)
    softmax_divisor = jnp.sum(exponent, axis=-1, keepdims=True)
    rounded_scores = lax.optimization_barrier(exponent.astype(jnp.bfloat16))
    sparse_result = jnp.einsum("afg,agv->afv", rounded_scores.astype(jnp.float32), window_value_rows.astype(jnp.float32)) / softmax_divisor
    sparse_result = sparse_result.astype(jnp.bfloat16)
    global_query = query_block_tiles[global_blocks].reshape(GLOBAL * BLOCK, DH)
    global_scores = jnp.dot(global_query, k_head.T, preferred_element_type=jnp.float32) * score_multiplier
    global_top = jnp.max(global_scores, axis=-1, keepdims=True)
    global_exp = jnp.exp(global_scores - global_top)
    global_out = jnp.dot(global_exp, v_head.astype(jnp.float32), precision=lax.Precision.HIGHEST)
    global_out = global_out / jnp.sum(global_exp, axis=-1, keepdims=True)
    global_out = global_out.astype(jnp.bfloat16).reshape(GLOBAL, BLOCK, DH)
    return sparse_result.at[global_blocks].set(global_out)


def reference(queries, key_vectors, value_vectors, random_blocks, global_blocks, out_weight):
    tokens_all = queries.shape[0]

    def split_heads(matrix):
        return matrix.reshape(tokens_all, HEADS, DH).transpose(1, 0, 2)

    attended = lax.map(lambda operands: head_attention(operands, global_blocks),
                       (split_heads(queries), split_heads(key_vectors), split_heads(value_vectors), random_blocks))
    merged = attended.reshape(HEADS, tokens_all, DH).transpose(1, 0, 2).reshape(tokens_all, HEADS * DH)
    group_width = HEADS_DEV * DH
    result = jnp.zeros((tokens_all, D), jnp.float32)
    for group_index in range(N_HEADS):
        start = group_index * group_width
        partial_sum = jnp.dot(merged[:, start:start + group_width], out_weight[start:start + group_width],
                              preferred_element_type=jnp.float32)
        rounded_scores = lax.optimization_barrier(partial_sum.astype(jnp.bfloat16))
        result = result + rounded_scores.astype(jnp.float32)
    return result.astype(jnp.bfloat16)
```

```python
import jax
import jax.numpy as jnp
from jax import lax
from jax.experimental import pallas as pl
from jax.experimental.pallas import tpu as pltpu
from jax.sharding import Mesh
from jax.sharding import PartitionSpec as P

DH = 128
BLOCK = 64
RANDOM = 3
GLOBAL = 2
CAP = 4
PLANES = 8
INPLANE = 8
SEQ = ("seq_0", "seq_1", "seq_2")
PLANE = ("seq_1", "seq_2")
VMEM_LIMIT = 56 * 2**20


def ring_step(shard, step):
    peers = lax.axis_size("seq_0")
    return lax.ppermute(shard, "seq_0", [(i, (i + step) % peers) for i in range(peers)])


def pick_kernel(n, first, codes, *refs):
    keys, values, out, sem = refs[:n], refs[n : 2 * n], refs[2 * n], refs[2 * n + 1]

    def one_peer(peer, carry):
        for run in range(n):
            for rank in range(CAP):
                code = codes[(peer * PLANES + first + run) * CAP + rank]
                rows = pl.ds(pl.multiple_of((code & 15) * BLOCK, BLOCK), BLOCK)
                cols = pl.ds(pl.multiple_of((code >> 4) * DH, DH), DH)
                for side, source in enumerate((keys[run], values[run])):
                    pltpu.make_async_copy(
                        source.at[rows, cols], out.at[peer, run, rank, side], sem
                    ).start()
        return carry

    lax.fori_loop(0, INPLANE, one_peer, 0)
    pltpu.make_async_copy(out, out, sem).wait()


def picked(codes, first, keys, values):
    n = len(keys)
    shape = (INPLANE, n, CAP, 2, BLOCK, DH)
    size = 2 * INPLANE * n * CAP * 2 * BLOCK * DH * 2
    return pl.pallas_call(
        lambda *refs: pick_kernel(n, first, *refs),
        out_shape=jax.ShapeDtypeStruct(shape, jnp.bfloat16),
        in_specs=[pl.BlockSpec(memory_space=pltpu.SMEM)]
        + [pl.BlockSpec(memory_space=pl.ANY)] * (2 * n),
        out_specs=pl.BlockSpec(memory_space=pl.ANY),
        scratch_shapes=[pltpu.SemaphoreType.DMA],
        cost_estimate=pl.CostEstimate(flops=0, bytes_accessed=size, transcendentals=0),
        name="pick_blocks",
    )(codes, *keys, *values)


def attend_kernel(
    counts, slots, place, q, k, v, kb, vb, ka, va, glob, gout, *refs
):
    n = len(counts)
    arrived, out, held, sems = refs[:n], refs[n], refs[n + 1], refs[n + 2]
    kpad, vpad = refs[n + 3], refs[n + 4]
    copies = []
    at = 0
    for part, count in enumerate(counts):
        copies.append(
            pltpu.make_async_copy(
                arrived[part], held.at[:, pl.ds(at, count)], sems.at[part]
            )
        )
        copies[-1].start()
        at += count
    heads = q.shape[1] // DH
    blocks = q.shape[0] // BLOCK
    rows = q.shape[0]
    for pad, before, own, after in ((kpad, kb, k, ka), (vpad, vb, v, va)):
        pad[0:BLOCK] = before[...]
        pad[BLOCK : BLOCK + rows] = own[...]
        pad[BLOCK + rows :] = after[...]
    for copy in copies:
        copy.wait()
    scale = DH ** (-0.5)
    col = lax.broadcasted_iota(jnp.int32, (BLOCK, (3 + RANDOM + GLOBAL) * BLOCK), 1)

    def one_block(b, carry):
        at_rows = pl.ds(pl.multiple_of(b * BLOCK, BLOCK), BLOCK)
        win_rows = pl.ds(pl.multiple_of(b * BLOCK, BLOCK), 3 * BLOCK)
        number = place[0] + b
        low = jnp.where(number == 0, BLOCK, 0)
        high = jnp.where(number == place[1] - 1, 2 * BLOCK, 3 * BLOCK)
        valid = (col >= low) & ((col < high) | (col >= 3 * BLOCK))
        for h in range(heads):
            hs = slice(h * DH, (h + 1) * DH)
            picks = []
            for r in range(RANDOM):
                slot = slots[(h * blocks + b) * RANDOM + r]
                picks.append((slot >> 5, (slot >> 2) & 7, slot & 3))
            keys = jnp.concatenate(
                [kpad[win_rows, hs]]
                + [held[p[0], p[1], p[2], 0] for p in picks]
                + [glob[g, 1, :, hs] for g in range(GLOBAL)],
                axis=0,
            )
            values = jnp.concatenate(
                [vpad[win_rows, hs]]
                + [held[p[0], p[1], p[2], 1] for p in picks]
                + [glob[g, 2, :, hs] for g in range(GLOBAL)],
                axis=0,
            )
            scores = lax.dot_general(
                q[at_rows, hs], keys, (((1,), (1,)), ((), ())),
                preferred_element_type=jnp.float32,
            ) * scale
            scores = jnp.where(valid, scores, -jnp.inf)
            peak = jnp.max(scores, axis=1, keepdims=True)
            weights = jnp.exp(scores - peak)
            total = jnp.sum(weights, axis=1, keepdims=True)
            summed = jnp.dot(
                weights.astype(jnp.bfloat16), values, preferred_element_type=jnp.float32
            )
            out[at_rows, hs] = (summed / total).astype(jnp.bfloat16)
        return carry

    lax.fori_loop(0, blocks, one_block, 0)
    for g in range(GLOBAL):

        @pl.when(place[2 + g] >= 0)
        def _():
            at_rows = pl.ds(pl.multiple_of(place[2 + g] * BLOCK, BLOCK), BLOCK)
            for h in range(heads):
                out[at_rows, h * DH : (h + 1) * DH] = gout[h, g * BLOCK : (g + 1) * BLOCK]


def attended(slots, place, q, k, v, kb, vb, ka, va, glob, gout, arrived):
    rows, features = q.shape
    counts = tuple(a.shape[1] for a in arrived)
    vmem = pl.BlockSpec(memory_space=pltpu.VMEM)
    smem = pl.BlockSpec(memory_space=pltpu.SMEM)
    return pl.pallas_call(
        lambda *refs: attend_kernel(counts, *refs),
        out_shape=jax.ShapeDtypeStruct((rows, features), jnp.bfloat16),
        in_specs=[smem, smem]
        + [vmem] * 9
        + [pl.BlockSpec(memory_space=pl.ANY)] * len(arrived),
        out_specs=vmem,
        scratch_shapes=[
            pltpu.VMEM((INPLANE, PLANES, CAP, 2, BLOCK, DH), jnp.bfloat16),
            pltpu.SemaphoreType.DMA((len(arrived),)),
            pltpu.VMEM((rows + 2 * BLOCK, features), jnp.bfloat16),
            pltpu.VMEM((rows + 2 * BLOCK, features), jnp.bfloat16),
        ],
        compiler_params=pltpu.CompilerParams(vmem_limit_bytes=VMEM_LIMIT),
        cost_estimate=pl.CostEstimate(
            flops=4 * rows * features * 512, bytes_accessed=12 * 2**20, transcendentals=rows * 4 * 512
        ),
        name="attend",
    )(slots, place, q, k, v, kb, vb, ka, va, glob, gout, *arrived)


def on_device(queries, key_vectors, value_vectors, random_blocks, global_blocks, out_weight):
    shards = lax.axis_size(SEQ)
    my_index = lax.axis_index(SEQ)
    my_plane = lax.axis_index("seq_0")
    rows, features = queries.shape
    heads = features // DH
    blocks = rows // BLOCK
    requests = heads * blocks * RANDOM

    flat = random_blocks.reshape(requests)
    holders = flat // blocks
    number = jnp.arange(requests, dtype=jnp.int32)
    codes = (number // (blocks * RANDOM)) * 16 + flat % blocks
    earlier = (holders[:, None] == holders[None, :]) & (number[None, :] < number[:, None])
    rank = jnp.sum(earlier.astype(jnp.int32), axis=1)
    apart = (holders // INPLANE - my_plane) % PLANES
    order = jnp.where(apart <= PLANES // 2, jnp.minimum(2 * apart, PLANES - 1), 2 * PLANES - 1 - 2 * apart)
    slots = ((holders % INPLANE) * PLANES + order) * CAP + rank
    every = jnp.arange(INPLANE * PLANES * CAP, dtype=jnp.int32)
    asked = jnp.sum(jnp.where(slots[None, :] == every[:, None], codes[None, :], 0), axis=1)
    asked = asked.reshape(INPLANE, PLANES * CAP)
    asked = lax.all_to_all(asked, PLANE, split_axis=0, concat_axis=0, tiled=True).reshape(-1)

    peers = [(i, i + 1) for i in range(shards - 1)]
    back = [(j, i) for i, j in peers]
    kb = lax.ppermute(key_vectors[rows - BLOCK :], SEQ, peers)
    vb = lax.ppermute(value_vectors[rows - BLOCK :], SEQ, peers)
    ka = lax.ppermute(key_vectors[:BLOCK], SEQ, back)
    va = lax.ppermute(value_vectors[:BLOCK], SEQ, back)

    up_k, up_v, down_k, down_v = key_vectors, value_vectors, key_vectors, value_vectors
    keys, values = [key_vectors], [value_vectors]
    arrived = []
    first = 0
    for step in range(1, PLANES // 2 + 1):
        last = step == PLANES // 2
        up_k = ring_step(up_k, 1)
        down_v = ring_step(down_v, -1)
        if last:
            keys.append(up_k)
            values.append(down_v)
        else:
            up_v = ring_step(up_v, 1)
            down_k = ring_step(down_k, -1)
            keys += [up_k, down_k]
            values += [up_v, down_v]
        picks = picked(asked, first, keys, values)
        first += len(keys)
        arrived.append(lax.all_to_all(picks, PLANE, split_axis=0, concat_axis=0, tiled=True))
        keys, values = [], []

    holder = global_blocks // blocks
    spot = global_blocks % blocks
    mine = holder == my_index
    own = []
    for g in range(GLOBAL):
        for source in (queries, key_vectors, value_vectors):
            piece = lax.dynamic_slice_in_dim(source, spot[g] * BLOCK, BLOCK, axis=0)
            own.append(jnp.where(mine[g], piece, jnp.zeros_like(piece)))
    glob = lax.psum(jnp.stack(own), SEQ).reshape(GLOBAL, 3, BLOCK, features)

    global_q = glob[:, 0].reshape(GLOBAL * BLOCK, heads, DH)
    scores = jnp.einsum(
        "qhd,khd->hqk", global_q, key_vectors.reshape(rows, heads, DH),
        preferred_element_type=jnp.float32,
    ) * (DH ** (-0.5))
    top = lax.pmax(jnp.max(scores, axis=-1), SEQ)
    weights = jnp.exp(scores - top[..., None])
    part = jnp.einsum(
        "hqk,khd->hqd", weights, value_vectors.reshape(rows, heads, DH).astype(jnp.float32),
        precision=lax.Precision.HIGHEST,
    )
    both = lax.psum(
        jnp.concatenate([part.reshape(-1, DH), jnp.sum(weights, axis=-1).reshape(-1, DH)]), SEQ
    )
    many = heads * GLOBAL * BLOCK
    totals = both[many:].reshape(heads, GLOBAL * BLOCK, 1)
    gout = (both[:many].reshape(heads, GLOBAL * BLOCK, DH) / totals).astype(jnp.bfloat16)

    place = jnp.concatenate(
        [
            jnp.stack([my_index * blocks, jnp.int32(shards * blocks)]).astype(jnp.int32),
            jnp.where(mine, spot, -1).astype(jnp.int32),
        ]
    )
    attention = attended(
        slots, place, queries, key_vectors, value_vectors, kb, vb, ka, va, glob, gout, arrived
    )
    weight = lax.all_to_all(out_weight, "heads", split_axis=1, concat_axis=0, tiled=True)
    whole = lax.all_gather(attention, "heads", axis=1, tiled=True)
    return jnp.dot(whole, weight, preferred_element_type=jnp.float32).astype(jnp.bfloat16)


def solution(mesh):
    torus = Mesh(
        mesh.devices.reshape(mesh.shape["heads"], 8, 4, 2), ("heads", "seq_0", "seq_1", "seq_2")
    )
    in_specs = (
        P(SEQ, "heads"),
        P(SEQ, "heads"),
        P(SEQ, "heads"),
        P("heads", SEQ, None),
        P(),
        P("heads", None),
    )
    out_specs = P(SEQ, "heads")
    return jax.shard_map(
        on_device, mesh=torus, in_specs=in_specs, out_specs=out_specs, check_vma=False
    )
```

```python
import jax
import jax.numpy as jnp
from jax import lax
from jax.experimental import pallas as pl
from jax.experimental.pallas import tpu as pltpu
from jax.sharding import Mesh
from jax.sharding import PartitionSpec as P

DH = 128
BLOCK = 64
RANDOM = 3
GLOBAL = 2
CAP = 4
PLANES = 8
INPLANE = 8
SEQ = ("seq_0", "seq_1", "seq_2")
PLANE = ("seq_1", "seq_2")
VMEM_LIMIT = 56 * 2**20


def ring_step(shard, step):
    peers = lax.axis_size("seq_0")
    return lax.ppermute(shard, "seq_0", [(i, (i + step) % peers) for i in range(peers)])


def across(shard, step):
    peers = lax.axis_size("heads")
    return lax.ppermute(shard, "heads", [(i, (i + step) % peers) for i in range(peers)])


def pick_kernel(n, first, codes, *refs):
    keys, values, out = refs[:n], refs[n : 2 * n], refs[2 * n]

    def one_peer(peer, carry):
        for run in range(n):
            for rank in range(CAP):
                code = codes[(peer * PLANES + first + run) * CAP + rank]
                rows = pl.ds(pl.multiple_of((code & 15) * BLOCK, BLOCK), BLOCK)
                cols = pl.ds(pl.multiple_of((code >> 4) * DH, DH), DH)
                out[peer, run, rank, 0] = keys[run][rows, cols]
                out[peer, run, rank, 1] = values[run][rows, cols]
        return carry

    lax.fori_loop(0, INPLANE, one_peer, 0)


def picked(codes, first, keys, values):
    n = len(keys)
    shape = (INPLANE, n, CAP, 2, BLOCK, DH)
    size = 2 * (sum(k.size for k in keys) * 2 + INPLANE * n * CAP * 2 * BLOCK * DH)
    vmem = pl.BlockSpec(memory_space=pltpu.VMEM)
    return pl.pallas_call(
        lambda *refs: pick_kernel(n, first, *refs),
        out_shape=jax.ShapeDtypeStruct(shape, jnp.bfloat16),
        in_specs=[pl.BlockSpec(memory_space=pltpu.SMEM)] + [vmem] * (2 * n),
        out_specs=vmem,
        compiler_params=pltpu.CompilerParams(vmem_limit_bytes=32 * 2**20),
        cost_estimate=pl.CostEstimate(flops=0, bytes_accessed=size, transcendentals=0),
        name="pick_blocks",
    )(codes, *keys, *values)


def exchanged(asked, first, blocks):
    n = len(blocks) // 2
    picks = picked(asked, first, blocks[:n], blocks[n:])
    return lax.all_to_all(picks, PLANE, split_axis=0, concat_axis=0, tiled=True)


def global_kernel(glob, k, v, out):
    heads = k.shape[1] // DH
    many = GLOBAL * BLOCK
    lane = lax.broadcasted_iota(jnp.int32, (many, DH), 1)
    for h in range(heads):
        hs = slice(h * DH, (h + 1) * DH)
        rows = slice(h * many, (h + 1) * many)
        asking = jnp.concatenate([glob[g, 0, :, hs] for g in range(GLOBAL)], axis=0)
        scores = lax.dot_general(
            asking, k[:, hs], (((1,), (1,)), ((), ())), preferred_element_type=jnp.float32
        ) * (DH ** (-0.5))
        top = jnp.max(scores, axis=1, keepdims=True).astype(jnp.bfloat16).astype(jnp.float32)
        weights = jnp.exp(scores - top)
        total = jnp.sum(weights, axis=1, keepdims=True)
        upper = weights.astype(jnp.bfloat16)
        lower = (weights - upper.astype(jnp.float32)).astype(jnp.bfloat16)
        part = jnp.dot(upper, v[:, hs], preferred_element_type=jnp.float32) + jnp.dot(
            lower, v[:, hs], preferred_element_type=jnp.float32
        )
        out[rows] = packed(part, top, total, lane)


def packed(part, top, total, lane):
    upper = total.astype(jnp.bfloat16).astype(jnp.float32)
    side = jnp.where(lane == 0, top, jnp.where(lane == 1, upper, total - upper))
    return jnp.concatenate([part, side], axis=1).astype(jnp.bfloat16)


def global_parts(glob, k, v):
    vmem = pl.BlockSpec(memory_space=pltpu.VMEM)
    heads = k.shape[1] // DH
    return pl.pallas_call(
        global_kernel,
        out_shape=jax.ShapeDtypeStruct((heads * GLOBAL * BLOCK, 2 * DH), jnp.bfloat16),
        in_specs=[vmem] * 3,
        out_specs=vmem,
        compiler_params=pltpu.CompilerParams(vmem_limit_bytes=32 * 2**20),
        name="global_parts",
    )(glob, k, v)


def merge_kernel(last, parts, out):
    rows = parts.shape[1]
    tops = [parts[p, :, DH : DH + 1].astype(jnp.float32) for p in range(parts.shape[0])]
    top = tops[0]
    for other in tops[1:]:
        top = jnp.maximum(top, other)
    part = jnp.zeros((rows, DH), jnp.float32)
    total = jnp.zeros((rows, 1), jnp.float32)
    for p, own in enumerate(tops):
        scale = jnp.exp(own - top)
        part += scale * parts[p, :, :DH].astype(jnp.float32)
        held = parts[p, :, DH + 1 : DH + 2].astype(jnp.float32)
        total += scale * (held + parts[p, :, DH + 2 : DH + 3].astype(jnp.float32))
    if last:
        out[...] = (part / total).astype(jnp.bfloat16)
    else:
        out[...] = packed(part, top, total, lax.broadcasted_iota(jnp.int32, (rows, DH), 1))


def merged(parts, last):
    vmem = pl.BlockSpec(memory_space=pltpu.VMEM)
    return pl.pallas_call(
        lambda *refs: merge_kernel(last, *refs),
        out_shape=jax.ShapeDtypeStruct((parts.shape[1], DH if last else 2 * DH), jnp.bfloat16),
        in_specs=[vmem],
        out_specs=vmem,
        name="merge_parts",
    )(parts)


def attend_kernel(
    counts, slots, place, q, k, v, kb, vb, ka, va, glob, gout, *refs
):
    n = len(counts)
    arrived, out, held, sems = refs[:n], refs[n], refs[n + 1], refs[n + 2]
    kpad, vpad = refs[n + 3], refs[n + 4]
    copies = []
    at = 0
    for part, count in enumerate(counts):
        copies.append(
            pltpu.make_async_copy(
                arrived[part], held.at[:, pl.ds(at, count)], sems.at[part]
            )
        )
        copies[-1].start()
        at += count
    heads = q.shape[1] // DH
    blocks = q.shape[0] // BLOCK
    rows = q.shape[0]
    for pad, before, own, after in ((kpad, kb, k, ka), (vpad, vb, v, va)):
        pad[0:BLOCK] = before[...]
        pad[BLOCK : BLOCK + rows] = own[...]
        pad[BLOCK + rows :] = after[...]
    for copy in copies:
        copy.wait()
    scale = DH ** (-0.5)
    col = lax.broadcasted_iota(jnp.int32, (BLOCK, (3 + RANDOM + GLOBAL) * BLOCK), 1)

    def one_block(b, carry):
        at_rows = pl.ds(pl.multiple_of(b * BLOCK, BLOCK), BLOCK)
        win_rows = pl.ds(pl.multiple_of(b * BLOCK, BLOCK), 3 * BLOCK)
        number = place[0] + b
        low = jnp.where(number == 0, BLOCK, 0)
        high = jnp.where(number == place[1] - 1, 2 * BLOCK, 3 * BLOCK)
        valid = (col >= low) & ((col < high) | (col >= 3 * BLOCK))
        for h in range(heads):
            hs = slice(h * DH, (h + 1) * DH)
            picks = []
            for r in range(RANDOM):
                slot = slots[(h * blocks + b) * RANDOM + r]
                picks.append((slot >> 5, (slot >> 2) & 7, slot & 3))
            keys = jnp.concatenate(
                [kpad[win_rows, hs]]
                + [held[p[0], p[1], p[2], 0] for p in picks]
                + [glob[g, 1, :, hs] for g in range(GLOBAL)],
                axis=0,
            )
            values = jnp.concatenate(
                [vpad[win_rows, hs]]
                + [held[p[0], p[1], p[2], 1] for p in picks]
                + [glob[g, 2, :, hs] for g in range(GLOBAL)],
                axis=0,
            )
            scores = lax.dot_general(
                q[at_rows, hs], keys, (((1,), (1,)), ((), ())),
                preferred_element_type=jnp.float32,
            ) * scale
            scores = jnp.where(valid, scores, -jnp.inf)
            peak = jnp.max(scores, axis=1, keepdims=True)
            weights = jnp.exp(scores - peak)
            total = jnp.sum(weights, axis=1, keepdims=True)
            summed = jnp.dot(
                weights.astype(jnp.bfloat16), values, preferred_element_type=jnp.float32
            )
            out[at_rows, hs] = (summed / total).astype(jnp.bfloat16)
        return carry

    lax.fori_loop(0, blocks, one_block, 0)
    for g in range(GLOBAL):

        @pl.when(place[2 + g] >= 0)
        def _():
            at_rows = pl.ds(pl.multiple_of(place[2 + g] * BLOCK, BLOCK), BLOCK)
            for h in range(heads):
                first = (h * GLOBAL + g) * BLOCK
                out[at_rows, h * DH : (h + 1) * DH] = gout[first : first + BLOCK]


def attended(slots, place, q, k, v, kb, vb, ka, va, glob, gout, arrived):
    rows, features = q.shape
    counts = tuple(a.shape[1] for a in arrived)
    vmem = pl.BlockSpec(memory_space=pltpu.VMEM)
    smem = pl.BlockSpec(memory_space=pltpu.SMEM)
    return pl.pallas_call(
        lambda *refs: attend_kernel(counts, *refs),
        out_shape=jax.ShapeDtypeStruct((rows, features), jnp.bfloat16),
        in_specs=[smem, smem]
        + [vmem] * 9
        + [pl.BlockSpec(memory_space=pl.ANY)] * len(arrived),
        out_specs=vmem,
        scratch_shapes=[
            pltpu.VMEM((INPLANE, PLANES, CAP, 2, BLOCK, DH), jnp.bfloat16),
            pltpu.SemaphoreType.DMA((len(arrived),)),
            pltpu.VMEM((rows + 2 * BLOCK, features), jnp.bfloat16),
            pltpu.VMEM((rows + 2 * BLOCK, features), jnp.bfloat16),
        ],
        compiler_params=pltpu.CompilerParams(vmem_limit_bytes=VMEM_LIMIT),
        cost_estimate=pl.CostEstimate(
            flops=4 * rows * features * 512, bytes_accessed=12 * 2**20, transcendentals=rows * 4 * 512
        ),
        name="attend",
    )(slots, place, q, k, v, kb, vb, ka, va, glob, gout, *arrived)


def on_device(queries, key_vectors, value_vectors, random_blocks, global_blocks, out_weight):
    shards = lax.axis_size(SEQ)
    my_index = lax.axis_index(SEQ)
    my_plane = lax.axis_index("seq_0")
    rows, features = queries.shape
    heads = features // DH
    blocks = rows // BLOCK
    requests = heads * blocks * RANDOM

    me = lax.axis_index("heads")
    peers = lax.axis_size("heads")
    width = out_weight.shape[1] // peers
    weights = []
    for away in (0, 1, -1, 2):
        piece = lax.dynamic_slice_in_dim(out_weight, ((me + away) % peers) * width, width, axis=1)
        weights.append(across(piece, away) if away else piece)

    flat = random_blocks.reshape(requests)
    holders = flat // blocks
    number = jnp.arange(requests, dtype=jnp.int32)
    codes = (number // (blocks * RANDOM)) * 16 + flat % blocks
    earlier = (holders[:, None] == holders[None, :]) & (number[None, :] < number[:, None])
    rank = jnp.sum(earlier.astype(jnp.int32), axis=1)
    apart = (holders // INPLANE - my_plane) % PLANES
    order = jnp.where(apart <= PLANES // 2, jnp.minimum(2 * apart, PLANES - 1), 2 * PLANES - 1 - 2 * apart)
    slots = ((holders % INPLANE) * PLANES + order) * CAP + rank
    every = jnp.arange(INPLANE * PLANES * CAP, dtype=jnp.int32)
    asked = jnp.sum(jnp.where(slots[None, :] == every[:, None], codes[None, :], 0), axis=1)
    asked = asked.reshape(INPLANE, PLANES * CAP)
    asked = lax.all_to_all(asked, PLANE, split_axis=0, concat_axis=0, tiled=True).reshape(-1)

    peers = [(i, i + 1) for i in range(shards - 1)]
    back = [(j, i) for i, j in peers]
    kb = lax.ppermute(key_vectors[rows - BLOCK :], SEQ, peers)
    vb = lax.ppermute(value_vectors[rows - BLOCK :], SEQ, peers)
    ka = lax.ppermute(key_vectors[:BLOCK], SEQ, back)
    va = lax.ppermute(value_vectors[:BLOCK], SEQ, back)

    holder = global_blocks // blocks
    spot = global_blocks % blocks
    mine = holder == my_index
    own = []
    for g in range(GLOBAL):
        for source in (queries, key_vectors, value_vectors):
            piece = lax.dynamic_slice_in_dim(source, spot[g] * BLOCK, BLOCK, axis=0)
            own.append(jnp.where(mine[g], piece, jnp.zeros_like(piece)))
    own = jnp.concatenate(own).reshape(INPLANE, -1, features)
    own = lax.all_to_all(own, PLANE, split_axis=0, concat_axis=0, tiled=True).sum(axis=0)
    own = lax.all_gather(own, "seq_0").sum(axis=0)
    glob = lax.all_gather(own, PLANE).reshape(GLOBAL, 3, BLOCK, features)

    parts = global_parts(glob, key_vectors, value_vectors).reshape(INPLANE, -1, 2 * DH)
    parts = lax.all_to_all(parts, PLANE, split_axis=0, concat_axis=0, tiled=True)
    parts = lax.all_gather(merged(parts, False), "seq_0")
    gout = lax.all_gather(merged(parts, True), PLANE, tiled=True)

    up_k, up_v, down_k, down_v = key_vectors, value_vectors, key_vectors, value_vectors
    keys, values = [key_vectors], [value_vectors]
    arrived = []
    first = 0
    waiting = None
    beside = {2: [kb, vb, ka, va, glob], 3: weights, 4: gout}
    for step in range(1, PLANES // 2 + 1):
        last = step == PLANES // 2
        up_k = ring_step(up_k, 1)
        down_v = ring_step(down_v, -1)
        if waiting is not None:
            waiting, _, _, arrived, beside[step] = lax.optimization_barrier(
                (waiting, up_k, down_v, arrived, beside[step])
            )
            arrived = arrived + [exchanged(asked, first, waiting)]
            first += len(waiting) // 2
        if last:
            keys.append(up_k)
            values.append(down_v)
        else:
            up_v = ring_step(up_v, 1)
            down_k = ring_step(down_k, -1)
            keys += [up_k, down_k]
            values += [up_v, down_v]
        waiting = keys + values
        keys, values = [], []
    waiting, arrived = lax.optimization_barrier((waiting, arrived))
    arrived = arrived + [exchanged(asked, first, waiting)]

    kb, vb, ka, va, glob = beside[2]
    weights, gout = beside[3], beside[4]
    place = jnp.concatenate(
        [
            jnp.stack([my_index * blocks, jnp.int32(shards * blocks)]).astype(jnp.int32),
            jnp.where(mine, spot, -1).astype(jnp.int32),
        ]
    )
    attention = attended(
        slots, place, queries, key_vectors, value_vectors, kb, vb, ka, va, glob, gout, arrived
    )
    half = rows // 2
    own_t, own_b = attention[:half], attention[half:]
    right_t, left_b = across(own_t, 1), across(own_b, -1)
    right_b, left_t = across(own_b, 1), across(own_t, -1)
    far_t, far_b = across(right_t, 1), across(left_b, -1)

    def product(*pieces):
        total = 0.0
        for piece, weight in zip(pieces, weights):
            total = total + jnp.dot(piece, weight, preferred_element_type=jnp.float32)
        return total.astype(jnp.bfloat16)

    return jnp.concatenate(
        [product(own_t, right_t, left_t, far_t), product(own_b, right_b, left_b, far_b)]
    )


def solution(mesh):
    torus = Mesh(
        mesh.devices.reshape(mesh.shape["heads"], 8, 4, 2), ("heads", "seq_0", "seq_1", "seq_2")
    )
    in_specs = (
        P(SEQ, "heads"),
        P(SEQ, "heads"),
        P(SEQ, "heads"),
        P("heads", SEQ, None),
        P(),
        P("heads", None),
    )
    out_specs = P(SEQ, "heads")
    return jax.shard_map(
        on_device, mesh=torus, in_specs=in_specs, out_specs=out_specs, check_vma=False
    )
```

```python
import jax
import jax.numpy as jnp
from jax import lax
from jax.experimental import pallas as pl
from jax.experimental.pallas import tpu as pltpu
from jax.sharding import Mesh
from jax.sharding import PartitionSpec as P

DH = 128
BLOCK = 64
RANDOM = 3
GLOBAL = 2
CAP = 4
PLANES = 8
INPLANE = 8
SEQ = ("seq_0", "seq_1", "seq_2")
PLANE = ("seq_1", "seq_2")
VMEM_LIMIT = 56 * 2**20


def ring_step(shard, step):
    peers = lax.axis_size("seq_0")
    return lax.ppermute(shard, "seq_0", [(i, (i + step) % peers) for i in range(peers)])


def across(shard, step):
    peers = lax.axis_size("heads")
    return lax.ppermute(shard, "heads", [(i, (i + step) % peers) for i in range(peers)])


def pick_kernel(n, first, codes, *refs):
    keys, values = refs[:n], refs[n : 2 * n]
    extra, out = refs[2 * n : -1], refs[-1]

    def one_peer(peer, carry):
        for run in range(n):
            for rank in range(CAP):
                code = codes[(peer * PLANES + first + run) * CAP + rank]
                rows = pl.ds(pl.multiple_of((code & 15) * BLOCK, BLOCK), BLOCK)
                cols = pl.ds(pl.multiple_of((code >> 4) * DH, DH), DH)
                at = (run * CAP + rank) * 2 * BLOCK
                out[peer, at : at + BLOCK] = keys[run][rows, cols]
                out[peer, at + BLOCK : at + 2 * BLOCK] = values[run][rows, cols]
        if extra:
            own = extra[0][pl.ds(pl.multiple_of(peer * BLOCK, BLOCK), BLOCK)].astype(out.dtype)
            at = n * CAP * 2 * BLOCK
            out[peer, at : at + BLOCK] = own[:, :DH]
            out[peer, at + BLOCK : at + 2 * BLOCK] = own[:, DH:]
        return carry

    lax.fori_loop(0, INPLANE, one_peer, 0)


def picked(codes, first, blocks, extra=()):
    n = len(blocks) // 2
    shape = (INPLANE, (n * CAP + len(extra)) * 2 * BLOCK, DH)
    size = 2 * (sum(k.size for k in blocks) + INPLANE * n * CAP * 2 * BLOCK * DH)
    vmem = pl.BlockSpec(memory_space=pltpu.VMEM)
    return pl.pallas_call(
        lambda *refs: pick_kernel(n, first, *refs),
        out_shape=jax.ShapeDtypeStruct(shape, jnp.bfloat16),
        in_specs=[pl.BlockSpec(memory_space=pltpu.SMEM)] + [vmem] * (2 * n + len(extra)),
        out_specs=vmem,
        compiler_params=pltpu.CompilerParams(vmem_limit_bytes=32 * 2**20),
        cost_estimate=pl.CostEstimate(flops=0, bytes_accessed=size, transcendentals=0),
        name="pick_blocks",
    )(codes, *blocks, *extra)


def over_plane(parts):
    return lax.all_to_all(parts, PLANE, split_axis=0, concat_axis=0, tiled=True)


def global_kernel(n, asking, *refs):
    keys, values = refs[:n], refs[n : 2 * n]
    held, out = refs[2 * n : -1], refs[-1]
    heads = asking.shape[1] // DH
    many = GLOBAL * BLOCK
    lane = lax.broadcasted_iota(jnp.int32, (many, DH), 1)
    for h in range(heads):
        hs = slice(h * DH, (h + 1) * DH)
        rows = slice(h * many, (h + 1) * many)
        scores = [
            lax.dot_general(
                asking[:, hs], k[:, hs], (((1,), (1,)), ((), ())),
                preferred_element_type=jnp.float32,
            ) * (DH ** (-0.5))
            for k in keys
        ]
        top = jnp.max(scores[0], axis=1, keepdims=True)
        for other in scores[1:]:
            top = jnp.maximum(top, jnp.max(other, axis=1, keepdims=True))
        top = top.astype(jnp.bfloat16).astype(jnp.float32)
        if held:
            before = held[0][rows, DH : DH + 1]
            top = jnp.maximum(top, before)
            scale = jnp.exp(before - top)
            part = held[0][rows, :DH] * scale
            total = held[0][rows, DH + 1 : DH + 2] * scale
        else:
            part = jnp.zeros((many, DH), jnp.float32)
            total = jnp.zeros((many, 1), jnp.float32)
        for score, v in zip(scores, values):
            weights = jnp.exp(score - top)
            total += jnp.sum(weights, axis=1, keepdims=True)
            part += jnp.dot(
                weights.astype(jnp.bfloat16), v[:, hs], preferred_element_type=jnp.float32
            )
        upper = total.astype(jnp.bfloat16).astype(jnp.float32)
        side = jnp.where(lane == 0, top, jnp.where(lane == 1, total, 0.0))
        side = jnp.where(lane == 2, upper, jnp.where(lane == 3, total - upper, side))
        out[rows] = jnp.concatenate([part, side], axis=1)


def global_parts(asking, blocks, held=()):
    n = len(blocks) // 2
    vmem = pl.BlockSpec(memory_space=pltpu.VMEM)
    rows = asking.shape[0] * asking.shape[1] // DH
    return pl.pallas_call(
        lambda *refs: global_kernel(n, *refs),
        out_shape=jax.ShapeDtypeStruct((rows, 2 * DH), jnp.float32),
        in_specs=[vmem] * (1 + len(blocks) + len(held)),
        out_specs=vmem,
        compiler_params=pltpu.CompilerParams(vmem_limit_bytes=32 * 2**20),
        cost_estimate=pl.CostEstimate(
            flops=4 * rows * DH * 768 * n, bytes_accessed=2**20 * n, transcendentals=rows * 768 * n
        ),
        name="global_parts",
    )(asking, *blocks, *held)


def merge_kernel(parts, out):
    peers = parts.shape[0]
    tops = [parts[p, BLOCK:, 0:1].astype(jnp.float32) for p in range(peers)]
    top = tops[0]
    for other in tops[1:]:
        top = jnp.maximum(top, other)
    part = jnp.zeros((BLOCK, DH), jnp.float32)
    total = jnp.zeros((BLOCK, 1), jnp.float32)
    for p, own in enumerate(tops):
        scale = jnp.exp(own - top)
        part += scale * parts[p, :BLOCK].astype(jnp.float32)
        upper = parts[p, BLOCK:, 2:3].astype(jnp.float32)
        total += scale * (upper + parts[p, BLOCK:, 3:4].astype(jnp.float32))
    whole = (part / total).astype(jnp.bfloat16)
    for p in range(peers):
        out[p] = whole


def merged(parts):
    peers, rows, _ = parts.shape
    return pl.pallas_call(
        merge_kernel,
        out_shape=jax.ShapeDtypeStruct((peers, BLOCK, DH), jnp.bfloat16),
        grid=(1,),
        in_specs=[pl.BlockSpec((peers, 2 * BLOCK, DH), lambda i: (0, rows // (2 * BLOCK) - 1, 0))],
        out_specs=pl.BlockSpec((peers, BLOCK, DH), lambda i: (0, 0, 0)),
        name="merge_parts",
    )(parts)


def patch_kernel(place, gout, attention, *out):
    blocks = attention.shape[0] // BLOCK
    heads = attention.shape[1] // DH
    half = blocks // 2
    for side in range(2):
        out[side][...] = attention[side * half * BLOCK : (side + 1) * half * BLOCK]
        for g in range(GLOBAL):
            spot = place[2 + g] - side * half

            @pl.when((place[2 + g] >= 0) & (spot >= 0) & (spot < half))
            def _():
                at_rows = pl.ds(pl.multiple_of(spot * BLOCK, BLOCK), BLOCK)
                for h in range(heads):
                    out[side][at_rows, h * DH : (h + 1) * DH] = gout[h * GLOBAL + g]


def patched(place, gout, attention):
    rows, features = attention.shape
    vmem = pl.BlockSpec(memory_space=pltpu.VMEM)
    half = jax.ShapeDtypeStruct((rows // 2, features), attention.dtype)
    return pl.pallas_call(
        patch_kernel,
        out_shape=(half, half),
        in_specs=[pl.BlockSpec(memory_space=pltpu.SMEM), vmem, vmem],
        out_specs=(vmem, vmem),
        name="global_rows",
    )(place, gout, attention)


def attend_kernel(
    counts, slots, place, q, k, v, before, after, glob, *refs
):
    n = len(counts)
    arrived, out, held, sems = refs[:n], refs[n], refs[n + 1], refs[n + 2]
    kpad, vpad = refs[n + 3], refs[n + 4]
    copies = []
    at = 0
    for part, count in enumerate(counts):
        copies.append(
            pltpu.make_async_copy(
                arrived[part].at[:, pl.ds(0, count)], held.at[:, pl.ds(at, count)], sems.at[part]
            )
        )
        copies[-1].start()
        at += count
    heads = q.shape[1] // DH
    blocks = q.shape[0] // BLOCK
    rows = q.shape[0]
    for side, (pad, own) in enumerate(((kpad, k), (vpad, v))):
        pad[0:BLOCK] = before[side * BLOCK : (side + 1) * BLOCK]
        pad[BLOCK : BLOCK + rows] = own[...]
        pad[BLOCK + rows :] = after[side * BLOCK : (side + 1) * BLOCK]
    for copy in copies:
        copy.wait()
    scale = DH ** (-0.5)
    col = lax.broadcasted_iota(jnp.int32, (BLOCK, (3 + RANDOM + GLOBAL) * BLOCK), 1)

    def one_block(b, carry):
        at_rows = pl.ds(pl.multiple_of(b * BLOCK, BLOCK), BLOCK)
        win_rows = pl.ds(pl.multiple_of(b * BLOCK, BLOCK), 3 * BLOCK)
        number = place[0] + b
        low = jnp.where(number == 0, BLOCK, 0)
        high = jnp.where(number == place[1] - 1, 2 * BLOCK, 3 * BLOCK)
        valid = (col >= low) & ((col < high) | (col >= 3 * BLOCK))
        for h in range(heads):
            hs = slice(h * DH, (h + 1) * DH)
            picks = []
            for r in range(RANDOM):
                slot = slots[(h * blocks + b) * RANDOM + r]
                at = pl.multiple_of((slot & 31) * 2 * BLOCK, 2 * BLOCK)
                picks.append((slot >> 5, at))
            keys = jnp.concatenate(
                [kpad[win_rows, hs]]
                + [held[p[0], pl.ds(p[1], BLOCK)] for p in picks]
                + [glob[g, 0, :, hs] for g in range(GLOBAL)],
                axis=0,
            )
            values = jnp.concatenate(
                [vpad[win_rows, hs]]
                + [held[p[0], pl.ds(p[1] + BLOCK, BLOCK)] for p in picks]
                + [glob[g, 1, :, hs] for g in range(GLOBAL)],
                axis=0,
            )
            scores = lax.dot_general(
                q[at_rows, hs], keys, (((1,), (1,)), ((), ())),
                preferred_element_type=jnp.float32,
            ) * scale
            scores = jnp.where(valid, scores, -jnp.inf)
            peak = jnp.max(scores, axis=1, keepdims=True)
            weights = jnp.exp(scores - peak)
            total = jnp.sum(weights, axis=1, keepdims=True)
            summed = jnp.dot(
                weights.astype(jnp.bfloat16), values, preferred_element_type=jnp.float32
            )
            out[at_rows, hs] = (summed / total).astype(jnp.bfloat16)
        return carry

    lax.fori_loop(0, blocks, one_block, 0)


def attended(slots, place, q, k, v, before, after, glob, arrived):
    rows, features = q.shape
    unit = CAP * 2 * BLOCK
    counts = tuple(a.shape[1] // unit * unit for a in arrived)
    vmem = pl.BlockSpec(memory_space=pltpu.VMEM)
    smem = pl.BlockSpec(memory_space=pltpu.SMEM)
    return pl.pallas_call(
        lambda *refs: attend_kernel(counts, *refs),
        out_shape=jax.ShapeDtypeStruct((rows, features), jnp.bfloat16),
        in_specs=[smem, smem]
        + [vmem] * 6
        + [pl.BlockSpec(memory_space=pl.ANY)] * len(arrived),
        out_specs=vmem,
        scratch_shapes=[
            pltpu.VMEM((INPLANE, PLANES * unit, DH), jnp.bfloat16),
            pltpu.SemaphoreType.DMA((len(arrived),)),
            pltpu.VMEM((rows + 2 * BLOCK, features), jnp.bfloat16),
            pltpu.VMEM((rows + 2 * BLOCK, features), jnp.bfloat16),
        ],
        compiler_params=pltpu.CompilerParams(vmem_limit_bytes=VMEM_LIMIT),
        cost_estimate=pl.CostEstimate(
            flops=4 * rows * features * 512, bytes_accessed=12 * 2**20, transcendentals=rows * 4 * 512
        ),
        name="attend",
    )(slots, place, q, k, v, before, after, glob, *arrived)


def on_device(queries, key_vectors, value_vectors, random_blocks, global_blocks, out_weight):
    shards = lax.axis_size(SEQ)
    my_index = lax.axis_index(SEQ)
    my_plane = lax.axis_index("seq_0")
    rows, features = queries.shape
    heads = features // DH
    blocks = rows // BLOCK
    requests = heads * blocks * RANDOM

    flat = random_blocks.reshape(requests)
    holders = flat // blocks
    number = jnp.arange(requests, dtype=jnp.int32)
    codes = (number // (blocks * RANDOM)) * 16 + flat % blocks
    earlier = (holders[:, None] == holders[None, :]) & (number[None, :] < number[:, None])
    rank = jnp.sum(earlier.astype(jnp.int32), axis=1)
    apart = (holders // INPLANE - my_plane) % PLANES
    order = jnp.where(apart <= PLANES // 2, jnp.minimum(2 * apart, PLANES - 1), 2 * PLANES - 1 - 2 * apart)
    slots = ((holders % INPLANE) * PLANES + order) * CAP + rank
    every = jnp.arange(INPLANE * PLANES * CAP, dtype=jnp.int32)
    asked = jnp.sum(jnp.where(slots[None, :] == every[:, None], codes[None, :], 0), axis=1)
    asked = asked.astype(jnp.bfloat16).reshape(INPLANE, 1, PLANES * CAP)
    asked = jnp.pad(asked, ((0, 0), (0, 15), (0, features - PLANES * CAP)))

    holder = global_blocks // blocks
    spot = global_blocks % blocks
    mine = holder == my_index

    def cut(source, g):
        piece = lax.dynamic_slice_in_dim(source, spot[g] * BLOCK, BLOCK, axis=0)
        return jnp.where(mine[g], piece, jnp.zeros_like(piece))

    asking = jnp.concatenate([cut(queries, g) for g in range(GLOBAL)])
    shared = jnp.concatenate(
        [cut(source, g) for g in range(GLOBAL) for source in (key_vectors, value_vectors)]
    ).reshape(INPLANE, -1, features)
    asking = jnp.broadcast_to(asking[None], (INPLANE, *asking.shape))
    found = over_plane(jnp.concatenate([asking, shared, asked], axis=1))
    many = GLOBAL * BLOCK
    asking = found[:, :many].sum(axis=0)
    shared = found[:, many:-16].sum(axis=0)
    asked = found[:, -16, : PLANES * CAP].astype(jnp.int32).reshape(-1)

    up_k, up_v, down_k, down_v = key_vectors, value_vectors, key_vectors, value_vectors
    picks = picked(asked, 0, [key_vectors, value_vectors])
    arrived = [over_plane(picks)]
    shared = jnp.broadcast_to(shared[None], (PLANES, *shared.shape))
    shared = lax.all_to_all(shared, "seq_0", split_axis=0, concat_axis=0, tiled=True).sum(axis=0)
    glob = lax.all_gather(shared, PLANE, tiled=True).reshape(GLOBAL, 2, BLOCK, features)
    ahead = [(i, i + 1) for i in range(shards - 1)]
    back = [(j, i) for i, j in ahead]
    me = lax.axis_index("heads")
    peers = lax.axis_size("heads")
    width = out_weight.shape[1] // peers

    def rows_for(away, after):
        piece = lax.dynamic_slice_in_dim(out_weight, ((me + away) % peers) * width, width, axis=1)
        if after is None:
            return piece
        piece, _ = lax.optimization_barrier((piece, after))
        return across(piece, away)

    weights = [rows_for(0, None)]
    first, parts = 1, ()
    for step in range(1, PLANES // 2 + 1):
        up_k = ring_step(up_k, 1)
        down_v = ring_step(down_v, -1)
        if step == 1:
            ends = jnp.concatenate([key_vectors[rows - BLOCK :], value_vectors[rows - BLOCK :]])
            starts = jnp.concatenate([key_vectors[:BLOCK], value_vectors[:BLOCK]])
            ends, starts, _, _ = lax.optimization_barrier((ends, starts, up_k, down_v))
            before = lax.ppermute(ends, SEQ, ahead)
            after = lax.ppermute(starts, SEQ, back)
            beside = (before, after)
        else:
            held, _, _, _, beside, parts = lax.optimization_barrier(
                (held, up_k, down_v, picks, beside, parts)
            )
            if step == 2:
                before, after = beside
            else:
                weights.append(beside)
            beside = rows_for(2 if step == 4 else (1, -1)[step - 2], up_k)
            picks = picked(asked, first, held)
            arrived.append(over_plane(picks))
            first += len(held) // 2
            both = held
            if step == 2:
                both = [*held[:2], key_vectors, *held[2:], value_vectors]
            parts = (global_parts(asking, both, parts),)
        if step < PLANES // 2:
            up_v = ring_step(up_v, 1)
            down_k = ring_step(down_k, -1)
            held = [up_k, down_k, up_v, down_v]
        else:
            held = [up_k, down_v]
    weights.append(beside)
    held, arrived, parts, glob = lax.optimization_barrier((held, arrived, parts, glob))
    parts = (global_parts(asking, held, parts),)
    arrived.append(over_plane(picked(asked, first, held, parts)))
    gout = over_plane(merged(arrived[-1]))

    place = jnp.concatenate(
        [
            jnp.stack([my_index * blocks, jnp.int32(shards * blocks)]).astype(jnp.int32),
            jnp.where(mine, spot, -1).astype(jnp.int32),
        ]
    )
    attention = attended(
        slots, place, queries, key_vectors, value_vectors, before, after, glob, arrived
    )
    own_t, own_b = patched(place, gout, attention)
    right_t, left_b = across(own_t, 1), across(own_b, -1)
    right_b, left_t = across(own_b, 1), across(own_t, -1)
    far_t, far_b = across(right_t, 1), across(left_b, -1)

    def product(*pieces):
        total = 0.0
        for piece, weight in zip(pieces, weights):
            total = total + jnp.dot(piece, weight, preferred_element_type=jnp.float32)
        return total.astype(jnp.bfloat16)

    return jnp.concatenate(
        [product(own_t, right_t, left_t, far_t), product(own_b, right_b, left_b, far_b)]
    )


def solution(mesh):
    torus = Mesh(
        mesh.devices.reshape(mesh.shape["heads"], 8, 4, 2), ("heads", "seq_0", "seq_1", "seq_2")
    )
    in_specs = (
        P(SEQ, "heads"),
        P(SEQ, "heads"),
        P(SEQ, "heads"),
        P("heads", SEQ, None),
        P(),
        P("heads", None),
    )
    out_specs = P(SEQ, "heads")
    return jax.shard_map(
        on_device, mesh=torus, in_specs=in_specs, out_specs=out_specs, check_vma=False
    )
```

```python
import jax
import jax.numpy as jnp
from jax import lax
from jax.experimental import pallas as pl
from jax.experimental.pallas import tpu as pltpu
from jax.sharding import Mesh
from jax.sharding import PartitionSpec as P

DH = 128
BLOCK = 64
RANDOM = 3
GLOBAL = 2
CAP = 4
PLANES = 8
INPLANE = 8
SEQ = ("seq_0", "seq_1", "seq_2")
PLANE = ("seq_1", "seq_2")
VMEM_LIMIT = 56 * 2**20


def ring_step(shard, step):
    peers = lax.axis_size("seq_0")
    return lax.ppermute(shard, "seq_0", [(i, (i + step) % peers) for i in range(peers)])


def across(shard, step):
    peers = lax.axis_size("heads")
    return lax.ppermute(shard, "heads", [(i, (i + step) % peers) for i in range(peers)])


def pick_kernel(n, first, codes, *refs):
    keys, values = refs[:n], refs[n : 2 * n]
    extra, out = refs[2 * n : -1], refs[-1]

    def one_peer(peer, carry):
        for run in range(n):
            for rank in range(CAP):
                code = codes[(peer * PLANES + first + run) * CAP + rank]
                rows = pl.ds(pl.multiple_of((code & 15) * BLOCK, BLOCK), BLOCK)
                cols = pl.ds(pl.multiple_of((code >> 4) * DH, DH), DH)
                at = (run * CAP + rank) * 2 * BLOCK
                out[peer, at : at + BLOCK] = keys[run][rows, cols]
                out[peer, at + BLOCK : at + 2 * BLOCK] = values[run][rows, cols]
        if extra:
            own = extra[0][pl.ds(pl.multiple_of(peer * BLOCK, BLOCK), BLOCK)].astype(out.dtype)
            at = n * CAP * 2 * BLOCK
            out[peer, at : at + BLOCK] = own[:, :DH]
            out[peer, at + BLOCK : at + 2 * BLOCK] = own[:, DH:]
        return carry

    lax.fori_loop(0, INPLANE, one_peer, 0)


def picked(codes, first, blocks, extra=()):
    n = len(blocks) // 2
    shape = (INPLANE, (n * CAP + len(extra)) * 2 * BLOCK, DH)
    size = 2 * (sum(k.size for k in blocks) + INPLANE * n * CAP * 2 * BLOCK * DH)
    vmem = pl.BlockSpec(memory_space=pltpu.VMEM)
    return pl.pallas_call(
        lambda *refs: pick_kernel(n, first, *refs),
        out_shape=jax.ShapeDtypeStruct(shape, jnp.bfloat16),
        in_specs=[pl.BlockSpec(memory_space=pltpu.SMEM)] + [vmem] * (2 * n + len(extra)),
        out_specs=vmem,
        compiler_params=pltpu.CompilerParams(vmem_limit_bytes=32 * 2**20),
        cost_estimate=pl.CostEstimate(flops=0, bytes_accessed=24 * 2**20, transcendentals=0),
        name="pick_blocks",
    )(codes, *blocks, *extra)


def over_plane(parts):
    return lax.all_to_all(parts, PLANE, split_axis=0, concat_axis=0, tiled=True)


def global_kernel(n, asking, *refs):
    keys, values = refs[:n], refs[n : 2 * n]
    held, out = refs[2 * n : -1], refs[-1]
    heads = asking.shape[1] // DH
    many = GLOBAL * BLOCK
    lane = lax.broadcasted_iota(jnp.int32, (many, DH), 1)
    for h in range(heads):
        hs = slice(h * DH, (h + 1) * DH)
        rows = slice(h * many, (h + 1) * many)
        scores = [
            lax.dot_general(
                asking[:, hs], k[:, hs], (((1,), (1,)), ((), ())),
                preferred_element_type=jnp.float32,
            ) * (DH ** (-0.5))
            for k in keys
        ]
        top = jnp.max(scores[0], axis=1, keepdims=True)
        for other in scores[1:]:
            top = jnp.maximum(top, jnp.max(other, axis=1, keepdims=True))
        top = top.astype(jnp.bfloat16).astype(jnp.float32)
        if held:
            before = held[0][rows, DH : DH + 1]
            top = jnp.maximum(top, before)
            scale = jnp.exp(before - top)
            part = held[0][rows, :DH] * scale
            total = held[0][rows, DH + 1 : DH + 2] * scale
        else:
            part = jnp.zeros((many, DH), jnp.float32)
            total = jnp.zeros((many, 1), jnp.float32)
        for score, v in zip(scores, values):
            weights = jnp.exp(score - top)
            total += jnp.sum(weights, axis=1, keepdims=True)
            part += jnp.dot(
                weights.astype(jnp.bfloat16), v[:, hs], preferred_element_type=jnp.float32
            )
        upper = total.astype(jnp.bfloat16).astype(jnp.float32)
        side = jnp.where(lane == 0, top, jnp.where(lane == 1, total, 0.0))
        side = jnp.where(lane == 2, upper, jnp.where(lane == 3, total - upper, side))
        out[rows] = jnp.concatenate([part, side], axis=1)


def global_parts(asking, blocks, held=()):
    n = len(blocks) // 2
    vmem = pl.BlockSpec(memory_space=pltpu.VMEM)
    rows = asking.shape[0] * asking.shape[1] // DH
    return pl.pallas_call(
        lambda *refs: global_kernel(n, *refs),
        out_shape=jax.ShapeDtypeStruct((rows, 2 * DH), jnp.float32),
        in_specs=[vmem] * (1 + len(blocks) + len(held)),
        out_specs=vmem,
        compiler_params=pltpu.CompilerParams(vmem_limit_bytes=32 * 2**20),
        cost_estimate=pl.CostEstimate(
            flops=4 * rows * DH * 768 * n, bytes_accessed=24 * 2**20, transcendentals=rows * 768 * n
        ),
        name="global_parts",
    )(asking, *blocks, *held)


def merge_kernel(parts, out):
    peers = parts.shape[0]
    tops = [parts[p, BLOCK:, 0:1].astype(jnp.float32) for p in range(peers)]
    top = tops[0]
    for other in tops[1:]:
        top = jnp.maximum(top, other)
    part = jnp.zeros((BLOCK, DH), jnp.float32)
    total = jnp.zeros((BLOCK, 1), jnp.float32)
    for p, own in enumerate(tops):
        scale = jnp.exp(own - top)
        part += scale * parts[p, :BLOCK].astype(jnp.float32)
        upper = parts[p, BLOCK:, 2:3].astype(jnp.float32)
        total += scale * (upper + parts[p, BLOCK:, 3:4].astype(jnp.float32))
    whole = (part / total).astype(jnp.bfloat16)
    for p in range(peers):
        out[p] = whole


def merged(parts):
    peers, rows, _ = parts.shape
    return pl.pallas_call(
        merge_kernel,
        out_shape=jax.ShapeDtypeStruct((peers, BLOCK, DH), jnp.bfloat16),
        grid=(1,),
        in_specs=[pl.BlockSpec((peers, 2 * BLOCK, DH), lambda i: (0, rows // (2 * BLOCK) - 1, 0))],
        out_specs=pl.BlockSpec((peers, BLOCK, DH), lambda i: (0, 0, 0)),
        name="merge_parts",
    )(parts)


def patch_kernel(place, gout, attention, *out):
    blocks = attention.shape[0] // BLOCK
    heads = attention.shape[1] // DH
    half = blocks // 2
    for side in range(2):
        out[side][...] = attention[side * half * BLOCK : (side + 1) * half * BLOCK]
        for g in range(GLOBAL):
            spot = place[2 + g] - side * half

            @pl.when((place[2 + g] >= 0) & (spot >= 0) & (spot < half))
            def _():
                at_rows = pl.ds(pl.multiple_of(spot * BLOCK, BLOCK), BLOCK)
                for h in range(heads):
                    out[side][at_rows, h * DH : (h + 1) * DH] = gout[h * GLOBAL + g]


def patched(place, gout, attention):
    rows, features = attention.shape
    vmem = pl.BlockSpec(memory_space=pltpu.VMEM)
    half = jax.ShapeDtypeStruct((rows // 2, features), attention.dtype)
    return pl.pallas_call(
        patch_kernel,
        out_shape=(half, half),
        in_specs=[pl.BlockSpec(memory_space=pltpu.SMEM), vmem, vmem],
        out_specs=(vmem, vmem),
        name="global_rows",
    )(place, gout, attention)


def attend_kernel(
    counts, slots, place, q, k, v, before, after, glob, *refs
):
    n = len(counts)
    arrived, out, held, sems = refs[:n], refs[n], refs[n + 1], refs[n + 2]
    kpad, vpad = refs[n + 3], refs[n + 4]
    copies = []
    at = 0
    for part, count in enumerate(counts):
        copies.append(
            pltpu.make_async_copy(
                arrived[part].at[:, pl.ds(0, count)], held.at[:, pl.ds(at, count)], sems.at[part]
            )
        )
        copies[-1].start()
        at += count
    heads = q.shape[1] // DH
    blocks = q.shape[0] // BLOCK
    rows = q.shape[0]
    for side, (pad, own) in enumerate(((kpad, k), (vpad, v))):
        pad[0:BLOCK] = before[side * BLOCK : (side + 1) * BLOCK]
        pad[BLOCK : BLOCK + rows] = own[...]
        pad[BLOCK + rows :] = after[side * BLOCK : (side + 1) * BLOCK]
    for copy in copies:
        copy.wait()
    scale = DH ** (-0.5)
    col = lax.broadcasted_iota(jnp.int32, (BLOCK, (3 + RANDOM + GLOBAL) * BLOCK), 1)

    def one_block(b, carry):
        at_rows = pl.ds(pl.multiple_of(b * BLOCK, BLOCK), BLOCK)
        win_rows = pl.ds(pl.multiple_of(b * BLOCK, BLOCK), 3 * BLOCK)
        number = place[0] + b
        low = jnp.where(number == 0, BLOCK, 0)
        high = jnp.where(number == place[1] - 1, 2 * BLOCK, 3 * BLOCK)
        valid = (col >= low) & ((col < high) | (col >= 3 * BLOCK))
        for h in range(heads):
            hs = slice(h * DH, (h + 1) * DH)
            picks = []
            for r in range(RANDOM):
                slot = slots[(h * blocks + b) * RANDOM + r]
                at = pl.multiple_of((slot & 31) * 2 * BLOCK, 2 * BLOCK)
                picks.append((slot >> 5, at))
            keys = jnp.concatenate(
                [kpad[win_rows, hs]]
                + [held[p[0], pl.ds(p[1], BLOCK)] for p in picks]
                + [glob[g, 0, :, hs] for g in range(GLOBAL)],
                axis=0,
            )
            values = jnp.concatenate(
                [vpad[win_rows, hs]]
                + [held[p[0], pl.ds(p[1] + BLOCK, BLOCK)] for p in picks]
                + [glob[g, 1, :, hs] for g in range(GLOBAL)],
                axis=0,
            )
            scores = lax.dot_general(
                q[at_rows, hs], keys, (((1,), (1,)), ((), ())),
                preferred_element_type=jnp.float32,
            ) * scale
            scores = jnp.where(valid, scores, -jnp.inf)
            peak = jnp.max(scores, axis=1, keepdims=True)
            weights = jnp.exp(scores - peak)
            total = jnp.sum(weights, axis=1, keepdims=True)
            summed = jnp.dot(
                weights.astype(jnp.bfloat16), values, preferred_element_type=jnp.float32
            )
            out[at_rows, hs] = (summed / total).astype(jnp.bfloat16)
        return carry

    lax.fori_loop(0, blocks, one_block, 0)


def attended(slots, place, q, k, v, before, after, glob, arrived):
    rows, features = q.shape
    unit = CAP * 2 * BLOCK
    counts = tuple(a.shape[1] // unit * unit for a in arrived)
    vmem = pl.BlockSpec(memory_space=pltpu.VMEM)
    smem = pl.BlockSpec(memory_space=pltpu.SMEM)
    return pl.pallas_call(
        lambda *refs: attend_kernel(counts, *refs),
        out_shape=jax.ShapeDtypeStruct((rows, features), jnp.bfloat16),
        in_specs=[smem, smem]
        + [vmem] * 6
        + [pl.BlockSpec(memory_space=pl.ANY)] * len(arrived),
        out_specs=vmem,
        scratch_shapes=[
            pltpu.VMEM((INPLANE, PLANES * unit, DH), jnp.bfloat16),
            pltpu.SemaphoreType.DMA((len(arrived),)),
            pltpu.VMEM((rows + 2 * BLOCK, features), jnp.bfloat16),
            pltpu.VMEM((rows + 2 * BLOCK, features), jnp.bfloat16),
        ],
        compiler_params=pltpu.CompilerParams(vmem_limit_bytes=VMEM_LIMIT),
        cost_estimate=pl.CostEstimate(
            flops=4 * rows * features * 512, bytes_accessed=12 * 2**20, transcendentals=rows * 4 * 512
        ),
        name="attend",
    )(slots, place, q, k, v, before, after, glob, *arrived)


def on_device(queries, key_vectors, value_vectors, random_blocks, global_blocks, out_weight):
    shards = lax.axis_size(SEQ)
    my_index = lax.axis_index(SEQ)
    my_plane = lax.axis_index("seq_0")
    rows, features = queries.shape
    heads = features // DH
    blocks = rows // BLOCK
    requests = heads * blocks * RANDOM

    flat = random_blocks.reshape(requests)
    holders = flat // blocks
    number = jnp.arange(requests, dtype=jnp.int32)
    codes = (number // (blocks * RANDOM)) * 16 + flat % blocks
    earlier = (holders[:, None] == holders[None, :]) & (number[None, :] < number[:, None])
    rank = jnp.sum(earlier.astype(jnp.int32), axis=1)
    apart = (holders // INPLANE - my_plane) % PLANES
    order = jnp.where(apart <= PLANES // 2, jnp.minimum(2 * apart, PLANES - 1), 2 * PLANES - 1 - 2 * apart)
    slots = ((holders % INPLANE) * PLANES + order) * CAP + rank
    every = jnp.arange(INPLANE * PLANES * CAP, dtype=jnp.int32)
    asked = jnp.sum(jnp.where(slots[None, :] == every[:, None], codes[None, :], 0), axis=1)
    asked = asked.astype(jnp.bfloat16).reshape(INPLANE, 1, PLANES * CAP)
    asked = jnp.pad(asked, ((0, 0), (0, 15), (0, features - PLANES * CAP)))

    holder = global_blocks // blocks
    spot = global_blocks % blocks
    mine = holder == my_index

    def cut(source, g):
        piece = lax.dynamic_slice_in_dim(source, spot[g] * BLOCK, BLOCK, axis=0)
        return jnp.where(mine[g], piece, jnp.zeros_like(piece))

    asking = jnp.concatenate([cut(queries, g) for g in range(GLOBAL)])
    shared = jnp.concatenate(
        [cut(source, g) for g in range(GLOBAL) for source in (key_vectors, value_vectors)]
    ).reshape(INPLANE, -1, features)
    asking = jnp.broadcast_to(asking[None], (INPLANE, *asking.shape))
    found = jnp.concatenate([asking, shared, asked], axis=1)
    up_k, down_v = ring_step(key_vectors, 1), ring_step(value_vectors, -1)
    up_v, down_k = ring_step(value_vectors, 1), ring_step(key_vectors, -1)
    me = lax.axis_index("heads")
    peers = lax.axis_size("heads")
    width = out_weight.shape[1] // peers
    weights = [
        lax.dynamic_slice_in_dim(out_weight, ((me + away) % peers) * width, width, axis=1)
        for away in (0, 1, -1, 2)
    ]
    ends = jnp.concatenate([key_vectors[rows - BLOCK :], value_vectors[rows - BLOCK :]])
    starts = jnp.concatenate([key_vectors[:BLOCK], value_vectors[:BLOCK]])
    found, ends, starts, weights, _, _ = lax.optimization_barrier(
        (found, ends, starts, weights, up_k, down_v)
    )
    found = over_plane(found)
    many = GLOBAL * BLOCK
    asking = found[:, :many].sum(axis=0)
    shared = found[:, many:-16].sum(axis=0)
    asked = found[:, -16, : PLANES * CAP].astype(jnp.int32).reshape(-1)

    asked, _, _ = lax.optimization_barrier((asked, up_v, down_k))
    picks = picked(asked, 0, [key_vectors, value_vectors])
    arrived = [over_plane(picks)]
    shared = jnp.broadcast_to(shared[None], (PLANES, *shared.shape))
    shared = lax.all_to_all(shared, "seq_0", split_axis=0, concat_axis=0, tiled=True).sum(axis=0)
    shared = jnp.broadcast_to(shared[None], (INPLANE, *shared.shape))
    glob = over_plane(shared).reshape(GLOBAL, 2, BLOCK, features)
    ahead = [(i, i + 1) for i in range(shards - 1)]
    back = [(j, i) for i, j in ahead]
    first, parts = 1, ()
    beside = [lax.ppermute(ends, SEQ, ahead), lax.ppermute(starts, SEQ, back)]
    held = [up_k, down_k, up_v, down_v]
    for step in range(2, PLANES // 2 + 1):
        if step == PLANES // 2:
            up_k, down_v, _ = lax.optimization_barrier((up_k, down_v, held))
        up_k = ring_step(up_k, 1)
        down_v = ring_step(down_v, -1)
        gate = (up_k, down_v) if step < PLANES // 2 else ()
        held, _, _, beside, parts = lax.optimization_barrier(
            (held, gate, picks, beside, parts)
        )
        if step == 2:
            before, after = beside
        else:
            weights[step - 2] = beside
        beside, _ = lax.optimization_barrier((weights[step - 1], held))
        beside = across(beside, (1, -1, 2)[step - 2])
        picks = picked(asked, first, held)
        arrived.append(over_plane(picks))
        first += len(held) // 2
        both = held
        if step == 2:
            both = [*held[:2], key_vectors, *held[2:], value_vectors]
        parts = (global_parts(asking, both, parts),)
        if step < PLANES // 2:
            up_v = ring_step(up_v, 1)
            down_k = ring_step(down_k, -1)
            held = [up_k, down_k, up_v, down_v]
        else:
            held = [up_k, down_v]
    weights[3] = beside
    held, arrived, parts, glob = lax.optimization_barrier((held, arrived, parts, glob))
    parts = (global_parts(asking, held, parts),)
    arrived.append(over_plane(picked(asked, first, held, parts)))
    gout = over_plane(merged(arrived[-1]))

    place = jnp.concatenate(
        [
            jnp.stack([my_index * blocks, jnp.int32(shards * blocks)]).astype(jnp.int32),
            jnp.where(mine, spot, -1).astype(jnp.int32),
        ]
    )
    attention = attended(
        slots, place, queries, key_vectors, value_vectors, before, after, glob, arrived
    )
    own_t, own_b = patched(place, gout, attention)
    right_t, left_b = across(own_t, 1), across(own_b, -1)
    right_b, left_t = across(own_b, 1), across(own_t, -1)
    far_t, far_b = across(right_t, 1), across(left_b, -1)

    def product(*pieces):
        total = 0.0
        for piece, weight in zip(pieces, weights):
            total = total + jnp.dot(piece, weight, preferred_element_type=jnp.float32)
        return total.astype(jnp.bfloat16)

    return jnp.concatenate(
        [product(own_t, right_t, left_t, far_t), product(own_b, right_b, left_b, far_b)]
    )


def solution(mesh):
    torus = Mesh(
        mesh.devices.reshape(mesh.shape["heads"], 8, 4, 2), ("heads", "seq_0", "seq_1", "seq_2")
    )
    in_specs = (
        P(SEQ, "heads"),
        P(SEQ, "heads"),
        P(SEQ, "heads"),
        P("heads", SEQ, None),
        P(),
        P("heads", None),
    )
    out_specs = P(SEQ, "heads")
    return jax.shard_map(
        on_device, mesh=torus, in_specs=in_specs, out_specs=out_specs, check_vma=False
    )
```

```python
import jax
import jax.numpy as jnp
from jax import lax
from jax.experimental import pallas as pl
from jax.experimental.pallas import tpu as pltpu
from jax.sharding import Mesh
from jax.sharding import PartitionSpec as P

DH = 128
BLOCK = 64
RANDOM = 3
GLOBAL = 2
CAP = 4
PLANES = 8
INPLANE = 8
SEQ = ("seq_0", "seq_1", "seq_2")
PLANE = ("seq_1", "seq_2")
VMEM_LIMIT = 56 * 2**20
COST = 24 * 2**20


def ring_step(shard, step):
    peers = lax.axis_size("seq_0")
    return lax.ppermute(shard, "seq_0", [(i, (i + step) % peers) for i in range(peers)])


def across(shard, step):
    peers = lax.axis_size("heads")
    return lax.ppermute(shard, "heads", [(i, (i + step) % peers) for i in range(peers)])


def pick_kernel(n, first, codes, *refs):
    keys, values = refs[:n], refs[n : 2 * n]
    extra, out = refs[2 * n : -1], refs[-1]

    def one_peer(peer, carry):
        for run in range(n):
            for rank in range(CAP):
                code = codes[(peer * PLANES + first + run) * CAP + rank]
                rows = pl.ds(pl.multiple_of((code & 15) * BLOCK, BLOCK), BLOCK)
                cols = pl.ds(pl.multiple_of((code >> 4) * DH, DH), DH)
                at = (run * CAP + rank) * 2 * BLOCK
                out[peer, at : at + BLOCK] = keys[run][rows, cols]
                out[peer, at + BLOCK : at + 2 * BLOCK] = values[run][rows, cols]
        if extra:
            own = extra[0][pl.ds(pl.multiple_of(peer * BLOCK, BLOCK), BLOCK)].astype(out.dtype)
            at = n * CAP * 2 * BLOCK
            out[peer, at : at + BLOCK] = own[:, :DH]
            out[peer, at + BLOCK : at + 2 * BLOCK] = own[:, DH:]
        return carry

    lax.fori_loop(0, INPLANE, one_peer, 0)


def picked(codes, first, blocks, extra=()):
    n = len(blocks) // 2
    shape = (INPLANE, (n * CAP + len(extra)) * 2 * BLOCK, DH)
    size = 2 * (sum(k.size for k in blocks) + INPLANE * n * CAP * 2 * BLOCK * DH)
    vmem = pl.BlockSpec(memory_space=pltpu.VMEM)
    return pl.pallas_call(
        lambda *refs: pick_kernel(n, first, *refs),
        out_shape=jax.ShapeDtypeStruct(shape, jnp.bfloat16),
        in_specs=[pl.BlockSpec(memory_space=pltpu.SMEM)] + [vmem] * (2 * n + len(extra)),
        out_specs=vmem,
        compiler_params=pltpu.CompilerParams(vmem_limit_bytes=32 * 2**20),
        cost_estimate=pl.CostEstimate(flops=0, bytes_accessed=24 * 2**20, transcendentals=0),
        name="pick_blocks",
    )(codes, *blocks, *extra)


def over_plane(parts):
    return lax.all_to_all(parts, PLANE, split_axis=0, concat_axis=0, tiled=True)


def global_kernel(n, asking, *refs):
    keys, values = refs[:n], refs[n : 2 * n]
    held, out = refs[2 * n : -1], refs[-1]
    heads = asking.shape[1] // DH
    many = GLOBAL * BLOCK
    lane = lax.broadcasted_iota(jnp.int32, (many, DH), 1)
    for h in range(heads):
        hs = slice(h * DH, (h + 1) * DH)
        rows = slice(h * many, (h + 1) * many)
        scores = [
            lax.dot_general(
                asking[:, hs], k[:, hs], (((1,), (1,)), ((), ())),
                preferred_element_type=jnp.float32,
            ) * (DH ** (-0.5))
            for k in keys
        ]
        top = jnp.max(scores[0], axis=1, keepdims=True)
        for other in scores[1:]:
            top = jnp.maximum(top, jnp.max(other, axis=1, keepdims=True))
        top = top.astype(jnp.bfloat16).astype(jnp.float32)
        if held:
            before = held[0][rows, DH : DH + 1]
            top = jnp.maximum(top, before)
            scale = jnp.exp(before - top)
            part = held[0][rows, :DH] * scale
            total = held[0][rows, DH + 1 : DH + 2] * scale
        else:
            part = jnp.zeros((many, DH), jnp.float32)
            total = jnp.zeros((many, 1), jnp.float32)
        for score, v in zip(scores, values):
            weights = jnp.exp(score - top)
            total += jnp.sum(weights, axis=1, keepdims=True)
            part += jnp.dot(
                weights.astype(jnp.bfloat16), v[:, hs], preferred_element_type=jnp.float32
            )
        upper = total.astype(jnp.bfloat16).astype(jnp.float32)
        side = jnp.where(lane == 0, top, jnp.where(lane == 1, total, 0.0))
        side = jnp.where(lane == 2, upper, jnp.where(lane == 3, total - upper, side))
        out[rows] = jnp.concatenate([part, side], axis=1)


def global_parts(asking, blocks, held=()):
    n = len(blocks) // 2
    vmem = pl.BlockSpec(memory_space=pltpu.VMEM)
    rows = asking.shape[0] * asking.shape[1] // DH
    return pl.pallas_call(
        lambda *refs: global_kernel(n, *refs),
        out_shape=jax.ShapeDtypeStruct((rows, 2 * DH), jnp.float32),
        in_specs=[vmem] * (1 + len(blocks) + len(held)),
        out_specs=vmem,
        compiler_params=pltpu.CompilerParams(vmem_limit_bytes=32 * 2**20),
        cost_estimate=pl.CostEstimate(
            flops=4 * rows * DH * 768 * n, bytes_accessed=24 * 2**20, transcendentals=rows * 768 * n
        ),
        name="global_parts",
    )(asking, *blocks, *held)


def merge_rows(parts, first, out):
    peers = parts.shape[0]
    sums, side = slice(first, first + BLOCK), slice(first + BLOCK, first + 2 * BLOCK)
    tops = [parts[p, side, 0:1].astype(jnp.float32) for p in range(peers)]
    top = tops[0]
    for other in tops[1:]:
        top = jnp.maximum(top, other)
    part = jnp.zeros((BLOCK, DH), jnp.float32)
    total = jnp.zeros((BLOCK, 1), jnp.float32)
    for p, own in enumerate(tops):
        scale = jnp.exp(own - top)
        part += scale * parts[p, sums].astype(jnp.float32)
        upper = parts[p, side, 2:3].astype(jnp.float32)
        total += scale * (upper + parts[p, side, 3:4].astype(jnp.float32))
    whole = (part / total).astype(jnp.bfloat16)
    for p in range(peers):
        out[p] = whole


def joined_kernel(low, gout, out):
    rows = low.shape[0]
    out[:rows] = low[...]
    for h in range(low.shape[1] // DH):
        for g in range(GLOBAL):
            at = rows + g * BLOCK
            out[at : at + BLOCK, h * DH : (h + 1) * DH] = gout[h * GLOBAL + g]


def joined(low, gout):
    vmem = pl.BlockSpec(memory_space=pltpu.VMEM)
    return pl.pallas_call(
        joined_kernel,
        out_shape=jax.ShapeDtypeStruct((low.shape[0] + GLOBAL * BLOCK, low.shape[1]), low.dtype),
        in_specs=[vmem, vmem],
        out_specs=vmem,
        name="join_global_rows",
    )(low, gout)


def place_kernel(place, top, low, out):
    half = top.shape[0]
    out[:half] = top[...]
    out[half:] = low[:half]
    for g in range(GLOBAL):

        @pl.when(place[2 + g] >= 0)
        def _():
            at_rows = pl.ds(pl.multiple_of(place[2 + g] * BLOCK, BLOCK), BLOCK)
            out[at_rows] = low[half + g * BLOCK : half + (g + 1) * BLOCK]


def placed(place, top, low):
    vmem = pl.BlockSpec(memory_space=pltpu.VMEM)
    return pl.pallas_call(
        place_kernel,
        out_shape=jax.ShapeDtypeStruct((2 * top.shape[0], top.shape[1]), top.dtype),
        in_specs=[pl.BlockSpec(memory_space=pltpu.SMEM), vmem, vmem],
        out_specs=vmem,
        compiler_params=pltpu.CompilerParams(vmem_limit_bytes=16 * 2**20),
        name="place_global_rows",
    )(place, top, low)


def attend_kernel(counts, slots, place, q, k, v, before, after, glob, *refs):
    n = len(counts)
    arrived, acc, stats, held, sems = refs[:n], refs[n], refs[n + 1], refs[n + 2], refs[n + 3]
    kpad, vpad = refs[n + 4], refs[n + 5]
    copies = []
    at = 0
    for part, count in enumerate(counts):
        copies.append(
            pltpu.make_async_copy(arrived[part], held.at[:, pl.ds(at, count)], sems.at[part])
        )
        copies[-1].start()
        at += count
    rows = q.shape[0]
    heads = q.shape[1] // DH
    blocks = rows // BLOCK
    for side, (pad, own) in enumerate(((kpad, k), (vpad, v))):
        pad[0:BLOCK] = before[side * BLOCK : (side + 1) * BLOCK]
        pad[BLOCK : BLOCK + rows] = own[...]
        pad[BLOCK + rows :] = after[side * BLOCK : (side + 1) * BLOCK]
    for copy in copies:
        copy.wait()
    scale = DH ** (-0.5)
    col = lax.broadcasted_iota(jnp.int32, (1, (3 + RANDOM + GLOBAL) * BLOCK), 1) // BLOCK
    lane = lax.broadcasted_iota(jnp.int32, (BLOCK, DH), 1)

    def one_block(b, carry):
        at_rows = pl.ds(pl.multiple_of(b * BLOCK, BLOCK), BLOCK)
        win_rows = pl.ds(pl.multiple_of(b * BLOCK, BLOCK), 3 * BLOCK)
        number = place[0] + b
        outside = jnp.where(number == 0, 0, -1), jnp.where(number == place[1] - 1, 2, -1)
        for h in range(heads):
            hs = slice(h * DH, (h + 1) * DH)
            picks = []
            bias = jnp.where((col == outside[0]) | (col == outside[1]), -jnp.inf, 0.0)
            for r in range(RANDOM):
                slot = slots[(h * blocks + b) * RANDOM + r]
                late = ((slot >> 2) & 7) == PLANES - 1
                bias = jnp.where(col == jnp.where(late, 3 + r, -1), -jnp.inf, bias)
                slot = jnp.where(late, 0, slot)
                picks.append((slot >> 5, pl.multiple_of((slot & 31) * 2 * BLOCK, 2 * BLOCK)))
            keys = jnp.concatenate(
                [kpad[win_rows, hs]]
                + [held[p[0], pl.ds(p[1], BLOCK)] for p in picks]
                + [glob[g, 0, :, hs] for g in range(GLOBAL)],
                axis=0,
            )
            values = jnp.concatenate(
                [vpad[win_rows, hs]]
                + [held[p[0], pl.ds(p[1] + BLOCK, BLOCK)] for p in picks]
                + [glob[g, 1, :, hs] for g in range(GLOBAL)],
                axis=0,
            )
            scores = lax.dot_general(
                q[at_rows, hs], keys, (((1,), (1,)), ((), ())),
                preferred_element_type=jnp.float32,
            ) * scale + bias
            peak = jnp.max(scores, axis=1, keepdims=True)
            weights = jnp.exp(scores - peak)
            total = jnp.sum(weights, axis=1, keepdims=True)
            acc[at_rows, hs] = jnp.dot(
                weights.astype(jnp.bfloat16), values, preferred_element_type=jnp.float32
            )
            stats[h, at_rows] = jnp.where(lane < DH // 2, peak, total)
        return carry

    lax.fori_loop(0, blocks, one_block, 0)


def attended(slots, place, q, k, v, before, after, glob, arrived):
    rows, features = q.shape
    counts = tuple(a.shape[1] for a in arrived)
    vmem = pl.BlockSpec(memory_space=pltpu.VMEM)
    smem = pl.BlockSpec(memory_space=pltpu.SMEM)
    return pl.pallas_call(
        lambda *refs: attend_kernel(counts, *refs),
        out_shape=(
            jax.ShapeDtypeStruct((rows, features), jnp.float32),
            jax.ShapeDtypeStruct((features // DH, rows, DH), jnp.float32),
        ),
        in_specs=[smem, smem] + [vmem] * 6 + [pl.BlockSpec(memory_space=pl.ANY)] * len(arrived),
        out_specs=(vmem, vmem),
        scratch_shapes=[
            pltpu.VMEM((INPLANE, sum(counts), DH), jnp.bfloat16),
            pltpu.SemaphoreType.DMA((len(arrived),)),
            pltpu.VMEM((rows + 2 * BLOCK, features), jnp.bfloat16),
            pltpu.VMEM((rows + 2 * BLOCK, features), jnp.bfloat16),
        ],
        compiler_params=pltpu.CompilerParams(vmem_limit_bytes=VMEM_LIMIT),
        cost_estimate=pl.CostEstimate(
            flops=4 * rows * features * 512, bytes_accessed=COST, transcendentals=rows * 4 * 512
        ),
        name="attend",
    )(slots, place, q, k, v, before, after, glob, *arrived)


def finish_kernel(late, q, acc, stats, blocks_late, top, low, gout, summed, held):
    scale = DH ** (-0.5)
    lane = lax.broadcasted_iota(jnp.int32, (BLOCK, DH), 1)
    summed[...] = acc[...]
    held[...] = stats[...]

    def one_late(i, carry):
        code = late[i]

        @pl.when(code >= 0)
        def _():
            h = code >> 4
            at_rows = pl.ds(pl.multiple_of((code & 15) * BLOCK, BLOCK), BLOCK)
            cols = pl.ds(pl.multiple_of(h * DH, DH), DH)
            at = pl.multiple_of((i & (CAP - 1)) * 2 * BLOCK, 2 * BLOCK)
            peer = i // CAP
            scores = lax.dot_general(
                q[at_rows, cols], blocks_late[peer, pl.ds(at, BLOCK)], (((1,), (1,)), ((), ())),
                preferred_element_type=jnp.float32,
            ) * scale
            before = held[h, at_rows, 0:1]
            peak = jnp.maximum(before, jnp.max(scores, axis=1, keepdims=True))
            weights = jnp.exp(scores - peak)
            less = jnp.exp(before - peak)
            total = held[h, at_rows, DH // 2 : DH // 2 + 1] * less
            total += jnp.sum(weights, axis=1, keepdims=True)
            summed[at_rows, cols] = summed[at_rows, cols] * less + jnp.dot(
                weights.astype(jnp.bfloat16), blocks_late[peer, pl.ds(at + BLOCK, BLOCK)],
                preferred_element_type=jnp.float32,
            )
            held[h, at_rows] = jnp.where(lane < DH // 2, peak, total)

        return carry

    lax.fori_loop(0, INPLANE * CAP, one_late, 0)
    merge_rows(blocks_late, 2 * CAP * BLOCK, gout)
    half = top.shape[0]
    for side, out in enumerate((top, low)):

        def one_block(b, carry):
            to_rows = pl.ds(pl.multiple_of(b * BLOCK, BLOCK), BLOCK)
            at_rows = pl.ds(pl.multiple_of(b * BLOCK + side * half, BLOCK), BLOCK)
            for h in range(held.shape[0]):
                hs = slice(h * DH, (h + 1) * DH)
                total = held[h, at_rows, DH // 2 : DH // 2 + 1]
                out[to_rows, hs] = (summed[at_rows, hs] / total).astype(jnp.bfloat16)
            return carry

        lax.fori_loop(0, half // BLOCK, one_block, 0)


def finished(late, q, acc, stats, blocks_late):
    vmem = pl.BlockSpec(memory_space=pltpu.VMEM)
    rows, features = q.shape
    half = jax.ShapeDtypeStruct((rows // 2, features), jnp.bfloat16)
    return pl.pallas_call(
        finish_kernel,
        out_shape=(half, half, jax.ShapeDtypeStruct((INPLANE, BLOCK, DH), jnp.bfloat16)),
        in_specs=[pl.BlockSpec(memory_space=pltpu.SMEM)] + [vmem] * 4,
        out_specs=(vmem, vmem, vmem),
        scratch_shapes=[
            pltpu.VMEM(acc.shape, jnp.float32),
            pltpu.VMEM(stats.shape, jnp.float32),
        ],
        compiler_params=pltpu.CompilerParams(vmem_limit_bytes=32 * 2**20),
        name="late_blocks",
    )(late, q, acc, stats, blocks_late)


def on_device(queries, key_vectors, value_vectors, random_blocks, global_blocks, out_weight):
    shards = lax.axis_size(SEQ)
    my_index = lax.axis_index(SEQ)
    my_plane = lax.axis_index("seq_0")
    rows, features = queries.shape
    heads = features // DH
    blocks = rows // BLOCK
    requests = heads * blocks * RANDOM

    flat = random_blocks.reshape(requests)
    holders = flat // blocks
    number = jnp.arange(requests, dtype=jnp.int32)
    codes = (number // (blocks * RANDOM)) * 16 + flat % blocks
    earlier = (holders[:, None] == holders[None, :]) & (number[None, :] < number[:, None])
    rank = jnp.sum(earlier.astype(jnp.int32), axis=1)
    apart = (holders // INPLANE - my_plane) % PLANES
    order = jnp.where(apart <= PLANES // 2, jnp.minimum(2 * apart, PLANES - 1), 2 * PLANES - 1 - 2 * apart)
    slots = ((holders % INPLANE) * PLANES + order) * CAP + rank
    every = jnp.arange(INPLANE * PLANES * CAP, dtype=jnp.int32)
    asked = jnp.sum(jnp.where(slots[None, :] == every[:, None], codes[None, :], 0), axis=1)
    asker = number // RANDOM
    asker = (asker // blocks) * 16 + asker % blocks + 1
    late = jnp.sum(jnp.where(slots[None, :] == every[:, None], asker[None, :], 0), axis=1) - 1
    late = late.reshape(INPLANE, PLANES, CAP)[:, PLANES - 1].reshape(-1)
    asked = asked.astype(jnp.bfloat16).reshape(INPLANE, 1, PLANES * CAP)
    asked = jnp.pad(asked, ((0, 0), (0, 15), (0, features - PLANES * CAP)))

    holder = global_blocks // blocks
    spot = global_blocks % blocks
    mine = holder == my_index

    def cut(source, g):
        piece = lax.dynamic_slice_in_dim(source, spot[g] * BLOCK, BLOCK, axis=0)
        return jnp.where(mine[g], piece, jnp.zeros_like(piece))

    asking = jnp.concatenate([cut(queries, g) for g in range(GLOBAL)])
    shared = jnp.concatenate(
        [cut(source, g) for g in range(GLOBAL) for source in (key_vectors, value_vectors)]
    ).reshape(INPLANE, -1, features)
    asking = jnp.broadcast_to(asking[None], (INPLANE, *asking.shape))
    found = jnp.concatenate([asking, shared, asked], axis=1)
    up_k, down_v = ring_step(key_vectors, 1), ring_step(value_vectors, -1)
    up_v, down_k = ring_step(value_vectors, 1), ring_step(key_vectors, -1)
    me = lax.axis_index("heads")
    peers = lax.axis_size("heads")
    width = out_weight.shape[1] // peers
    weights = [
        lax.dynamic_slice_in_dim(out_weight, ((me + away) % peers) * width, width, axis=1)
        for away in (0, 1, -1, 2)
    ]
    ends = jnp.concatenate([key_vectors[rows - BLOCK :], value_vectors[rows - BLOCK :]])
    starts = jnp.concatenate([key_vectors[:BLOCK], value_vectors[:BLOCK]])
    found, ends, starts, weights, _, _ = lax.optimization_barrier(
        (found, ends, starts, weights, up_k, down_v)
    )
    found = over_plane(found)
    many = GLOBAL * BLOCK
    asking = found[:, :many].sum(axis=0)
    shared = found[:, many:-16].sum(axis=0)
    asked = found[:, -16, : PLANES * CAP].astype(jnp.int32).reshape(-1)

    asked, _, _ = lax.optimization_barrier((asked, up_v, down_k))
    picks = picked(asked, 0, [key_vectors, value_vectors])
    arrived = [over_plane(picks)]
    ahead = [(i, i + 1) for i in range(shards - 1)]
    back = [(j, i) for i, j in ahead]
    first, parts = 1, ()
    beside = [lax.ppermute(ends, SEQ, ahead), lax.ppermute(starts, SEQ, back)]
    held = [up_k, down_k, up_v, down_v]
    first_pair = (up_v, down_k)
    for step in range(2, PLANES // 2 + 1):
        if step > 2:
            up_k, down_v, _ = lax.optimization_barrier((up_k, down_v, held if step == PLANES // 2 else first_pair))
        up_k = ring_step(up_k, 1)
        down_v = ring_step(down_v, -1)
        if step > 2:
            shared, _ = lax.optimization_barrier((shared, arrived[-1]))
        if step == 3:
            shared = jnp.broadcast_to(shared[None], (PLANES, *shared.shape))
            shared = lax.all_to_all(shared, "seq_0", split_axis=0, concat_axis=0, tiled=True)
            shared = shared.sum(axis=0)
        elif step == 4:
            shared = over_plane(jnp.broadcast_to(shared[None], (INPLANE, *shared.shape)))
            glob = shared.reshape(GLOBAL, 2, BLOCK, features)
        if step < PLANES // 2:
            up_v, down_k, _ = lax.optimization_barrier((up_v, down_k, picks))
        gate = (up_k, down_v) if step < PLANES // 2 else ()
        held, _, _, tied, parts = lax.optimization_barrier(
            (held, gate, arrived[-1], beside if step > 2 else (), parts)
        )
        if step > 2:
            weights[step - 2], before, after = tied
        else:
            before, after = beside
        beside, _ = lax.optimization_barrier((weights[step - 1], held))
        beside = (across(beside, (1, -1, 2)[step - 2]), before, after)
        picks = picked(asked, first, held)
        arrived.append(over_plane(picks))
        first += len(held) // 2
        both = held
        if step == 2:
            both = [*held[:2], key_vectors, *held[2:], value_vectors]
        parts = (global_parts(asking, both, parts),)
        if step < PLANES // 2:
            up_v = ring_step(up_v, 1)
            down_k = ring_step(down_k, -1)
            held = [up_k, down_k, up_v, down_v]
        else:
            held = [up_k, down_v]
    weights[3], before, after = beside
    held, arrived, parts, glob = lax.optimization_barrier((held, arrived, parts, glob))
    parts = (global_parts(asking, held, parts),)
    arrived.append(over_plane(picked(asked, first, held, parts)))
    place = jnp.concatenate(
        [
            jnp.stack([my_index * blocks, jnp.int32(shards * blocks)]).astype(jnp.int32),
            jnp.where(mine, spot, -1).astype(jnp.int32),
        ]
    )
    acc, stats = attended(
        slots, place, queries, key_vectors, value_vectors, before, after, glob, arrived[:-1]
    )
    own_t, own_b, gout = finished(late, queries, acc, stats, arrived[-1])
    right_t, left_t = across(own_t, 1), across(own_t, -1)
    own_b = joined(own_b, over_plane(gout))
    right_b, left_b = across(own_b, 1), across(own_b, -1)
    far_t, far_b = across(right_t, 1), across(left_b, -1)

    def product(*pieces):
        total = 0.0
        for piece, weight in zip(pieces, weights):
            total = total + jnp.dot(piece, weight, preferred_element_type=jnp.float32)
        return total.astype(jnp.bfloat16)

    return placed(
        place, product(own_t, right_t, left_t, far_t), product(own_b, right_b, left_b, far_b)
    )


def solution(mesh):
    torus = Mesh(
        mesh.devices.reshape(mesh.shape["heads"], 8, 4, 2), ("heads", "seq_0", "seq_1", "seq_2")
    )
    in_specs = (
        P(SEQ, "heads"),
        P(SEQ, "heads"),
        P(SEQ, "heads"),
        P("heads", SEQ, None),
        P(),
        P("heads", None),
    )
    out_specs = P(SEQ, "heads")
    return jax.shard_map(
        on_device, mesh=torus, in_specs=in_specs, out_specs=out_specs, check_vma=False
    )
```

```python
import jax
import jax.numpy as jnp
from jax import lax
from jax.experimental import pallas as pl
from jax.experimental.pallas import tpu as pltpu
from jax.sharding import Mesh
from jax.sharding import PartitionSpec as P

DH = 128
BLOCK = 64
RANDOM = 3
GLOBAL = 2
CAP = 4
PLANES = 8
INPLANE = 8
SEQ = ("seq_0", "seq_1", "seq_2")
PLANE = ("seq_1", "seq_2")
VMEM_LIMIT = 56 * 2**20
COST = 24 * 2**20


def ring_step(shard, step):
    peers = lax.axis_size("seq_0")
    return lax.ppermute(shard, "seq_0", [(i, (i + step) % peers) for i in range(peers)])


def across(shard, step):
    peers = lax.axis_size("heads")
    return lax.ppermute(shard, "heads", [(i, (i + step) % peers) for i in range(peers)])


def pick_kernel(n, first, codes, *refs):
    keys, values = refs[:n], refs[n : 2 * n]
    extra, out = refs[2 * n : -1], refs[-1]

    def one_peer(peer, carry):
        for run in range(n):
            for rank in range(CAP):
                code = codes[(peer * PLANES + first + run) * CAP + rank]
                rows = pl.ds(pl.multiple_of((code & 15) * BLOCK, BLOCK), BLOCK)
                cols = pl.ds(pl.multiple_of((code >> 4) * DH, DH), DH)
                at = (run * CAP + rank) * 2 * BLOCK
                out[peer, at : at + BLOCK] = keys[run][rows, cols]
                out[peer, at + BLOCK : at + 2 * BLOCK] = values[run][rows, cols]
        at = n * CAP * 2 * BLOCK
        if extra and extra[0].shape[0] < BLOCK:
            few = extra[0].shape[0]
            for h in range(extra[0].shape[1] // DH):
                out[peer, at + h * few : at + (h + 1) * few] = extra[0][:, h * DH : (h + 1) * DH]
        elif extra:
            own = extra[0][pl.ds(pl.multiple_of(peer * BLOCK, BLOCK), BLOCK)].astype(out.dtype)
            out[peer, at : at + BLOCK] = own[:, :DH]
            out[peer, at + BLOCK : at + 2 * BLOCK] = own[:, DH:]
        return carry

    lax.fori_loop(0, INPLANE, one_peer, 0)


def picked(codes, first, blocks, extra=()):
    n = len(blocks) // 2
    tail = sum(e.size if e.shape[0] < BLOCK else e.size // INPLANE for e in extra) // DH
    shape = (INPLANE, n * CAP * 2 * BLOCK + tail, DH)
    size = 2 * (sum(k.size for k in blocks) + INPLANE * n * CAP * 2 * BLOCK * DH)
    vmem = pl.BlockSpec(memory_space=pltpu.VMEM)
    return pl.pallas_call(
        lambda *refs: pick_kernel(n, first, *refs),
        out_shape=jax.ShapeDtypeStruct(shape, jnp.bfloat16),
        in_specs=[pl.BlockSpec(memory_space=pltpu.SMEM)] + [vmem] * (2 * n + len(extra)),
        out_specs=vmem,
        compiler_params=pltpu.CompilerParams(vmem_limit_bytes=32 * 2**20),
        cost_estimate=pl.CostEstimate(flops=0, bytes_accessed=24 * 2**20, transcendentals=0),
        name="pick_blocks",
    )(codes, *blocks, *extra)


def over_plane(parts):
    return lax.all_to_all(parts, PLANE, split_axis=0, concat_axis=0, tiled=True)


def global_kernel(n, asking, *refs):
    keys, values = refs[:n], refs[n : 2 * n]
    held, out = refs[2 * n : -1], refs[-1]
    heads = asking.shape[1] // DH
    many = GLOBAL * BLOCK
    lane = lax.broadcasted_iota(jnp.int32, (many, DH), 1)
    for h in range(heads):
        hs = slice(h * DH, (h + 1) * DH)
        rows = slice(h * many, (h + 1) * many)
        scores = [
            lax.dot_general(
                asking[:, hs], k[:, hs], (((1,), (1,)), ((), ())),
                preferred_element_type=jnp.float32,
            ) * (DH ** (-0.5))
            for k in keys
        ]
        top = jnp.max(scores[0], axis=1, keepdims=True)
        for other in scores[1:]:
            top = jnp.maximum(top, jnp.max(other, axis=1, keepdims=True))
        top = top.astype(jnp.bfloat16).astype(jnp.float32)
        if held:
            before = held[0][rows, DH : DH + 1]
            top = jnp.maximum(top, before)
            scale = jnp.exp(before - top)
            part = held[0][rows, :DH] * scale
            total = held[0][rows, DH + 1 : DH + 2] * scale
        else:
            part = jnp.zeros((many, DH), jnp.float32)
            total = jnp.zeros((many, 1), jnp.float32)
        for score, v in zip(scores, values):
            weights = jnp.exp(score - top)
            total += jnp.sum(weights, axis=1, keepdims=True)
            part += jnp.dot(
                weights.astype(jnp.bfloat16), v[:, hs], preferred_element_type=jnp.float32
            )
        upper = total.astype(jnp.bfloat16).astype(jnp.float32)
        side = jnp.where(lane == 0, top, jnp.where(lane == 1, total, 0.0))
        side = jnp.where(lane == 2, upper, jnp.where(lane == 3, total - upper, side))
        out[rows] = jnp.concatenate([part, side], axis=1)


def global_parts(asking, blocks, held=()):
    n = len(blocks) // 2
    vmem = pl.BlockSpec(memory_space=pltpu.VMEM)
    rows = asking.shape[0] * asking.shape[1] // DH
    return pl.pallas_call(
        lambda *refs: global_kernel(n, *refs),
        out_shape=jax.ShapeDtypeStruct((rows, 2 * DH), jnp.float32),
        in_specs=[vmem] * (1 + len(blocks) + len(held)),
        out_specs=vmem,
        compiler_params=pltpu.CompilerParams(vmem_limit_bytes=32 * 2**20),
        cost_estimate=pl.CostEstimate(
            flops=4 * rows * DH * 768 * n, bytes_accessed=24 * 2**20, transcendentals=rows * 768 * n
        ),
        name="global_parts",
    )(asking, *blocks, *held)


def merge_rows(parts, first, out):
    peers = parts.shape[0]
    sums, side = slice(first, first + BLOCK), slice(first + BLOCK, first + 2 * BLOCK)
    tops = [parts[p, side, 0:1].astype(jnp.float32) for p in range(peers)]
    top = tops[0]
    for other in tops[1:]:
        top = jnp.maximum(top, other)
    part = jnp.zeros((BLOCK, DH), jnp.float32)
    total = jnp.zeros((BLOCK, 1), jnp.float32)
    for p, own in enumerate(tops):
        scale = jnp.exp(own - top)
        part += scale * parts[p, sums].astype(jnp.float32)
        upper = parts[p, side, 2:3].astype(jnp.float32)
        total += scale * (upper + parts[p, side, 3:4].astype(jnp.float32))
    whole = (part / total).astype(jnp.bfloat16)
    for p in range(peers):
        out[p] = whole


def times(pieces, weights):
    total = jnp.dot(pieces[0][...], weights[0][...], preferred_element_type=jnp.float32)
    for piece, weight in zip(pieces[1:], weights[1:]):
        total += jnp.dot(piece[...], weight[...], preferred_element_type=jnp.float32)
    return total.astype(jnp.bfloat16)


def upper_kernel(*refs):
    refs[8][...] = times(refs[:4], refs[4:8])


def lower_kernel(place, top, *refs):
    low, rows, weights, out = refs[:4], refs[4:8], refs[8:12], refs[12]
    half = top.shape[0]
    out[:half] = top[...]
    out[half:] = times(low, weights)
    replaced = times(rows, weights)
    for g in range(GLOBAL):

        @pl.when(place[2 + g] >= 0)
        def _():
            at_rows = pl.ds(pl.multiple_of(place[2 + g] * BLOCK, BLOCK), BLOCK)
            out[at_rows] = replaced[g * BLOCK : (g + 1) * BLOCK]


def product(pieces, weights, place=None, top=None, rows=()):
    features, width = weights[0].shape
    step = width // 4
    whole = [pl.BlockSpec(p.shape, lambda i: (0, 0)) for p in (*pieces, *rows)]
    sliced = [pl.BlockSpec((features, step), lambda i: (0, i))] * 4
    head = [] if top is None else [place, top]
    half = pieces[0].shape[0]
    tall = half if top is None else 2 * half
    specs = [] if top is None else [
        pl.BlockSpec(memory_space=pltpu.SMEM), pl.BlockSpec((half, step), lambda i: (0, i))
    ]
    return pl.pallas_call(
        upper_kernel if top is None else lower_kernel,
        out_shape=jax.ShapeDtypeStruct((tall, width), jnp.bfloat16),
        grid=(4,),
        in_specs=specs + whole + sliced,
        out_specs=pl.BlockSpec((tall, step), lambda i: (0, i)),
        compiler_params=pltpu.CompilerParams(vmem_limit_bytes=32 * 2**20),
        cost_estimate=pl.CostEstimate(
            flops=8 * half * features * width, bytes_accessed=8 * 2**20, transcendentals=0
        ),
        name="upper_product" if top is None else "lower_product",
    )(*head, *pieces, *rows, *weights)


def attend_kernel(counts, slots, place, q, k, v, before, after, *refs):
    n = len(counts)
    arrived, acc, stats, held, sems = refs[:n], refs[n], refs[n + 1], refs[n + 2], refs[n + 3]
    kpad, vpad = refs[n + 4], refs[n + 5]
    copies = []
    at = 0
    for part, count in enumerate(counts):
        copies.append(
            pltpu.make_async_copy(arrived[part], held.at[:, pl.ds(at, count)], sems.at[part])
        )
        copies[-1].start()
        at += count
    rows = q.shape[0]
    heads = q.shape[1] // DH
    blocks = rows // BLOCK
    for side, (pad, own) in enumerate(((kpad, k), (vpad, v))):
        pad[0:BLOCK] = before[side * BLOCK : (side + 1) * BLOCK]
        pad[BLOCK : BLOCK + rows] = own[...]
        pad[BLOCK + rows :] = after[side * BLOCK : (side + 1) * BLOCK]
    for copy in copies:
        copy.wait()
    scale = DH ** (-0.5)
    col = lax.broadcasted_iota(jnp.int32, (1, (3 + RANDOM + GLOBAL) * BLOCK), 1) // BLOCK
    lane = lax.broadcasted_iota(jnp.int32, (BLOCK, DH), 1)
    few = GLOBAL * 2 * BLOCK // INPLANE

    def one_block(b, carry):
        at_rows = pl.ds(pl.multiple_of(b * BLOCK, BLOCK), BLOCK)
        win_rows = pl.ds(pl.multiple_of(b * BLOCK, BLOCK), 3 * BLOCK)
        number = place[0] + b
        outside = jnp.where(number == 0, 0, -1), jnp.where(number == place[1] - 1, 2, -1)
        for pair in range(0, heads, 2):
            both = range(pair, pair + 2)
            found, scores = [], []
            for h in both:
                hs = slice(h * DH, (h + 1) * DH)
                picks = []
                bias = jnp.where((col == outside[0]) | (col == outside[1]), -jnp.inf, 0.0)
                for r in range(RANDOM):
                    slot = slots[(h * blocks + b) * RANDOM + r]
                    late = ((slot >> 2) & 7) == PLANES - 1
                    bias = jnp.where(col == jnp.where(late, 3 + r, -1), -jnp.inf, bias)
                    slot = jnp.where(late, 0, slot)
                    picks.append((slot >> 5, pl.multiple_of((slot & 31) * 2 * BLOCK, 2 * BLOCK)))
                found.append(picks)
                at = sum(counts) + (h - heads) * few
                keys = jnp.concatenate(
                    [kpad[win_rows, hs]]
                    + [held[p[0], pl.ds(p[1], BLOCK)] for p in picks]
                    + [held[4 * g + i, at : at + few] for g in range(GLOBAL) for i in range(2)],
                    axis=0,
                )
                scores.append(
                    lax.dot_general(
                        q[at_rows, hs], keys, (((1,), (1,)), ((), ())),
                        preferred_element_type=jnp.float32,
                    ) * scale + bias
                )
            peaks = [jnp.max(own, axis=1, keepdims=True) for own in scores]
            weights = [jnp.exp(own - peak) for own, peak in zip(scores, peaks)]
            totals = [jnp.sum(own, axis=1, keepdims=True) for own in weights]
            sums = []
            for h, picks, own in zip(both, found, weights):
                hs = slice(h * DH, (h + 1) * DH)
                at = sum(counts) + (h - heads) * few
                values = jnp.concatenate(
                    [vpad[win_rows, hs]]
                    + [held[p[0], pl.ds(p[1] + BLOCK, BLOCK)] for p in picks]
                    + [held[4 * g + 2 + i, at : at + few] for g in range(GLOBAL) for i in range(2)],
                    axis=0,
                )
                sums.append(
                    jnp.dot(own.astype(jnp.bfloat16), values, preferred_element_type=jnp.float32)
                )
            for h, own, peak, total in zip(both, sums, peaks, totals):
                acc[at_rows, h * DH : (h + 1) * DH] = own
                stats[h, at_rows] = jnp.where(lane < DH // 2, peak, total)
        return carry

    lax.fori_loop(0, blocks, one_block, 0)


def attended(slots, place, q, k, v, before, after, arrived):
    rows, features = q.shape
    counts = tuple(a.shape[1] for a in arrived)
    vmem = pl.BlockSpec(memory_space=pltpu.VMEM)
    smem = pl.BlockSpec(memory_space=pltpu.SMEM)
    return pl.pallas_call(
        lambda *refs: attend_kernel(counts, *refs),
        out_shape=(
            jax.ShapeDtypeStruct((rows, features), jnp.float32),
            jax.ShapeDtypeStruct((features // DH, rows, DH), jnp.float32),
        ),
        in_specs=[smem, smem] + [vmem] * 5 + [pl.BlockSpec(memory_space=pl.ANY)] * len(arrived),
        out_specs=(vmem, vmem),
        scratch_shapes=[
            pltpu.VMEM((INPLANE, sum(counts), DH), jnp.bfloat16),
            pltpu.SemaphoreType.DMA((len(arrived),)),
            pltpu.VMEM((rows + 2 * BLOCK, features), jnp.bfloat16),
            pltpu.VMEM((rows + 2 * BLOCK, features), jnp.bfloat16),
        ],
        compiler_params=pltpu.CompilerParams(vmem_limit_bytes=VMEM_LIMIT),
        cost_estimate=pl.CostEstimate(
            flops=4 * rows * features * 512, bytes_accessed=COST, transcendentals=rows * 4 * 512
        ),
        name="attend",
    )(slots, place, q, k, v, before, after, *arrived)


def finish_kernel(late, q, acc, stats, blocks_late, top, low, gout, summed, held):
    scale = DH ** (-0.5)
    lane = lax.broadcasted_iota(jnp.int32, (BLOCK, DH), 1)
    summed[...] = acc[...]
    held[...] = stats[...]

    def one_peer(peer, carry):
        found = []
        for rank in range(CAP):
            code = late[peer * CAP + rank]
            near = jnp.maximum(code, 0)
            at_rows = pl.ds(pl.multiple_of((near & 15) * BLOCK, BLOCK), BLOCK)
            cols = pl.ds(pl.multiple_of((near >> 4) * DH, DH), DH)
            scores = lax.dot_general(
                q[at_rows, cols], blocks_late[peer, 2 * rank * BLOCK : (2 * rank + 1) * BLOCK],
                (((1,), (1,)), ((), ())), preferred_element_type=jnp.float32,
            ) * scale
            found.append((code, near >> 4, at_rows, cols, scores))
        peaks = [jnp.max(own[-1], axis=1, keepdims=True) for own in found]
        weights = [jnp.exp(own[-1] - peak) for own, peak in zip(found, peaks)]
        totals = [jnp.sum(own, axis=1, keepdims=True) for own in weights]
        sums = [
            jnp.dot(
                own.astype(jnp.bfloat16),
                blocks_late[peer, (2 * rank + 1) * BLOCK : (2 * rank + 2) * BLOCK],
                preferred_element_type=jnp.float32,
            )
            for rank, own in enumerate(weights)
        ]
        for (code, h, at_rows, cols, _), peak, total, own in zip(found, peaks, totals, sums):

            @pl.when(code >= 0)
            def _():
                before = held[h, at_rows, 0:1]
                top = jnp.maximum(before, peak)
                less, more = jnp.exp(before - top), jnp.exp(peak - top)
                summed[at_rows, cols] = summed[at_rows, cols] * less + own * more
                both = held[h, at_rows, DH // 2 : DH // 2 + 1] * less + total * more
                held[h, at_rows] = jnp.where(lane < DH // 2, top, both)

        return carry

    lax.fori_loop(0, INPLANE, one_peer, 0)
    merge_rows(blocks_late, 2 * CAP * BLOCK, gout)
    half = top.shape[0]
    for side, out in enumerate((top, low)):

        def one_block(b, carry):
            to_rows = pl.ds(pl.multiple_of(b * BLOCK, BLOCK), BLOCK)
            at_rows = pl.ds(pl.multiple_of(b * BLOCK + side * half, BLOCK), BLOCK)
            for h in range(held.shape[0]):
                hs = slice(h * DH, (h + 1) * DH)
                total = held[h, at_rows, DH // 2 : DH // 2 + 1]
                out[to_rows, hs] = (summed[at_rows, hs] / total).astype(jnp.bfloat16)
            return carry

        lax.fori_loop(0, half // BLOCK, one_block, 0)


def finished(late, q, acc, stats, blocks_late):
    vmem = pl.BlockSpec(memory_space=pltpu.VMEM)
    rows, features = q.shape
    half = jax.ShapeDtypeStruct((rows // 2, features), jnp.bfloat16)
    return pl.pallas_call(
        finish_kernel,
        out_shape=(half, half, jax.ShapeDtypeStruct((INPLANE, BLOCK, DH), jnp.bfloat16)),
        in_specs=[pl.BlockSpec(memory_space=pltpu.SMEM)] + [vmem] * 4,
        out_specs=(vmem, vmem, vmem),
        scratch_shapes=[
            pltpu.VMEM(acc.shape, jnp.float32),
            pltpu.VMEM(stats.shape, jnp.float32),
        ],
        compiler_params=pltpu.CompilerParams(vmem_limit_bytes=32 * 2**20),
        name="late_blocks",
    )(late, q, acc, stats, blocks_late)


def on_device(queries, key_vectors, value_vectors, random_blocks, global_blocks, out_weight):
    shards = lax.axis_size(SEQ)
    my_index = lax.axis_index(SEQ)
    my_plane = lax.axis_index("seq_0")
    rows, features = queries.shape
    heads = features // DH
    blocks = rows // BLOCK
    requests = heads * blocks * RANDOM

    flat = random_blocks.reshape(requests)
    holders = flat // blocks
    number = jnp.arange(requests, dtype=jnp.int32)
    codes = (number // (blocks * RANDOM)) * 16 + flat % blocks
    earlier = (holders[:, None] == holders[None, :]) & (number[None, :] < number[:, None])
    rank = jnp.sum(earlier.astype(jnp.int32), axis=1)
    apart = (holders // INPLANE - my_plane) % PLANES
    order = jnp.where(apart <= PLANES // 2, jnp.minimum(2 * apart, PLANES - 1), 2 * PLANES - 1 - 2 * apart)
    slots = ((holders % INPLANE) * PLANES + order) * CAP + rank
    every = jnp.arange(INPLANE * PLANES * CAP, dtype=jnp.int32)
    asked = jnp.sum(jnp.where(slots[None, :] == every[:, None], codes[None, :], 0), axis=1)
    asker = number // RANDOM
    asker = (asker // blocks) * 16 + asker % blocks + 1
    late = jnp.sum(jnp.where(slots[None, :] == every[:, None], asker[None, :], 0), axis=1) - 1
    late = late.reshape(INPLANE, PLANES, CAP)[:, PLANES - 1].reshape(-1)
    asked = asked.astype(jnp.bfloat16).reshape(INPLANE, 1, PLANES * CAP)
    asked = jnp.pad(asked, ((0, 0), (0, 15), (0, features - PLANES * CAP)))

    holder = global_blocks // blocks
    spot = global_blocks % blocks
    mine = holder == my_index

    def cut(source, g):
        piece = lax.dynamic_slice_in_dim(source, spot[g] * BLOCK, BLOCK, axis=0)
        return jnp.where(mine[g], piece, jnp.zeros_like(piece))

    asking = jnp.concatenate([cut(queries, g) for g in range(GLOBAL)])
    shared = jnp.concatenate(
        [cut(source, g) for g in range(GLOBAL) for source in (key_vectors, value_vectors)]
    ).reshape(INPLANE, -1, features)
    asking = jnp.broadcast_to(asking[None], (INPLANE, *asking.shape))
    found = jnp.concatenate([asking, shared, asked], axis=1)
    up_k, down_v = ring_step(key_vectors, 1), ring_step(value_vectors, -1)
    up_v, down_k = ring_step(value_vectors, 1), ring_step(key_vectors, -1)
    me = lax.axis_index("heads")
    peers = lax.axis_size("heads")
    width = out_weight.shape[1] // peers
    weights = [
        lax.dynamic_slice_in_dim(out_weight, ((me + away) % peers) * width, width, axis=1)
        for away in (0, 1, -1, 2)
    ]
    ends = jnp.concatenate([key_vectors[rows - BLOCK :], value_vectors[rows - BLOCK :]])
    starts = jnp.concatenate([key_vectors[:BLOCK], value_vectors[:BLOCK]])
    found, ends, starts, weights, _, _ = lax.optimization_barrier(
        (found, ends, starts, weights, up_k, down_v)
    )
    found = over_plane(found)
    many = GLOBAL * BLOCK
    asking = found[:, :many].sum(axis=0)
    shared = found[:, many:-16].sum(axis=0)
    asked = found[:, -16, : PLANES * CAP].astype(jnp.int32).reshape(-1)

    asked, _, _ = lax.optimization_barrier((asked, up_v, down_k))
    picks = picked(asked, 0, [key_vectors, value_vectors])
    arrived = [over_plane(picks)]
    ahead = [(i, i + 1) for i in range(shards - 1)]
    back = [(j, i) for i, j in ahead]
    for apart in (1, 2, 4):
        pairs = [(i, i ^ apart) for i in range(PLANES)]
        shared = shared + lax.ppermute(shared, "seq_0", pairs)
    first, parts = 1, ()
    beside = [lax.ppermute(ends, SEQ, ahead), lax.ppermute(starts, SEQ, back)]
    held = [up_k, down_k, up_v, down_v]
    first_pair = (up_v, down_k)
    for step in range(2, PLANES // 2 + 1):
        if step > 2:
            up_k, down_v, _ = lax.optimization_barrier((up_k, down_v, held if step == PLANES // 2 else first_pair))
        up_k = ring_step(up_k, 1)
        down_v = ring_step(down_v, -1)
        if step < PLANES // 2:
            up_v, down_k, _ = lax.optimization_barrier((up_v, down_k, picks))
        gate = (up_k, down_v) if step < PLANES // 2 else ()
        held, _, _, tied, parts, shared = lax.optimization_barrier(
            (held, gate, arrived[-1], beside if step > 2 else (), parts, shared)
        )
        if step > 2:
            weights[turn], before, after = tied
        else:
            before, after = beside
        turn, away = ((3, 2), (1, 1), (2, -1))[step - 2]
        beside, _ = lax.optimization_barrier((weights[turn], held))
        beside = (across(beside, away), before, after)
        picks = picked(asked, first, held, (shared,) if step == PLANES // 2 else ())
        arrived.append(over_plane(picks))
        first += len(held) // 2
        both = held
        if step == 2:
            both = [*held[:2], key_vectors, *held[2:], value_vectors]
        parts = (global_parts(asking, both, parts),)
        if step < PLANES // 2:
            up_v = ring_step(up_v, 1)
            down_k = ring_step(down_k, -1)
            held = [up_k, down_k, up_v, down_v]
        else:
            held = [up_k, down_v]
    held, arrived, parts, beside = lax.optimization_barrier((held, arrived, parts, beside))
    weights[turn], before, after = beside
    parts = (global_parts(asking, held, parts),)
    arrived.append(over_plane(picked(asked, first, held, parts)))
    place = jnp.concatenate(
        [
            jnp.stack([my_index * blocks, jnp.int32(shards * blocks)]).astype(jnp.int32),
            jnp.where(mine, spot, -1).astype(jnp.int32),
        ]
    )
    acc, stats = attended(
        slots, place, queries, key_vectors, value_vectors, before, after, arrived[:-1]
    )
    own_t, own_b, gout = finished(late, queries, acc, stats, arrived[-1])
    right_t, left_t = across(own_t, 1), across(own_t, -1)
    right_b, left_b = across(own_b, 1), across(own_b, -1)
    far_t, far_b = across(right_t, 1), across(left_b, -1)
    gout = over_plane(gout).reshape(heads, GLOBAL * BLOCK, DH)
    gout = gout.transpose(1, 0, 2).reshape(GLOBAL * BLOCK, features)
    rows_g = (gout, across(gout, 1), across(gout, -1), across(gout, 2))
    top = product((own_t, right_t, left_t, far_t), weights)
    return product((own_b, right_b, left_b, far_b), weights, place, top, rows_g)


def solution(mesh):
    torus = Mesh(
        mesh.devices.reshape(mesh.shape["heads"], 8, 4, 2), ("heads", "seq_0", "seq_1", "seq_2")
    )
    in_specs = (
        P(SEQ, "heads"),
        P(SEQ, "heads"),
        P(SEQ, "heads"),
        P("heads", SEQ, None),
        P(),
        P("heads", None),
    )
    out_specs = P(SEQ, "heads")
    return jax.shard_map(
        on_device, mesh=torus, in_specs=in_specs, out_specs=out_specs, check_vma=False
    )
```

```python
import jax
import jax.numpy as jnp
from jax import lax
from jax.experimental import pallas as pl
from jax.experimental.pallas import tpu as pltpu
from jax.sharding import Mesh
from jax.sharding import PartitionSpec as P

DH = 128
BLOCK = 64
RANDOM = 3
GLOBAL = 2
CAP = 4
PLANES = 8
INPLANE = 8
SEQ = ("seq_0", "seq_1", "seq_2")
PLANE = ("seq_1", "seq_2")
VMEM_LIMIT = 56 * 2**20
COST = 24 * 2**20


def ring_step(shard, step):
    peers = lax.axis_size("seq_0")
    return lax.ppermute(shard, "seq_0", [(i, (i + step) % peers) for i in range(peers)])


def across(shard, step):
    peers = lax.axis_size("heads")
    return lax.ppermute(shard, "heads", [(i, (i + step) % peers) for i in range(peers)])


def pick_kernel(n, first, codes, *refs):
    keys, values = refs[:n], refs[n : 2 * n]
    extra, out = refs[2 * n : -1], refs[-1]

    def one_peer(peer, carry):
        for run in range(n):
            for rank in range(CAP):
                code = codes[(peer * PLANES + first + run) * CAP + rank]
                rows = pl.ds(pl.multiple_of((code & 15) * BLOCK, BLOCK), BLOCK)
                cols = pl.ds(pl.multiple_of((code >> 4) * DH, DH), DH)
                at = (run * CAP + rank) * 2 * BLOCK
                out[peer, at : at + BLOCK] = keys[run][rows, cols]
                out[peer, at + BLOCK : at + 2 * BLOCK] = values[run][rows, cols]
        at = n * CAP * 2 * BLOCK
        if extra and extra[0].shape[0] < BLOCK:
            few = extra[0].shape[0]
            for h in range(extra[0].shape[1] // DH):
                out[peer, at + h * few : at + (h + 1) * few] = extra[0][:, h * DH : (h + 1) * DH]
        elif extra:
            own = extra[0][pl.ds(pl.multiple_of(peer * BLOCK, BLOCK), BLOCK)].astype(out.dtype)
            out[peer, at : at + BLOCK] = own[:, :DH]
            out[peer, at + BLOCK : at + 2 * BLOCK] = own[:, DH:]
        return carry

    lax.fori_loop(0, INPLANE, one_peer, 0)


def picked(codes, first, blocks, extra=()):
    n = len(blocks) // 2
    tail = sum(e.size if e.shape[0] < BLOCK else e.size // INPLANE for e in extra) // DH
    shape = (INPLANE, n * CAP * 2 * BLOCK + tail, DH)
    size = 2 * (sum(k.size for k in blocks) + INPLANE * n * CAP * 2 * BLOCK * DH)
    vmem = pl.BlockSpec(memory_space=pltpu.VMEM)
    return pl.pallas_call(
        lambda *refs: pick_kernel(n, first, *refs),
        out_shape=jax.ShapeDtypeStruct(shape, jnp.bfloat16),
        in_specs=[pl.BlockSpec(memory_space=pltpu.SMEM)] + [vmem] * (2 * n + len(extra)),
        out_specs=vmem,
        compiler_params=pltpu.CompilerParams(vmem_limit_bytes=32 * 2**20),
        cost_estimate=pl.CostEstimate(flops=0, bytes_accessed=24 * 2**20, transcendentals=0),
        name="pick_blocks",
    )(codes, *blocks, *extra)


def over_plane(parts):
    return lax.all_to_all(parts, PLANE, split_axis=0, concat_axis=0, tiled=True)


def global_kernel(n, asking, *refs):
    keys, values = refs[:n], refs[n : 2 * n]
    held, out = refs[2 * n : -1], refs[-1]
    heads = asking.shape[1] // DH
    many = GLOBAL * BLOCK
    lane = lax.broadcasted_iota(jnp.int32, (many, DH), 1)
    for h in range(heads):
        hs = slice(h * DH, (h + 1) * DH)
        rows = slice(h * many, (h + 1) * many)
        scores = [
            lax.dot_general(
                asking[:, hs], k[:, hs], (((1,), (1,)), ((), ())),
                preferred_element_type=jnp.float32,
            ) * (DH ** (-0.5))
            for k in keys
        ]
        top = jnp.max(scores[0], axis=1, keepdims=True)
        for other in scores[1:]:
            top = jnp.maximum(top, jnp.max(other, axis=1, keepdims=True))
        top = top.astype(jnp.bfloat16).astype(jnp.float32)
        if held:
            before = held[0][rows, DH : DH + 1]
            top = jnp.maximum(top, before)
            scale = jnp.exp(before - top)
            part = held[0][rows, :DH] * scale
            total = held[0][rows, DH + 1 : DH + 2] * scale
        else:
            part = jnp.zeros((many, DH), jnp.float32)
            total = jnp.zeros((many, 1), jnp.float32)
        for score, v in zip(scores, values):
            weights = jnp.exp(score - top)
            total += jnp.sum(weights, axis=1, keepdims=True)
            part += jnp.dot(
                weights.astype(jnp.bfloat16), v[:, hs], preferred_element_type=jnp.float32
            )
        upper = total.astype(jnp.bfloat16).astype(jnp.float32)
        side = jnp.where(lane == 0, top, jnp.where(lane == 1, total, 0.0))
        side = jnp.where(lane == 2, upper, jnp.where(lane == 3, total - upper, side))
        out[rows] = jnp.concatenate([part, side], axis=1)


def global_parts(asking, blocks, held=()):
    n = len(blocks) // 2
    vmem = pl.BlockSpec(memory_space=pltpu.VMEM)
    rows = asking.shape[0] * asking.shape[1] // DH
    return pl.pallas_call(
        lambda *refs: global_kernel(n, *refs),
        out_shape=jax.ShapeDtypeStruct((rows, 2 * DH), jnp.float32),
        in_specs=[vmem] * (1 + len(blocks) + len(held)),
        out_specs=vmem,
        compiler_params=pltpu.CompilerParams(vmem_limit_bytes=32 * 2**20),
        cost_estimate=pl.CostEstimate(
            flops=4 * rows * DH * 768 * n, bytes_accessed=24 * 2**20, transcendentals=rows * 768 * n
        ),
        name="global_parts",
    )(asking, *blocks, *held)


def merge_kernel(parts, out):
    peers = parts.shape[0]
    sums, side = slice(0, BLOCK), slice(BLOCK, 2 * BLOCK)
    tops = [parts[p, side, 0:1].astype(jnp.float32) for p in range(peers)]
    top = tops[0]
    for other in tops[1:]:
        top = jnp.maximum(top, other)
    part = jnp.zeros((BLOCK, DH), jnp.float32)
    total = jnp.zeros((BLOCK, 1), jnp.float32)
    for p, own in enumerate(tops):
        scale = jnp.exp(own - top)
        part += scale * parts[p, sums].astype(jnp.float32)
        upper = parts[p, side, 2:3].astype(jnp.float32)
        total += scale * (upper + parts[p, side, 3:4].astype(jnp.float32))
    whole = (part / total).astype(jnp.bfloat16)
    for p in range(peers):
        out[p] = whole


def merged(parts):
    peers, rows, _ = parts.shape
    return pl.pallas_call(
        merge_kernel,
        out_shape=jax.ShapeDtypeStruct((peers, BLOCK, DH), jnp.bfloat16),
        grid=(1,),
        in_specs=[pl.BlockSpec((peers, 2 * BLOCK, DH), lambda i: (0, rows // (2 * BLOCK) - 1, 0))],
        out_specs=pl.BlockSpec((peers, BLOCK, DH), lambda i: (0, 0, 0)),
        name="merge_parts",
    )(parts)


def times(pieces, weights):
    total = jnp.dot(pieces[0][...], weights[0][...], preferred_element_type=jnp.float32)
    for piece, weight in zip(pieces[1:], weights[1:]):
        total += jnp.dot(piece[...], weight[...], preferred_element_type=jnp.float32)
    return total.astype(jnp.bfloat16)


def upper_kernel(*refs):
    refs[8][...] = times(refs[:4], refs[4:8])


def lower_kernel(place, top, *refs):
    low, rows, weights, out = refs[:4], refs[4:8], refs[8:12], refs[12]
    half = top.shape[0]
    out[:half] = top[...]
    out[half:] = times(low, weights)
    replaced = times(rows, weights)
    for g in range(GLOBAL):

        @pl.when(place[2 + g] >= 0)
        def _():
            at_rows = pl.ds(pl.multiple_of(place[2 + g] * BLOCK, BLOCK), BLOCK)
            out[at_rows] = replaced[g * BLOCK : (g + 1) * BLOCK]


def product(pieces, weights, place=None, top=None, rows=()):
    features, width = weights[0].shape
    step = width // 4
    whole = [pl.BlockSpec(p.shape, lambda i: (0, 0)) for p in (*pieces, *rows)]
    sliced = [pl.BlockSpec((features, step), lambda i: (0, i))] * 4
    head = [] if top is None else [place, top]
    half = pieces[0].shape[0]
    tall = half if top is None else 2 * half
    specs = [] if top is None else [
        pl.BlockSpec(memory_space=pltpu.SMEM), pl.BlockSpec((half, step), lambda i: (0, i))
    ]
    return pl.pallas_call(
        upper_kernel if top is None else lower_kernel,
        out_shape=jax.ShapeDtypeStruct((tall, width), jnp.bfloat16),
        grid=(4,),
        in_specs=specs + whole + sliced,
        out_specs=pl.BlockSpec((tall, step), lambda i: (0, i)),
        compiler_params=pltpu.CompilerParams(vmem_limit_bytes=32 * 2**20),
        cost_estimate=pl.CostEstimate(
            flops=8 * half * features * width, bytes_accessed=8 * 2**20, transcendentals=0
        ),
        name="upper_product" if top is None else "lower_product",
    )(*head, *pieces, *rows, *weights)


def attend_kernel(counts, slots, place, q, k, v, before, after, *refs):
    n = len(counts)
    arrived, acc, stats, held, sems = refs[:n], refs[n], refs[n + 1], refs[n + 2], refs[n + 3]
    kpad, vpad = refs[n + 4], refs[n + 5]
    copies = []
    at = 0
    for part, count in enumerate(counts):
        copies.append(
            pltpu.make_async_copy(arrived[part], held.at[:, pl.ds(at, count)], sems.at[part])
        )
        copies[-1].start()
        at += count
    rows = q.shape[0]
    heads = q.shape[1] // DH
    blocks = rows // BLOCK
    for side, (pad, own) in enumerate(((kpad, k), (vpad, v))):
        pad[0:BLOCK] = before[side * BLOCK : (side + 1) * BLOCK]
        pad[BLOCK : BLOCK + rows] = own[...]
        pad[BLOCK + rows :] = after[side * BLOCK : (side + 1) * BLOCK]
    for copy in copies:
        copy.wait()
    scale = DH ** (-0.5)
    col = lax.broadcasted_iota(jnp.int32, (1, (3 + RANDOM + GLOBAL) * BLOCK), 1) // BLOCK
    lane = lax.broadcasted_iota(jnp.int32, (BLOCK, DH), 1)
    few = GLOBAL * 2 * BLOCK // INPLANE

    def one_block(b, carry):
        at_rows = pl.ds(pl.multiple_of(b * BLOCK, BLOCK), BLOCK)
        win_rows = pl.ds(pl.multiple_of(b * BLOCK, BLOCK), 3 * BLOCK)
        number = place[0] + b
        outside = jnp.where(number == 0, 0, -1), jnp.where(number == place[1] - 1, 2, -1)
        for pair in range(0, heads, 2):
            both = range(pair, pair + 2)
            found, scores = [], []
            for h in both:
                hs = slice(h * DH, (h + 1) * DH)
                picks = []
                bias = jnp.where((col == outside[0]) | (col == outside[1]), -jnp.inf, 0.0)
                for r in range(RANDOM):
                    slot = slots[(h * blocks + b) * RANDOM + r]
                    late = ((slot >> 2) & 7) == PLANES - 1
                    bias = jnp.where(col == jnp.where(late, 3 + r, -1), -jnp.inf, bias)
                    slot = jnp.where(late, 0, slot)
                    picks.append((slot >> 5, pl.multiple_of((slot & 31) * 2 * BLOCK, 2 * BLOCK)))
                found.append(picks)
                at = sum(counts) + (h - heads) * few
                keys = jnp.concatenate(
                    [kpad[win_rows, hs]]
                    + [held[p[0], pl.ds(p[1], BLOCK)] for p in picks]
                    + [held[4 * g + i, at : at + few] for g in range(GLOBAL) for i in range(2)],
                    axis=0,
                )
                scores.append(
                    lax.dot_general(
                        q[at_rows, hs], keys, (((1,), (1,)), ((), ())),
                        preferred_element_type=jnp.float32,
                    ) * scale + bias
                )
            peaks = [jnp.max(own, axis=1, keepdims=True) for own in scores]
            weights = [jnp.exp(own - peak) for own, peak in zip(scores, peaks)]
            totals = [jnp.sum(own, axis=1, keepdims=True) for own in weights]
            sums = []
            for h, picks, own in zip(both, found, weights):
                hs = slice(h * DH, (h + 1) * DH)
                at = sum(counts) + (h - heads) * few
                values = jnp.concatenate(
                    [vpad[win_rows, hs]]
                    + [held[p[0], pl.ds(p[1] + BLOCK, BLOCK)] for p in picks]
                    + [held[4 * g + 2 + i, at : at + few] for g in range(GLOBAL) for i in range(2)],
                    axis=0,
                )
                sums.append(
                    jnp.dot(own.astype(jnp.bfloat16), values, preferred_element_type=jnp.float32)
                )
            for h, own, peak, total in zip(both, sums, peaks, totals):
                acc[at_rows, h * DH : (h + 1) * DH] = own
                stats[h, at_rows] = jnp.where(lane < DH // 2, peak, total)
        return carry

    lax.fori_loop(0, blocks, one_block, 0)


def attended(slots, place, q, k, v, before, after, arrived):
    rows, features = q.shape
    counts = tuple(a.shape[1] for a in arrived)
    vmem = pl.BlockSpec(memory_space=pltpu.VMEM)
    smem = pl.BlockSpec(memory_space=pltpu.SMEM)
    return pl.pallas_call(
        lambda *refs: attend_kernel(counts, *refs),
        out_shape=(
            jax.ShapeDtypeStruct((rows, features), jnp.float32),
            jax.ShapeDtypeStruct((features // DH, rows, DH), jnp.float32),
        ),
        in_specs=[smem, smem] + [vmem] * 5 + [pl.BlockSpec(memory_space=pl.ANY)] * len(arrived),
        out_specs=(vmem, vmem),
        scratch_shapes=[
            pltpu.VMEM((INPLANE, sum(counts), DH), jnp.bfloat16),
            pltpu.SemaphoreType.DMA((len(arrived),)),
            pltpu.VMEM((rows + 2 * BLOCK, features), jnp.bfloat16),
            pltpu.VMEM((rows + 2 * BLOCK, features), jnp.bfloat16),
        ],
        compiler_params=pltpu.CompilerParams(vmem_limit_bytes=VMEM_LIMIT),
        cost_estimate=pl.CostEstimate(
            flops=4 * rows * features * 512, bytes_accessed=COST, transcendentals=rows * 4 * 512
        ),
        name="attend",
    )(slots, place, q, k, v, before, after, *arrived)


def finish_kernel(late, q, acc, stats, blocks_late, top, low, summed, held):
    scale = DH ** (-0.5)
    lane = lax.broadcasted_iota(jnp.int32, (BLOCK, DH), 1)
    summed[...] = acc[...]
    held[...] = stats[...]

    def one_peer(peer, carry):
        found = []
        for rank in range(CAP):
            code = late[peer * CAP + rank]
            near = jnp.maximum(code, 0)
            at_rows = pl.ds(pl.multiple_of((near & 15) * BLOCK, BLOCK), BLOCK)
            cols = pl.ds(pl.multiple_of((near >> 4) * DH, DH), DH)
            scores = lax.dot_general(
                q[at_rows, cols], blocks_late[peer, 2 * rank * BLOCK : (2 * rank + 1) * BLOCK],
                (((1,), (1,)), ((), ())), preferred_element_type=jnp.float32,
            ) * scale
            found.append((code, near >> 4, at_rows, cols, scores))
        peaks = [jnp.max(own[-1], axis=1, keepdims=True) for own in found]
        weights = [jnp.exp(own[-1] - peak) for own, peak in zip(found, peaks)]
        totals = [jnp.sum(own, axis=1, keepdims=True) for own in weights]
        sums = [
            jnp.dot(
                own.astype(jnp.bfloat16),
                blocks_late[peer, (2 * rank + 1) * BLOCK : (2 * rank + 2) * BLOCK],
                preferred_element_type=jnp.float32,
            )
            for rank, own in enumerate(weights)
        ]
        for (code, h, at_rows, cols, _), peak, total, own in zip(found, peaks, totals, sums):

            @pl.when(code >= 0)
            def _():
                before = held[h, at_rows, 0:1]
                top = jnp.maximum(before, peak)
                less, more = jnp.exp(before - top), jnp.exp(peak - top)
                summed[at_rows, cols] = summed[at_rows, cols] * less + own * more
                both = held[h, at_rows, DH // 2 : DH // 2 + 1] * less + total * more
                held[h, at_rows] = jnp.where(lane < DH // 2, top, both)

        return carry

    lax.fori_loop(0, INPLANE, one_peer, 0)
    half = top.shape[0]
    for side, out in enumerate((top, low)):

        def one_block(b, carry):
            to_rows = pl.ds(pl.multiple_of(b * BLOCK, BLOCK), BLOCK)
            at_rows = pl.ds(pl.multiple_of(b * BLOCK + side * half, BLOCK), BLOCK)
            for h in range(held.shape[0]):
                hs = slice(h * DH, (h + 1) * DH)
                total = held[h, at_rows, DH // 2 : DH // 2 + 1]
                out[to_rows, hs] = (summed[at_rows, hs] / total).astype(jnp.bfloat16)
            return carry

        lax.fori_loop(0, half // BLOCK, one_block, 0)


def finished(late, q, acc, stats, blocks_late):
    vmem = pl.BlockSpec(memory_space=pltpu.VMEM)
    rows, features = q.shape
    half = jax.ShapeDtypeStruct((rows // 2, features), jnp.bfloat16)
    return pl.pallas_call(
        finish_kernel,
        out_shape=(half, half),
        in_specs=[pl.BlockSpec(memory_space=pltpu.SMEM)] + [vmem] * 4,
        out_specs=(vmem, vmem),
        scratch_shapes=[
            pltpu.VMEM(acc.shape, jnp.float32),
            pltpu.VMEM(stats.shape, jnp.float32),
        ],
        compiler_params=pltpu.CompilerParams(vmem_limit_bytes=32 * 2**20),
        cost_estimate=pl.CostEstimate(flops=0, bytes_accessed=COST, transcendentals=0),
        name="late_blocks",
    )(late, q, acc, stats, blocks_late)


def on_device(queries, key_vectors, value_vectors, random_blocks, global_blocks, out_weight):
    shards = lax.axis_size(SEQ)
    my_index = lax.axis_index(SEQ)
    my_plane = lax.axis_index("seq_0")
    rows, features = queries.shape
    heads = features // DH
    blocks = rows // BLOCK
    requests = heads * blocks * RANDOM

    flat = random_blocks.reshape(requests)
    holders = flat // blocks
    number = jnp.arange(requests, dtype=jnp.int32)
    codes = (number // (blocks * RANDOM)) * 16 + flat % blocks
    earlier = (holders[:, None] == holders[None, :]) & (number[None, :] < number[:, None])
    rank = jnp.sum(earlier.astype(jnp.int32), axis=1)
    apart = (holders // INPLANE - my_plane) % PLANES
    order = jnp.where(apart <= PLANES // 2, jnp.minimum(2 * apart, PLANES - 1), 2 * PLANES - 1 - 2 * apart)
    slots = ((holders % INPLANE) * PLANES + order) * CAP + rank
    every = jnp.arange(INPLANE * PLANES * CAP, dtype=jnp.int32)
    asked = jnp.sum(jnp.where(slots[None, :] == every[:, None], codes[None, :], 0), axis=1)
    asker = number // RANDOM
    asker = (asker // blocks) * 16 + asker % blocks + 1
    late = jnp.sum(jnp.where(slots[None, :] == every[:, None], asker[None, :], 0), axis=1) - 1
    late = late.reshape(INPLANE, PLANES, CAP)[:, PLANES - 1].reshape(-1)
    asked = asked.astype(jnp.bfloat16).reshape(INPLANE, 1, PLANES * CAP)
    asked = jnp.pad(asked, ((0, 0), (0, 15), (0, features - PLANES * CAP)))

    holder = global_blocks // blocks
    spot = global_blocks % blocks
    mine = holder == my_index

    def cut(source, g):
        piece = lax.dynamic_slice_in_dim(source, spot[g] * BLOCK, BLOCK, axis=0)
        return jnp.where(mine[g], piece, jnp.zeros_like(piece))

    asking = jnp.concatenate([cut(queries, g) for g in range(GLOBAL)])
    shared = jnp.concatenate(
        [cut(source, g) for g in range(GLOBAL) for source in (key_vectors, value_vectors)]
    ).reshape(INPLANE, -1, features)
    asking = jnp.broadcast_to(asking[None], (INPLANE, *asking.shape))
    found = jnp.concatenate([asking, shared, asked], axis=1)
    up_k, down_v = ring_step(key_vectors, 1), ring_step(value_vectors, -1)
    up_v, down_k = ring_step(value_vectors, 1), ring_step(key_vectors, -1)
    me = lax.axis_index("heads")
    peers = lax.axis_size("heads")
    width = out_weight.shape[1] // peers
    weights = [
        lax.dynamic_slice_in_dim(out_weight, ((me + away) % peers) * width, width, axis=1)
        for away in (0, 1, -1, 2)
    ]
    ends = jnp.concatenate([key_vectors[rows - BLOCK :], value_vectors[rows - BLOCK :]])
    starts = jnp.concatenate([key_vectors[:BLOCK], value_vectors[:BLOCK]])
    found, ends, starts, weights, _, _ = lax.optimization_barrier(
        (found, ends, starts, weights, up_k, down_v)
    )
    found = over_plane(found)
    many = GLOBAL * BLOCK
    asking = found[:, :many].sum(axis=0)
    shared = found[:, many:-16].sum(axis=0)
    asked = found[:, -16, : PLANES * CAP].astype(jnp.int32).reshape(-1)

    firsts, seconds = [(up_k, down_v)], [(up_v, down_k)]
    for step in range(2, PLANES // 2 + 1):
        up, down = firsts[-1]
        if step == 3:
            up, down, _ = lax.optimization_barrier((up, down, seconds[0]))
        firsts.append((ring_step(up, 1), ring_step(down, -1)))
        if step < PLANES // 2:
            up, down = seconds[-1]
            seconds.append((ring_step(up, 1), ring_step(down, -1)))
    ahead = [(i, i + 1) for i in range(shards - 1)]
    back = [(j, i) for i, j in ahead]
    before, after = lax.ppermute(ends, SEQ, ahead), lax.ppermute(starts, SEQ, back)

    def doubled(own, apart, when):
        own, _ = lax.optimization_barrier((own, when))
        return own + lax.ppermute(own, "seq_0", [(i, i ^ apart) for i in range(PLANES)])

    def spread(turn, away, when):
        piece, _ = lax.optimization_barrier((weights[turn], when))
        return across(piece, away)

    asked, before, after, _ = lax.optimization_barrier((asked, before, after, firsts[1]))
    picks = picked(asked, 0, [key_vectors, value_vectors])
    arrived = [over_plane(picks)]
    shared = doubled(shared, 1, seconds[0])
    weights[3] = spread(3, 2, seconds[0])
    first, parts = 1, ()
    for step in range(1, PLANES // 2):
        (up_k, down_v), (up_v, down_k) = firsts[step - 1], seconds[step - 1]
        held = [up_k, down_k, up_v, down_v]
        held, _, _, parts, shared = lax.optimization_barrier(
            (held, firsts[min(step + 1, PLANES // 2 - 1)], picks, parts, shared)
        )
        if step == 2:
            weights[3], held = lax.optimization_barrier((weights[3], held))
            weights[1] = spread(1, 1, firsts[2])
        elif step == 3:
            weights[1], held = lax.optimization_barrier((weights[1], held))
            weights[2] = spread(2, -1, seconds[1])
        picks = picked(asked, first, held, (shared,) if step == 3 else ())
        arrived.append(over_plane(picks))
        first += len(held) // 2
        if step == 1:
            held = [*held[:2], key_vectors, *held[2:], value_vectors]
        parts = (global_parts(asking, held, parts),)
        if step < 3:
            shared = doubled(shared, 2 * step, firsts[step])
    held, arrived, parts, weights[2] = lax.optimization_barrier(
        (list(firsts[-1]), arrived, parts, weights[2])
    )
    parts = (global_parts(asking, held, parts),)
    arrived.append(over_plane(picked(asked, first, held, parts)))

    place = jnp.concatenate(
        [
            jnp.stack([my_index * blocks, jnp.int32(shards * blocks)]).astype(jnp.int32),
            jnp.where(mine, spot, -1).astype(jnp.int32),
        ]
    )
    acc, stats = attended(
        slots, place, queries, key_vectors, value_vectors, before, after, arrived[:-1]
    )
    arrived[-1], acc = lax.optimization_barrier((arrived[-1], acc))
    rows_here = merged(arrived[-1])
    gout = over_plane(rows_here)
    arrived[-1], _ = lax.optimization_barrier((arrived[-1], rows_here))
    own_t, own_b = finished(late, queries, acc, stats, arrived[-1])
    own_t, own_b, gout = lax.optimization_barrier((own_t, own_b, gout))
    right_t, left_t = across(own_t, 1), across(own_t, -1)
    right_b, left_b = across(own_b, 1), across(own_b, -1)
    far_t, far_b = across(right_t, 1), across(left_b, -1)
    gout = gout.reshape(heads, -1, DH).transpose(1, 0, 2).reshape(-1, features)
    rows_g = (gout, across(gout, 1), across(gout, -1), across(gout, 2))
    top = product((own_t, right_t, left_t, far_t), weights)
    return product((own_b, right_b, left_b, far_b), weights, place, top, rows_g)


def solution(mesh):
    torus = Mesh(
        mesh.devices.reshape(mesh.shape["heads"], 8, 4, 2), ("heads", "seq_0", "seq_1", "seq_2")
    )
    in_specs = (
        P(SEQ, "heads"),
        P(SEQ, "heads"),
        P(SEQ, "heads"),
        P("heads", SEQ, None),
        P(),
        P("heads", None),
    )
    out_specs = P(SEQ, "heads")
    return jax.shard_map(
        on_device, mesh=torus, in_specs=in_specs, out_specs=out_specs, check_vma=False
    )
```

```python
import jax
import jax.numpy as jnp
from jax import lax
from jax.experimental import pallas as pl
from jax.experimental.pallas import tpu as pltpu
from jax.sharding import Mesh
from jax.sharding import PartitionSpec as P

DH = 128
BLOCK = 64
RANDOM = 3
GLOBAL = 2
CAP = 4
PLANES = 8
INPLANE = 8
SEQ = ("seq_0", "seq_1", "seq_2")
PLANE = ("seq_1", "seq_2")
VMEM_LIMIT = 56 * 2**20
COST = 24 * 2**20


def ring_step(shard, step):
    peers = lax.axis_size("seq_0")
    return lax.ppermute(shard, "seq_0", [(i, (i + step) % peers) for i in range(peers)])


def across(shard, step):
    peers = lax.axis_size("heads")
    return lax.ppermute(shard, "heads", [(i, (i + step) % peers) for i in range(peers)])


def pick_kernel(n, first, codes, *refs):
    keys, values = refs[:n], refs[n : 2 * n]
    extra, out = refs[2 * n : -1], refs[-1]

    def one_peer(peer, carry):
        for run in range(n):
            for rank in range(CAP):
                code = codes[(peer * PLANES + first + run) * CAP + rank]
                rows = pl.ds(pl.multiple_of((code & 15) * BLOCK, BLOCK), BLOCK)
                cols = pl.ds(pl.multiple_of((code >> 4) * DH, DH), DH)
                at = (run * CAP + rank) * 2 * BLOCK
                out[peer, at : at + BLOCK] = keys[run][rows, cols]
                out[peer, at + BLOCK : at + 2 * BLOCK] = values[run][rows, cols]
        at = n * CAP * 2 * BLOCK
        if extra and extra[0].shape[0] < BLOCK:
            few = extra[0].shape[0]
            for h in range(extra[0].shape[1] // DH):
                out[peer, at + h * few : at + (h + 1) * few] = extra[0][:, h * DH : (h + 1) * DH]
        elif extra:
            own = extra[0][pl.ds(pl.multiple_of(peer * BLOCK, BLOCK), BLOCK)].astype(out.dtype)
            out[peer, at : at + BLOCK] = own[:, :DH]
            out[peer, at + BLOCK : at + 2 * BLOCK] = own[:, DH:]
        return carry

    lax.fori_loop(0, INPLANE, one_peer, 0)


def picked(codes, first, blocks, extra=()):
    n = len(blocks) // 2
    tail = sum(e.size if e.shape[0] < BLOCK else e.size // INPLANE for e in extra) // DH
    shape = (INPLANE, n * CAP * 2 * BLOCK + tail, DH)
    size = 2 * (sum(k.size for k in blocks) + INPLANE * n * CAP * 2 * BLOCK * DH)
    vmem = pl.BlockSpec(memory_space=pltpu.VMEM)
    return pl.pallas_call(
        lambda *refs: pick_kernel(n, first, *refs),
        out_shape=jax.ShapeDtypeStruct(shape, jnp.bfloat16),
        in_specs=[pl.BlockSpec(memory_space=pltpu.SMEM)] + [vmem] * (2 * n + len(extra)),
        out_specs=vmem,
        compiler_params=pltpu.CompilerParams(vmem_limit_bytes=32 * 2**20),
        cost_estimate=pl.CostEstimate(flops=0, bytes_accessed=24 * 2**20, transcendentals=0),
        name="pick_blocks",
    )(codes, *blocks, *extra)


def over_plane(parts):
    return lax.all_to_all(parts, PLANE, split_axis=0, concat_axis=0, tiled=True)


def global_kernel(n, asking, *refs):
    keys, values = refs[:n], refs[n : 2 * n]
    held, out = refs[2 * n : -1], refs[-1]
    heads = asking.shape[1] // DH
    many = GLOBAL * BLOCK
    lane = lax.broadcasted_iota(jnp.int32, (many, DH), 1)
    for h in range(heads):
        hs = slice(h * DH, (h + 1) * DH)
        rows = slice(h * many, (h + 1) * many)
        scores = [
            lax.dot_general(
                asking[:, hs], k[:, hs], (((1,), (1,)), ((), ())),
                preferred_element_type=jnp.float32,
            ) * (DH ** (-0.5))
            for k in keys
        ]
        top = jnp.max(scores[0], axis=1, keepdims=True)
        for other in scores[1:]:
            top = jnp.maximum(top, jnp.max(other, axis=1, keepdims=True))
        top = top.astype(jnp.bfloat16).astype(jnp.float32)
        if held:
            before = held[0][rows, DH : DH + 1]
            top = jnp.maximum(top, before)
            scale = jnp.exp(before - top)
            part = held[0][rows, :DH] * scale
            total = held[0][rows, DH + 1 : DH + 2] * scale
        else:
            part = jnp.zeros((many, DH), jnp.float32)
            total = jnp.zeros((many, 1), jnp.float32)
        for score, v in zip(scores, values):
            weights = jnp.exp(score - top)
            total += jnp.sum(weights, axis=1, keepdims=True)
            part += jnp.dot(
                weights.astype(jnp.bfloat16), v[:, hs], preferred_element_type=jnp.float32
            )
        upper = total.astype(jnp.bfloat16).astype(jnp.float32)
        side = jnp.where(lane == 0, top, jnp.where(lane == 1, total, 0.0))
        side = jnp.where(lane == 2, upper, jnp.where(lane == 3, total - upper, side))
        out[rows] = jnp.concatenate([part, side], axis=1)


def global_parts(asking, blocks, held=()):
    n = len(blocks) // 2
    vmem = pl.BlockSpec(memory_space=pltpu.VMEM)
    rows = asking.shape[0] * asking.shape[1] // DH
    return pl.pallas_call(
        lambda *refs: global_kernel(n, *refs),
        out_shape=jax.ShapeDtypeStruct((rows, 2 * DH), jnp.float32),
        in_specs=[vmem] * (1 + len(blocks) + len(held)),
        out_specs=vmem,
        compiler_params=pltpu.CompilerParams(vmem_limit_bytes=32 * 2**20),
        cost_estimate=pl.CostEstimate(
            flops=4 * rows * DH * 768 * n, bytes_accessed=24 * 2**20, transcendentals=rows * 768 * n
        ),
        name="global_parts",
    )(asking, *blocks, *held)


def merge_rows(parts, first, out):
    peers = parts.shape[0]
    sums, side = slice(first, first + BLOCK), slice(first + BLOCK, first + 2 * BLOCK)
    tops = [parts[p, side, 0:1].astype(jnp.float32) for p in range(peers)]
    top = tops[0]
    for other in tops[1:]:
        top = jnp.maximum(top, other)
    part = jnp.zeros((BLOCK, DH), jnp.float32)
    total = jnp.zeros((BLOCK, 1), jnp.float32)
    for p, own in enumerate(tops):
        scale = jnp.exp(own - top)
        part += scale * parts[p, sums].astype(jnp.float32)
        upper = parts[p, side, 2:3].astype(jnp.float32)
        total += scale * (upper + parts[p, side, 3:4].astype(jnp.float32))
    whole = (part / total).astype(jnp.bfloat16)
    for p in range(peers):
        out[p] = whole


def times(pieces, weights):
    total = jnp.dot(pieces[0][...], weights[0][...], preferred_element_type=jnp.float32)
    for piece, weight in zip(pieces[1:], weights[1:]):
        total += jnp.dot(piece[...], weight[...], preferred_element_type=jnp.float32)
    return total.astype(jnp.bfloat16)


def upper_kernel(*refs):
    refs[8][...] = times(refs[:4], refs[4:8])


def lower_kernel(place, top, *refs):
    low, rows, weights, out = refs[:4], refs[4:8], refs[8:12], refs[12]
    half = top.shape[0]
    out[:half] = top[...]
    out[half:] = times(low, weights)
    replaced = times(rows, weights)
    for g in range(GLOBAL):

        @pl.when(place[2 + g] >= 0)
        def _():
            at_rows = pl.ds(pl.multiple_of(place[2 + g] * BLOCK, BLOCK), BLOCK)
            out[at_rows] = replaced[g * BLOCK : (g + 1) * BLOCK]


def product(pieces, weights, place=None, top=None, rows=()):
    features, width = weights[0].shape
    step = width // 4
    whole = [pl.BlockSpec(p.shape, lambda i: (0, 0)) for p in (*pieces, *rows)]
    sliced = [pl.BlockSpec((features, step), lambda i: (0, i))] * 4
    head = [] if top is None else [place, top]
    half = pieces[0].shape[0]
    tall = half if top is None else 2 * half
    specs = [] if top is None else [
        pl.BlockSpec(memory_space=pltpu.SMEM), pl.BlockSpec((half, step), lambda i: (0, i))
    ]
    return pl.pallas_call(
        upper_kernel if top is None else lower_kernel,
        out_shape=jax.ShapeDtypeStruct((tall, width), jnp.bfloat16),
        grid=(4,),
        in_specs=specs + whole + sliced,
        out_specs=pl.BlockSpec((tall, step), lambda i: (0, i)),
        compiler_params=pltpu.CompilerParams(vmem_limit_bytes=32 * 2**20),
        cost_estimate=pl.CostEstimate(
            flops=8 * half * features * width, bytes_accessed=8 * 2**20, transcendentals=0
        ),
        name="upper_product" if top is None else "lower_product",
    )(*head, *pieces, *rows, *weights)


def attend_kernel(counts, slots, place, q, k, v, before, after, *refs):
    n = len(counts)
    arrived, acc, stats, held, sems = refs[:n], refs[n], refs[n + 1], refs[n + 2], refs[n + 3]
    kpad, vpad = refs[n + 4], refs[n + 5]
    copies = []
    at = 0
    for part, count in enumerate(counts):
        copies.append(
            pltpu.make_async_copy(arrived[part], held.at[:, pl.ds(at, count)], sems.at[part])
        )
        copies[-1].start()
        at += count
    rows = q.shape[0]
    heads = q.shape[1] // DH
    blocks = rows // BLOCK
    for side, (pad, own) in enumerate(((kpad, k), (vpad, v))):
        pad[0:BLOCK] = before[side * BLOCK : (side + 1) * BLOCK]
        pad[BLOCK : BLOCK + rows] = own[...]
        pad[BLOCK + rows :] = after[side * BLOCK : (side + 1) * BLOCK]
    for copy in copies:
        copy.wait()
    scale = DH ** (-0.5)
    col = lax.broadcasted_iota(jnp.int32, (1, (3 + RANDOM + GLOBAL) * BLOCK), 1) // BLOCK
    lane = lax.broadcasted_iota(jnp.int32, (BLOCK, DH), 1)
    few = GLOBAL * 2 * BLOCK // INPLANE

    def one_block(b, carry):
        at_rows = pl.ds(pl.multiple_of(b * BLOCK, BLOCK), BLOCK)
        win_rows = pl.ds(pl.multiple_of(b * BLOCK, BLOCK), 3 * BLOCK)
        number = place[0] + b
        outside = jnp.where(number == 0, 0, -1), jnp.where(number == place[1] - 1, 2, -1)
        for pair in range(0, heads, 2):
            both = range(pair, pair + 2)
            found, scores = [], []
            for h in both:
                hs = slice(h * DH, (h + 1) * DH)
                picks = []
                bias = jnp.where((col == outside[0]) | (col == outside[1]), -jnp.inf, 0.0)
                for r in range(RANDOM):
                    slot = slots[(h * blocks + b) * RANDOM + r]
                    late = ((slot >> 2) & 7) == PLANES - 1
                    bias = jnp.where(col == jnp.where(late, 3 + r, -1), -jnp.inf, bias)
                    slot = jnp.where(late, 0, slot)
                    picks.append((slot >> 5, pl.multiple_of((slot & 31) * 2 * BLOCK, 2 * BLOCK)))
                found.append(picks)
                at = sum(counts) + (h - heads) * few
                keys = jnp.concatenate(
                    [kpad[win_rows, hs]]
                    + [held[p[0], pl.ds(p[1], BLOCK)] for p in picks]
                    + [held[4 * g + i, at : at + few] for g in range(GLOBAL) for i in range(2)],
                    axis=0,
                )
                scores.append(
                    lax.dot_general(
                        q[at_rows, hs], keys, (((1,), (1,)), ((), ())),
                        preferred_element_type=jnp.float32,
                    ) * scale + bias
                )
            peaks = [jnp.max(own, axis=1, keepdims=True) for own in scores]
            weights = [jnp.exp(own - peak) for own, peak in zip(scores, peaks)]
            totals = [jnp.sum(own, axis=1, keepdims=True) for own in weights]
            sums = []
            for h, picks, own in zip(both, found, weights):
                hs = slice(h * DH, (h + 1) * DH)
                at = sum(counts) + (h - heads) * few
                values = jnp.concatenate(
                    [vpad[win_rows, hs]]
                    + [held[p[0], pl.ds(p[1] + BLOCK, BLOCK)] for p in picks]
                    + [held[4 * g + 2 + i, at : at + few] for g in range(GLOBAL) for i in range(2)],
                    axis=0,
                )
                sums.append(
                    jnp.dot(own.astype(jnp.bfloat16), values, preferred_element_type=jnp.float32)
                )
            for h, own, peak, total in zip(both, sums, peaks, totals):
                acc[at_rows, h * DH : (h + 1) * DH] = own
                stats[h, at_rows] = jnp.where(lane < DH // 2, peak, total)
        return carry

    lax.fori_loop(0, blocks, one_block, 0)


def attended(slots, place, q, k, v, before, after, arrived):
    rows, features = q.shape
    counts = tuple(a.shape[1] for a in arrived)
    vmem = pl.BlockSpec(memory_space=pltpu.VMEM)
    smem = pl.BlockSpec(memory_space=pltpu.SMEM)
    return pl.pallas_call(
        lambda *refs: attend_kernel(counts, *refs),
        out_shape=(
            jax.ShapeDtypeStruct((rows, features), jnp.float32),
            jax.ShapeDtypeStruct((features // DH, rows, DH), jnp.float32),
        ),
        in_specs=[smem, smem] + [vmem] * 5 + [pl.BlockSpec(memory_space=pl.ANY)] * len(arrived),
        out_specs=(vmem, vmem),
        scratch_shapes=[
            pltpu.VMEM((INPLANE, sum(counts), DH), jnp.bfloat16),
            pltpu.SemaphoreType.DMA((len(arrived),)),
            pltpu.VMEM((rows + 2 * BLOCK, features), jnp.bfloat16),
            pltpu.VMEM((rows + 2 * BLOCK, features), jnp.bfloat16),
        ],
        compiler_params=pltpu.CompilerParams(vmem_limit_bytes=VMEM_LIMIT),
        cost_estimate=pl.CostEstimate(
            flops=4 * rows * features * 512, bytes_accessed=COST, transcendentals=rows * 4 * 512
        ),
        name="attend",
    )(slots, place, q, k, v, before, after, *arrived)


def finish_kernel(late, q, acc, stats, blocks_late, top, low, gout, summed, held):
    scale = DH ** (-0.5)
    lane = lax.broadcasted_iota(jnp.int32, (BLOCK, DH), 1)
    summed[...] = acc[...]
    held[...] = stats[...]

    def one_peer(peer, carry):
        found = []
        for rank in range(CAP):
            code = late[peer * CAP + rank]
            near = jnp.maximum(code, 0)
            at_rows = pl.ds(pl.multiple_of((near & 15) * BLOCK, BLOCK), BLOCK)
            cols = pl.ds(pl.multiple_of((near >> 4) * DH, DH), DH)
            scores = lax.dot_general(
                q[at_rows, cols], blocks_late[peer, 2 * rank * BLOCK : (2 * rank + 1) * BLOCK],
                (((1,), (1,)), ((), ())), preferred_element_type=jnp.float32,
            ) * scale
            found.append((code, near >> 4, at_rows, cols, scores))
        peaks = [jnp.max(own[-1], axis=1, keepdims=True) for own in found]
        weights = [jnp.exp(own[-1] - peak) for own, peak in zip(found, peaks)]
        totals = [jnp.sum(own, axis=1, keepdims=True) for own in weights]
        sums = [
            jnp.dot(
                own.astype(jnp.bfloat16),
                blocks_late[peer, (2 * rank + 1) * BLOCK : (2 * rank + 2) * BLOCK],
                preferred_element_type=jnp.float32,
            )
            for rank, own in enumerate(weights)
        ]
        for (code, h, at_rows, cols, _), peak, total, own in zip(found, peaks, totals, sums):

            @pl.when(code >= 0)
            def _():
                before = held[h, at_rows, 0:1]
                top = jnp.maximum(before, peak)
                less, more = jnp.exp(before - top), jnp.exp(peak - top)
                summed[at_rows, cols] = summed[at_rows, cols] * less + own * more
                both = held[h, at_rows, DH // 2 : DH // 2 + 1] * less + total * more
                held[h, at_rows] = jnp.where(lane < DH // 2, top, both)

        return carry

    lax.fori_loop(0, INPLANE, one_peer, 0)
    merge_rows(blocks_late, 2 * CAP * BLOCK, gout)
    half = top.shape[0]
    for side, out in enumerate((top, low)):

        def one_block(b, carry):
            to_rows = pl.ds(pl.multiple_of(b * BLOCK, BLOCK), BLOCK)
            at_rows = pl.ds(pl.multiple_of(b * BLOCK + side * half, BLOCK), BLOCK)
            for h in range(held.shape[0]):
                hs = slice(h * DH, (h + 1) * DH)
                total = held[h, at_rows, DH // 2 : DH // 2 + 1]
                out[to_rows, hs] = (summed[at_rows, hs] / total).astype(jnp.bfloat16)
            return carry

        lax.fori_loop(0, half // BLOCK, one_block, 0)


def finished(late, q, acc, stats, blocks_late):
    vmem = pl.BlockSpec(memory_space=pltpu.VMEM)
    rows, features = q.shape
    half = jax.ShapeDtypeStruct((rows // 2, features), jnp.bfloat16)
    return pl.pallas_call(
        finish_kernel,
        out_shape=(half, half, jax.ShapeDtypeStruct((INPLANE, BLOCK, DH), jnp.bfloat16)),
        in_specs=[pl.BlockSpec(memory_space=pltpu.SMEM)] + [vmem] * 4,
        out_specs=(vmem, vmem, vmem),
        scratch_shapes=[
            pltpu.VMEM(acc.shape, jnp.float32),
            pltpu.VMEM(stats.shape, jnp.float32),
        ],
        compiler_params=pltpu.CompilerParams(vmem_limit_bytes=32 * 2**20),
        name="late_blocks",
    )(late, q, acc, stats, blocks_late)


def on_device(queries, key_vectors, value_vectors, random_blocks, global_blocks, out_weight):
    shards = lax.axis_size(SEQ)
    my_index = lax.axis_index(SEQ)
    my_plane = lax.axis_index("seq_0")
    rows, features = queries.shape
    heads = features // DH
    blocks = rows // BLOCK
    requests = heads * blocks * RANDOM

    flat = random_blocks.reshape(requests)
    holders = flat // blocks
    number = jnp.arange(requests, dtype=jnp.int32)
    codes = (number // (blocks * RANDOM)) * 16 + flat % blocks
    earlier = (holders[:, None] == holders[None, :]) & (number[None, :] < number[:, None])
    rank = jnp.sum(earlier.astype(jnp.int32), axis=1)
    apart = (holders // INPLANE - my_plane) % PLANES
    order = jnp.where(apart <= PLANES // 2, jnp.minimum(2 * apart, PLANES - 1), 2 * PLANES - 1 - 2 * apart)
    slots = ((holders % INPLANE) * PLANES + order) * CAP + rank
    every = jnp.arange(INPLANE * PLANES * CAP, dtype=jnp.int32)
    asked = jnp.sum(jnp.where(slots[None, :] == every[:, None], codes[None, :], 0), axis=1)
    asker = number // RANDOM
    asker = (asker // blocks) * 16 + asker % blocks + 1
    late = jnp.sum(jnp.where(slots[None, :] == every[:, None], asker[None, :], 0), axis=1) - 1
    late = late.reshape(INPLANE, PLANES, CAP)[:, PLANES - 1].reshape(-1)
    asked = asked.astype(jnp.bfloat16).reshape(INPLANE, 1, PLANES * CAP)
    asked = jnp.pad(asked, ((0, 0), (0, 15), (0, features - PLANES * CAP)))

    holder = global_blocks // blocks
    spot = global_blocks % blocks
    mine = holder == my_index

    def cut(source, g):
        piece = lax.dynamic_slice_in_dim(source, spot[g] * BLOCK, BLOCK, axis=0)
        return jnp.where(mine[g], piece, jnp.zeros_like(piece))

    asking = jnp.concatenate([cut(queries, g) for g in range(GLOBAL)])
    shared = jnp.concatenate(
        [cut(source, g) for g in range(GLOBAL) for source in (key_vectors, value_vectors)]
    ).reshape(INPLANE, -1, features)
    asking = jnp.broadcast_to(asking[None], (INPLANE, *asking.shape))
    found = jnp.concatenate([asking, shared, asked], axis=1)
    up_k, down_v = ring_step(key_vectors, 1), ring_step(value_vectors, -1)
    up_v, down_k = ring_step(value_vectors, 1), ring_step(key_vectors, -1)
    me = lax.axis_index("heads")
    peers = lax.axis_size("heads")
    width = out_weight.shape[1] // peers
    weights = [
        lax.dynamic_slice_in_dim(out_weight, ((me + away) % peers) * width, width, axis=1)
        for away in (0, 1, -1, 2)
    ]
    ends = jnp.concatenate([key_vectors[rows - BLOCK :], value_vectors[rows - BLOCK :]])
    starts = jnp.concatenate([key_vectors[:BLOCK], value_vectors[:BLOCK]])
    found, ends, starts, weights, _, _ = lax.optimization_barrier(
        (found, ends, starts, weights, up_k, down_v)
    )
    found = over_plane(found)
    many = GLOBAL * BLOCK
    asking = found[:, :many].sum(axis=0)
    shared = found[:, many:-16].sum(axis=0)
    asked = found[:, -16, : PLANES * CAP].astype(jnp.int32).reshape(-1)

    asked, _, _ = lax.optimization_barrier((asked, up_v, down_k))
    picks = picked(asked, 0, [key_vectors, value_vectors])
    arrived = [over_plane(picks)]
    ahead = [(i, i + 1) for i in range(shards - 1)]
    back = [(j, i) for i, j in ahead]

    def doubled(own, apart):
        return own + lax.ppermute(own, "seq_0", [(i, i ^ apart) for i in range(PLANES)])

    shared = doubled(shared, 1)
    first, parts = 1, ()
    beside = [lax.ppermute(ends, SEQ, ahead), lax.ppermute(starts, SEQ, back)]
    held = [up_k, down_k, up_v, down_v]
    first_pair = (up_v, down_k)
    for step in range(2, PLANES // 2 + 1):
        if step > 2:
            up_k, down_v, _ = lax.optimization_barrier((up_k, down_v, held if step == PLANES // 2 else first_pair))
        up_k = ring_step(up_k, 1)
        down_v = ring_step(down_v, -1)
        if step < PLANES // 2:
            up_v, down_k, _ = lax.optimization_barrier((up_v, down_k, picks))
        gate = (up_k, down_v) if step < PLANES // 2 else ()
        held, _, _, tied, parts, shared = lax.optimization_barrier(
            (held, gate, arrived[-1], beside if step > 2 else (), parts, shared)
        )
        if step > 2:
            weights[turn], before, after = tied
        else:
            before, after = beside
        turn, away = ((3, 2), (1, 1), (2, -1))[step - 2]
        beside, _ = lax.optimization_barrier((weights[turn], held))
        beside = (across(beside, away), before, after)
        if step < PLANES // 2:
            shared = doubled(shared, 2 * (step - 1))
        picks = picked(asked, first, held, (shared,) if step == PLANES // 2 else ())
        arrived.append(over_plane(picks))
        first += len(held) // 2
        both = held
        if step == 2:
            both = [*held[:2], key_vectors, *held[2:], value_vectors]
        parts = (global_parts(asking, both, parts),)
        if step < PLANES // 2:
            up_v = ring_step(up_v, 1)
            down_k = ring_step(down_k, -1)
            held = [up_k, down_k, up_v, down_v]
        else:
            held = [up_k, down_v]
    held, _, parts, beside = lax.optimization_barrier((held, picks, parts, beside))
    weights[turn], before, after = beside
    parts = (global_parts(asking, held, parts),)
    arrived.append(over_plane(picked(asked, first, held, parts)))
    place = jnp.concatenate(
        [
            jnp.stack([my_index * blocks, jnp.int32(shards * blocks)]).astype(jnp.int32),
            jnp.where(mine, spot, -1).astype(jnp.int32),
        ]
    )
    acc, stats = attended(
        slots, place, queries, key_vectors, value_vectors, before, after, arrived[:-1]
    )
    own_t, own_b, gout = finished(late, queries, acc, stats, arrived[-1])
    right_t, left_t = across(own_t, 1), across(own_t, -1)
    right_b, left_b = across(own_b, 1), across(own_b, -1)
    far_t, far_b = across(right_t, 1), across(left_b, -1)
    gout = over_plane(gout).reshape(heads, GLOBAL * BLOCK, DH)
    gout = gout.transpose(1, 0, 2).reshape(GLOBAL * BLOCK, features)
    rows_g = (gout, across(gout, 1), across(gout, -1), across(gout, 2))
    top = product((own_t, right_t, left_t, far_t), weights)
    return product((own_b, right_b, left_b, far_b), weights, place, top, rows_g)


def solution(mesh):
    torus = Mesh(
        mesh.devices.reshape(mesh.shape["heads"], 8, 4, 2), ("heads", "seq_0", "seq_1", "seq_2")
    )
    in_specs = (
        P(SEQ, "heads"),
        P(SEQ, "heads"),
        P(SEQ, "heads"),
        P("heads", SEQ, None),
        P(),
        P("heads", None),
    )
    out_specs = P(SEQ, "heads")
    return jax.shard_map(
        on_device, mesh=torus, in_specs=in_specs, out_specs=out_specs, check_vma=False
    )
```

```python
import jax
import jax.numpy as jnp
from jax import lax
from jax.experimental import pallas as pl
from jax.experimental.pallas import tpu as pltpu
from jax.sharding import Mesh
from jax.sharding import PartitionSpec as P

DH = 128
BLOCK = 64
RANDOM = 3
GLOBAL = 2
CAP = 4
PLANES = 8
INPLANE = 8
SEQ = ("seq_0", "seq_1", "seq_2")
PLANE = ("seq_1", "seq_2")
VMEM_LIMIT = 56 * 2**20
COST = 24 * 2**20


def ring_step(shard, step):
    peers = lax.axis_size("seq_0")
    return lax.ppermute(shard, "seq_0", [(i, (i + step) % peers) for i in range(peers)])


def across(shard, step):
    peers = lax.axis_size("heads")
    return lax.ppermute(shard, "heads", [(i, (i + step) % peers) for i in range(peers)])


def pick_kernel(n, first, codes, *refs):
    keys, values = refs[:n], refs[n : 2 * n]
    extra, out = refs[2 * n : -1], refs[-1]

    def one_peer(peer, carry):
        for run in range(n):
            for rank in range(CAP):
                code = codes[(peer * PLANES + first + run) * CAP + rank]
                rows = pl.ds(pl.multiple_of((code & 15) * BLOCK, BLOCK), BLOCK)
                cols = pl.ds(pl.multiple_of((code >> 4) * DH, DH), DH)
                at = (run * CAP + rank) * 2 * BLOCK
                out[peer, at : at + BLOCK] = keys[run][rows, cols]
                out[peer, at + BLOCK : at + 2 * BLOCK] = values[run][rows, cols]
        at = n * CAP * 2 * BLOCK
        if extra and extra[0].shape[0] < BLOCK:
            few = extra[0].shape[0]
            for h in range(extra[0].shape[1] // DH):
                out[peer, at + h * few : at + (h + 1) * few] = extra[0][:, h * DH : (h + 1) * DH]
        elif extra:
            own = extra[0][pl.ds(pl.multiple_of(peer * BLOCK, BLOCK), BLOCK)].astype(out.dtype)
            out[peer, at : at + BLOCK] = own[:, :DH]
            out[peer, at + BLOCK : at + 2 * BLOCK] = own[:, DH:]
        return carry

    lax.fori_loop(0, INPLANE, one_peer, 0)


def picked(codes, first, blocks, extra=()):
    n = len(blocks) // 2
    tail = sum(e.size if e.shape[0] < BLOCK else e.size // INPLANE for e in extra) // DH
    shape = (INPLANE, n * CAP * 2 * BLOCK + tail, DH)
    size = 2 * (sum(k.size for k in blocks) + INPLANE * n * CAP * 2 * BLOCK * DH)
    vmem = pl.BlockSpec(memory_space=pltpu.VMEM)
    return pl.pallas_call(
        lambda *refs: pick_kernel(n, first, *refs),
        out_shape=jax.ShapeDtypeStruct(shape, jnp.bfloat16),
        in_specs=[pl.BlockSpec(memory_space=pltpu.SMEM)] + [vmem] * (2 * n + len(extra)),
        out_specs=vmem,
        compiler_params=pltpu.CompilerParams(vmem_limit_bytes=32 * 2**20),
        cost_estimate=pl.CostEstimate(flops=0, bytes_accessed=24 * 2**20, transcendentals=0),
        name="pick_blocks",
    )(codes, *blocks, *extra)


def over_plane(parts):
    return lax.all_to_all(parts, PLANE, split_axis=0, concat_axis=0, tiled=True)


def global_kernel(n, asking, *refs):
    keys, values = refs[:n], refs[n : 2 * n]
    held, out = refs[2 * n : -1], refs[-1]
    heads = asking.shape[1] // DH
    many = GLOBAL * BLOCK
    lane = lax.broadcasted_iota(jnp.int32, (many, DH), 1)
    for h in range(heads):
        hs = slice(h * DH, (h + 1) * DH)
        rows = slice(h * many, (h + 1) * many)
        scores = [
            lax.dot_general(
                asking[:, hs], k[:, hs], (((1,), (1,)), ((), ())),
                preferred_element_type=jnp.float32,
            ) * (DH ** (-0.5))
            for k in keys
        ]
        top = jnp.max(scores[0], axis=1, keepdims=True)
        for other in scores[1:]:
            top = jnp.maximum(top, jnp.max(other, axis=1, keepdims=True))
        top = top.astype(jnp.bfloat16).astype(jnp.float32)
        if held:
            before = held[0][rows, DH : DH + 1]
            top = jnp.maximum(top, before)
            scale = jnp.exp(before - top)
            part = held[0][rows, :DH] * scale
            total = held[0][rows, DH + 1 : DH + 2] * scale
        else:
            part = jnp.zeros((many, DH), jnp.float32)
            total = jnp.zeros((many, 1), jnp.float32)
        for score, v in zip(scores, values):
            weights = jnp.exp(score - top)
            total += jnp.sum(weights, axis=1, keepdims=True)
            part += jnp.dot(
                weights.astype(jnp.bfloat16), v[:, hs], preferred_element_type=jnp.float32
            )
        upper = total.astype(jnp.bfloat16).astype(jnp.float32)
        side = jnp.where(lane == 0, top, jnp.where(lane == 1, total, 0.0))
        side = jnp.where(lane == 2, upper, jnp.where(lane == 3, total - upper, side))
        out[rows] = jnp.concatenate([part, side], axis=1)


def global_parts(asking, blocks, held=()):
    n = len(blocks) // 2
    vmem = pl.BlockSpec(memory_space=pltpu.VMEM)
    rows = asking.shape[0] * asking.shape[1] // DH
    return pl.pallas_call(
        lambda *refs: global_kernel(n, *refs),
        out_shape=jax.ShapeDtypeStruct((rows, 2 * DH), jnp.float32),
        in_specs=[vmem] * (1 + len(blocks) + len(held)),
        out_specs=vmem,
        compiler_params=pltpu.CompilerParams(vmem_limit_bytes=32 * 2**20),
        cost_estimate=pl.CostEstimate(
            flops=4 * rows * DH * 768 * n, bytes_accessed=24 * 2**20, transcendentals=rows * 768 * n
        ),
        name="global_parts",
    )(asking, *blocks, *held)


def merge_rows(parts, first, out):
    peers = parts.shape[0]
    sums, side = slice(first, first + BLOCK), slice(first + BLOCK, first + 2 * BLOCK)
    tops = [parts[p, side, 0:1].astype(jnp.float32) for p in range(peers)]
    top = tops[0]
    for other in tops[1:]:
        top = jnp.maximum(top, other)
    part = jnp.zeros((BLOCK, DH), jnp.float32)
    total = jnp.zeros((BLOCK, 1), jnp.float32)
    for p, own in enumerate(tops):
        scale = jnp.exp(own - top)
        part += scale * parts[p, sums].astype(jnp.float32)
        upper = parts[p, side, 2:3].astype(jnp.float32)
        total += scale * (upper + parts[p, side, 3:4].astype(jnp.float32))
    whole = (part / total).astype(jnp.bfloat16)
    for p in range(peers):
        out[p] = whole


def times(pieces, weights):
    total = jnp.dot(pieces[0][...], weights[0][...], preferred_element_type=jnp.float32)
    for piece, weight in zip(pieces[1:], weights[1:]):
        total += jnp.dot(piece[...], weight[...], preferred_element_type=jnp.float32)
    return total.astype(jnp.bfloat16)


def upper_kernel(*refs):
    refs[8][...] = times(refs[:4], refs[4:8])


def lower_kernel(place, top, *refs):
    low, rows, weights, out = refs[:4], refs[4:8], refs[8:12], refs[12]
    half = top.shape[0]
    out[:half] = top[...]
    out[half:] = times(low, weights)
    replaced = times(rows, weights)
    for g in range(GLOBAL):

        @pl.when(place[2 + g] >= 0)
        def _():
            at_rows = pl.ds(pl.multiple_of(place[2 + g] * BLOCK, BLOCK), BLOCK)
            out[at_rows] = replaced[g * BLOCK : (g + 1) * BLOCK]


def product(pieces, weights, place=None, top=None, rows=()):
    features, width = weights[0].shape
    step = width // 4
    whole = [pl.BlockSpec(p.shape, lambda i: (0, 0)) for p in (*pieces, *rows)]
    sliced = [pl.BlockSpec((features, step), lambda i: (0, i))] * 4
    head = [] if top is None else [place, top]
    half = pieces[0].shape[0]
    tall = half if top is None else 2 * half
    specs = [] if top is None else [
        pl.BlockSpec(memory_space=pltpu.SMEM), pl.BlockSpec((half, step), lambda i: (0, i))
    ]
    return pl.pallas_call(
        upper_kernel if top is None else lower_kernel,
        out_shape=jax.ShapeDtypeStruct((tall, width), jnp.bfloat16),
        grid=(4,),
        in_specs=specs + whole + sliced,
        out_specs=pl.BlockSpec((tall, step), lambda i: (0, i)),
        compiler_params=pltpu.CompilerParams(vmem_limit_bytes=32 * 2**20),
        cost_estimate=pl.CostEstimate(
            flops=8 * half * features * width, bytes_accessed=8 * 2**20, transcendentals=0
        ),
        name="upper_product" if top is None else "lower_product",
    )(*head, *pieces, *rows, *weights)


def attend_kernel(counts, slots, place, q, k, v, before, after, *refs):
    n = len(counts)
    arrived, acc, stats, held, sems = refs[:n], refs[n], refs[n + 1], refs[n + 2], refs[n + 3]
    kpad, vpad = refs[n + 4], refs[n + 5]
    copies = []
    at = 0
    for part, count in enumerate(counts):
        copies.append(
            pltpu.make_async_copy(arrived[part], held.at[:, pl.ds(at, count)], sems.at[part])
        )
        copies[-1].start()
        at += count
    rows = q.shape[0]
    heads = q.shape[1] // DH
    blocks = rows // BLOCK
    for side, (pad, own) in enumerate(((kpad, k), (vpad, v))):
        pad[0:BLOCK] = before[side * BLOCK : (side + 1) * BLOCK]
        pad[BLOCK : BLOCK + rows] = own[...]
        pad[BLOCK + rows :] = after[side * BLOCK : (side + 1) * BLOCK]
    for copy in copies:
        copy.wait()
    scale = DH ** (-0.5)
    col = lax.broadcasted_iota(jnp.int32, (1, (3 + RANDOM + GLOBAL) * BLOCK), 1) // BLOCK
    lane = lax.broadcasted_iota(jnp.int32, (BLOCK, DH), 1)
    few = GLOBAL * 2 * BLOCK // INPLANE

    def one_block(b, carry):
        at_rows = pl.ds(pl.multiple_of(b * BLOCK, BLOCK), BLOCK)
        win_rows = pl.ds(pl.multiple_of(b * BLOCK, BLOCK), 3 * BLOCK)
        number = place[0] + b
        outside = jnp.where(number == 0, 0, -1), jnp.where(number == place[1] - 1, 2, -1)
        for pair in range(0, heads, 2):
            both = range(pair, pair + 2)
            found, scores = [], []
            for h in both:
                hs = slice(h * DH, (h + 1) * DH)
                picks = []
                bias = jnp.where((col == outside[0]) | (col == outside[1]), -jnp.inf, 0.0)
                for r in range(RANDOM):
                    slot = slots[(h * blocks + b) * RANDOM + r]
                    late = ((slot >> 2) & 7) == PLANES - 1
                    bias = jnp.where(col == jnp.where(late, 3 + r, -1), -jnp.inf, bias)
                    slot = jnp.where(late, 0, slot)
                    picks.append((slot >> 5, pl.multiple_of((slot & 31) * 2 * BLOCK, 2 * BLOCK)))
                found.append(picks)
                at = sum(counts) + (h - heads) * few
                keys = jnp.concatenate(
                    [kpad[win_rows, hs]]
                    + [held[p[0], pl.ds(p[1], BLOCK)] for p in picks]
                    + [held[4 * g + i, at : at + few] for g in range(GLOBAL) for i in range(2)],
                    axis=0,
                )
                scores.append(
                    lax.dot_general(
                        q[at_rows, hs], keys, (((1,), (1,)), ((), ())),
                        preferred_element_type=jnp.float32,
                    ) * scale + bias
                )
            peaks = [jnp.max(own, axis=1, keepdims=True) for own in scores]
            weights = [jnp.exp(own - peak) for own, peak in zip(scores, peaks)]
            totals = [jnp.sum(own, axis=1, keepdims=True) for own in weights]
            sums = []
            for h, picks, own in zip(both, found, weights):
                hs = slice(h * DH, (h + 1) * DH)
                at = sum(counts) + (h - heads) * few
                values = jnp.concatenate(
                    [vpad[win_rows, hs]]
                    + [held[p[0], pl.ds(p[1] + BLOCK, BLOCK)] for p in picks]
                    + [held[4 * g + 2 + i, at : at + few] for g in range(GLOBAL) for i in range(2)],
                    axis=0,
                )
                sums.append(
                    jnp.dot(own.astype(jnp.bfloat16), values, preferred_element_type=jnp.float32)
                )
            for h, own, peak, total in zip(both, sums, peaks, totals):
                acc[at_rows, h * DH : (h + 1) * DH] = own
                stats[h, at_rows] = jnp.where(lane < DH // 2, peak, total)
        return carry

    lax.fori_loop(0, blocks, one_block, 0)


def attended(slots, place, q, k, v, before, after, arrived):
    rows, features = q.shape
    counts = tuple(a.shape[1] for a in arrived)
    vmem = pl.BlockSpec(memory_space=pltpu.VMEM)
    smem = pl.BlockSpec(memory_space=pltpu.SMEM)
    return pl.pallas_call(
        lambda *refs: attend_kernel(counts, *refs),
        out_shape=(
            jax.ShapeDtypeStruct((rows, features), jnp.float32),
            jax.ShapeDtypeStruct((features // DH, rows, DH), jnp.float32),
        ),
        in_specs=[smem, smem] + [vmem] * 5 + [pl.BlockSpec(memory_space=pl.ANY)] * len(arrived),
        out_specs=(vmem, vmem),
        scratch_shapes=[
            pltpu.VMEM((INPLANE, sum(counts), DH), jnp.bfloat16),
            pltpu.SemaphoreType.DMA((len(arrived),)),
            pltpu.VMEM((rows + 2 * BLOCK, features), jnp.bfloat16),
            pltpu.VMEM((rows + 2 * BLOCK, features), jnp.bfloat16),
        ],
        compiler_params=pltpu.CompilerParams(vmem_limit_bytes=VMEM_LIMIT),
        cost_estimate=pl.CostEstimate(
            flops=4 * rows * features * 512, bytes_accessed=COST, transcendentals=rows * 4 * 512
        ),
        name="attend",
    )(slots, place, q, k, v, before, after, *arrived)


def finish_kernel(late, q, acc, stats, blocks_late, top, low, gout, summed, held):
    scale = DH ** (-0.5)
    lane = lax.broadcasted_iota(jnp.int32, (BLOCK, DH), 1)
    summed[...] = acc[...]
    held[...] = stats[...]

    def one_peer(peer, carry):
        found = []
        for rank in range(CAP):
            code = late[peer * CAP + rank]
            near = jnp.maximum(code, 0)
            at_rows = pl.ds(pl.multiple_of((near & 15) * BLOCK, BLOCK), BLOCK)
            cols = pl.ds(pl.multiple_of((near >> 4) * DH, DH), DH)
            scores = lax.dot_general(
                q[at_rows, cols], blocks_late[peer, 2 * rank * BLOCK : (2 * rank + 1) * BLOCK],
                (((1,), (1,)), ((), ())), preferred_element_type=jnp.float32,
            ) * scale
            found.append((code, near >> 4, at_rows, cols, scores))
        peaks = [jnp.max(own[-1], axis=1, keepdims=True) for own in found]
        weights = [jnp.exp(own[-1] - peak) for own, peak in zip(found, peaks)]
        totals = [jnp.sum(own, axis=1, keepdims=True) for own in weights]
        sums = [
            jnp.dot(
                own.astype(jnp.bfloat16),
                blocks_late[peer, (2 * rank + 1) * BLOCK : (2 * rank + 2) * BLOCK],
                preferred_element_type=jnp.float32,
            )
            for rank, own in enumerate(weights)
        ]
        for (code, h, at_rows, cols, _), peak, total, own in zip(found, peaks, totals, sums):

            @pl.when(code >= 0)
            def _():
                before = held[h, at_rows, 0:1]
                top = jnp.maximum(before, peak)
                less, more = jnp.exp(before - top), jnp.exp(peak - top)
                summed[at_rows, cols] = summed[at_rows, cols] * less + own * more
                both = held[h, at_rows, DH // 2 : DH // 2 + 1] * less + total * more
                held[h, at_rows] = jnp.where(lane < DH // 2, top, both)

        return carry

    lax.fori_loop(0, INPLANE, one_peer, 0)
    merge_rows(blocks_late, 2 * CAP * BLOCK, gout)
    half = top.shape[0]
    for side, out in enumerate((top, low)):

        def one_block(b, carry):
            to_rows = pl.ds(pl.multiple_of(b * BLOCK, BLOCK), BLOCK)
            at_rows = pl.ds(pl.multiple_of(b * BLOCK + side * half, BLOCK), BLOCK)
            for h in range(held.shape[0]):
                hs = slice(h * DH, (h + 1) * DH)
                total = held[h, at_rows, DH // 2 : DH // 2 + 1]
                out[to_rows, hs] = (summed[at_rows, hs] / total).astype(jnp.bfloat16)
            return carry

        lax.fori_loop(0, half // BLOCK, one_block, 0)


def finished(late, q, acc, stats, blocks_late):
    vmem = pl.BlockSpec(memory_space=pltpu.VMEM)
    rows, features = q.shape
    half = jax.ShapeDtypeStruct((rows // 2, features), jnp.bfloat16)
    return pl.pallas_call(
        finish_kernel,
        out_shape=(half, half, jax.ShapeDtypeStruct((INPLANE, BLOCK, DH), jnp.bfloat16)),
        in_specs=[pl.BlockSpec(memory_space=pltpu.SMEM)] + [vmem] * 4,
        out_specs=(vmem, vmem, vmem),
        scratch_shapes=[
            pltpu.VMEM(acc.shape, jnp.float32),
            pltpu.VMEM(stats.shape, jnp.float32),
        ],
        compiler_params=pltpu.CompilerParams(vmem_limit_bytes=32 * 2**20),
        name="late_blocks",
    )(late, q, acc, stats, blocks_late)


def on_device(queries, key_vectors, value_vectors, random_blocks, global_blocks, out_weight):
    shards = lax.axis_size(SEQ)
    my_index = lax.axis_index(SEQ)
    my_plane = lax.axis_index("seq_0")
    rows, features = queries.shape
    heads = features // DH
    blocks = rows // BLOCK
    requests = heads * blocks * RANDOM

    flat = random_blocks.reshape(requests)
    holders = flat // blocks
    number = jnp.arange(requests, dtype=jnp.int32)
    codes = (number // (blocks * RANDOM)) * 16 + flat % blocks
    earlier = (holders[:, None] == holders[None, :]) & (number[None, :] < number[:, None])
    rank = jnp.sum(earlier.astype(jnp.int32), axis=1)
    apart = (holders // INPLANE - my_plane) % PLANES
    order = jnp.where(apart <= PLANES // 2, jnp.minimum(2 * apart, PLANES - 1), 2 * PLANES - 1 - 2 * apart)
    slots = ((holders % INPLANE) * PLANES + order) * CAP + rank
    every = jnp.arange(INPLANE * PLANES * CAP, dtype=jnp.int32)
    asked = jnp.sum(jnp.where(slots[None, :] == every[:, None], codes[None, :], 0), axis=1)
    asker = number // RANDOM
    asker = (asker // blocks) * 16 + asker % blocks + 1
    late = jnp.sum(jnp.where(slots[None, :] == every[:, None], asker[None, :], 0), axis=1) - 1
    late = late.reshape(INPLANE, PLANES, CAP)[:, PLANES - 1].reshape(-1)
    asked = asked.astype(jnp.bfloat16).reshape(INPLANE, 1, PLANES * CAP)
    asked = jnp.pad(asked, ((0, 0), (0, 15), (0, features - PLANES * CAP)))

    holder = global_blocks // blocks
    spot = global_blocks % blocks
    mine = holder == my_index

    def cut(source, g):
        piece = lax.dynamic_slice_in_dim(source, spot[g] * BLOCK, BLOCK, axis=0)
        return jnp.where(mine[g], piece, jnp.zeros_like(piece))

    asking = jnp.concatenate([cut(queries, g) for g in range(GLOBAL)])
    shared = jnp.concatenate(
        [cut(source, g) for g in range(GLOBAL) for source in (key_vectors, value_vectors)]
    ).reshape(INPLANE, -1, features)
    asking = jnp.broadcast_to(asking[None], (INPLANE, *asking.shape))
    found = jnp.concatenate([asking, shared, asked], axis=1)
    up_k, down_v = ring_step(key_vectors, 1), ring_step(value_vectors, -1)
    up_v, down_k = ring_step(value_vectors, 1), ring_step(key_vectors, -1)
    me = lax.axis_index("heads")
    peers = lax.axis_size("heads")
    width = out_weight.shape[1] // peers
    weights = [
        lax.dynamic_slice_in_dim(out_weight, ((me + away) % peers) * width, width, axis=1)
        for away in (0, 1, -1, 2)
    ]
    ends = jnp.concatenate([key_vectors[rows - BLOCK :], value_vectors[rows - BLOCK :]])
    starts = jnp.concatenate([key_vectors[:BLOCK], value_vectors[:BLOCK]])
    found, ends, starts, weights, _, _ = lax.optimization_barrier(
        (found, ends, starts, weights, up_k, down_v)
    )
    found = over_plane(found)
    many = GLOBAL * BLOCK
    asking = found[:, :many].sum(axis=0)
    shared = found[:, many:-16].sum(axis=0)
    asked = found[:, -16, : PLANES * CAP].astype(jnp.int32).reshape(-1)

    picks, arrived = (), []
    ahead = [(i, i + 1) for i in range(shards - 1)]
    back = [(j, i) for i, j in ahead]

    def doubled(own, apart):
        return own + lax.ppermute(own, "seq_0", [(i, i ^ apart) for i in range(PLANES)])

    shared = doubled(shared, 1)
    first, parts = 0, ()
    beside = ()
    held = [key_vectors, up_k, down_k, value_vectors, up_v, down_v]
    first_pair = (up_v, down_k)
    for step in range(2, PLANES // 2 + 1):
        if step > 2:
            up_k, down_v, _ = lax.optimization_barrier((up_k, down_v, held if step == PLANES // 2 else first_pair))
        up_k = ring_step(up_k, 1)
        down_v = ring_step(down_v, -1)
        if step < PLANES // 2:
            up_v, down_k, _ = lax.optimization_barrier((up_v, down_k, picks))
        gate = (up_k, down_v) if step < PLANES // 2 else ()
        held, _, _, tied, parts, shared = lax.optimization_barrier(
            (held, gate, arrived[-1:], beside if step > 2 else (), parts, shared)
        )
        if step > 2:
            weights[turn] = tied[0]
        if step > 3:
            before, after = tied[1:]
        turn, away = ((3, 2), (1, 1), (2, -1))[step - 2]
        beside, _ = lax.optimization_barrier((weights[turn], held))
        beside = (across(beside, away),)
        if step == 3:
            ends, starts, _ = lax.optimization_barrier((ends, starts, held))
            beside += (lax.ppermute(ends, SEQ, ahead), lax.ppermute(starts, SEQ, back))
        if step == 3:
            shared, _ = lax.optimization_barrier((shared, held))
            shared = doubled(doubled(shared, 2), 4)
        picks = picked(asked, first, held, (shared,) if step == PLANES // 2 else ())
        arrived.append(over_plane(picks))
        first += len(held) // 2
        parts = (global_parts(asking, held, parts),)
        if step < PLANES // 2:
            up_v = ring_step(up_v, 1)
            down_k = ring_step(down_k, -1)
            held = [up_k, down_k, up_v, down_v]
        else:
            held = [up_k, down_v]
    held, _, parts, beside = lax.optimization_barrier((held, picks, parts, beside))
    weights[turn] = beside[0]
    parts = (global_parts(asking, held, parts),)
    arrived.append(over_plane(picked(asked, first, held, parts)))
    place = jnp.concatenate(
        [
            jnp.stack([my_index * blocks, jnp.int32(shards * blocks)]).astype(jnp.int32),
            jnp.where(mine, spot, -1).astype(jnp.int32),
        ]
    )
    acc, stats = attended(
        slots, place, queries, key_vectors, value_vectors, before, after, arrived[:-1]
    )
    own_t, own_b, gout = finished(late, queries, acc, stats, arrived[-1])
    right_t, left_t = across(own_t, 1), across(own_t, -1)
    right_b, left_b = across(own_b, 1), across(own_b, -1)
    far_t, far_b = across(right_t, 1), across(left_b, -1)
    gout = over_plane(gout).reshape(heads, GLOBAL * BLOCK, DH)
    gout = gout.transpose(1, 0, 2).reshape(GLOBAL * BLOCK, features)
    rows_g = (gout, across(gout, 1), across(gout, -1), across(gout, 2))
    top = product((own_t, right_t, left_t, far_t), weights)
    return product((own_b, right_b, left_b, far_b), weights, place, top, rows_g)


def solution(mesh):
    torus = Mesh(
        mesh.devices.reshape(mesh.shape["heads"], 8, 4, 2), ("heads", "seq_0", "seq_1", "seq_2")
    )
    in_specs = (
        P(SEQ, "heads"),
        P(SEQ, "heads"),
        P(SEQ, "heads"),
        P("heads", SEQ, None),
        P(),
        P("heads", None),
    )
    out_specs = P(SEQ, "heads")
    return jax.shard_map(
        on_device, mesh=torus, in_specs=in_specs, out_specs=out_specs, check_vma=False
    )
```

```python
import jax
import jax.numpy as jnp
from jax import lax
from jax.experimental import pallas as pl
from jax.experimental.pallas import tpu as pltpu
from jax.sharding import Mesh
from jax.sharding import PartitionSpec as P

DH = 128
BLOCK = 64
RANDOM = 3
GLOBAL = 2
CAP = 4
PLANES = 8
INPLANE = 8
SEQ = ("seq_0", "seq_1", "seq_2")
PLANE = ("seq_1", "seq_2")
VMEM_LIMIT = 56 * 2**20
COST = 24 * 2**20


def ring_step(shard, step):
    peers = lax.axis_size("seq_0")
    return lax.ppermute(shard, "seq_0", [(i, (i + step) % peers) for i in range(peers)])


def across(shard, step):
    peers = lax.axis_size("heads")
    return lax.ppermute(shard, "heads", [(i, (i + step) % peers) for i in range(peers)])


def pick_kernel(n, first, codes, *refs):
    keys, values = refs[:n], refs[n : 2 * n]
    extra, out = refs[2 * n : -1], refs[-1]

    def one_peer(peer, carry):
        for run in range(n):
            for rank in range(CAP):
                code = codes[(peer * PLANES + first + run) * CAP + rank]
                rows = pl.ds(pl.multiple_of((code & 15) * BLOCK, BLOCK), BLOCK)
                cols = pl.ds(pl.multiple_of((code >> 4) * DH, DH), DH)
                at = (run * CAP + rank) * 2 * BLOCK
                out[peer, at : at + BLOCK] = keys[run][rows, cols]
                out[peer, at + BLOCK : at + 2 * BLOCK] = values[run][rows, cols]
        at = n * CAP * 2 * BLOCK
        if extra and extra[0].shape[0] < BLOCK:
            few = extra[0].shape[0]
            for h in range(extra[0].shape[1] // DH):
                out[peer, at + h * few : at + (h + 1) * few] = extra[0][:, h * DH : (h + 1) * DH]
        elif extra:
            own = extra[0][pl.ds(pl.multiple_of(peer * BLOCK, BLOCK), BLOCK)].astype(out.dtype)
            out[peer, at : at + BLOCK] = own[:, :DH]
            out[peer, at + BLOCK : at + 2 * BLOCK] = own[:, DH:]
        return carry

    lax.fori_loop(0, INPLANE, one_peer, 0)


def picked(codes, first, blocks, extra=()):
    n = len(blocks) // 2
    tail = sum(e.size if e.shape[0] < BLOCK else e.size // INPLANE for e in extra) // DH
    shape = (INPLANE, n * CAP * 2 * BLOCK + tail, DH)
    size = 2 * (sum(k.size for k in blocks) + INPLANE * n * CAP * 2 * BLOCK * DH)
    vmem = pl.BlockSpec(memory_space=pltpu.VMEM)
    return pl.pallas_call(
        lambda *refs: pick_kernel(n, first, *refs),
        out_shape=jax.ShapeDtypeStruct(shape, jnp.bfloat16),
        in_specs=[pl.BlockSpec(memory_space=pltpu.SMEM)] + [vmem] * (2 * n + len(extra)),
        out_specs=vmem,
        compiler_params=pltpu.CompilerParams(vmem_limit_bytes=32 * 2**20),
        cost_estimate=pl.CostEstimate(flops=0, bytes_accessed=24 * 2**20, transcendentals=0),
        name="pick_blocks",
    )(codes, *blocks, *extra)


def over_plane(parts):
    return lax.all_to_all(parts, PLANE, split_axis=0, concat_axis=0, tiled=True)


def global_kernel(n, asking, *refs):
    keys, values = refs[:n], refs[n : 2 * n]
    held, out = refs[2 * n : -1], refs[-1]
    heads = asking.shape[1] // DH
    many = GLOBAL * BLOCK
    lane = lax.broadcasted_iota(jnp.int32, (many, DH), 1)
    for h in range(heads):
        hs = slice(h * DH, (h + 1) * DH)
        rows = slice(h * many, (h + 1) * many)
        scores = [
            lax.dot_general(
                asking[:, hs], k[:, hs], (((1,), (1,)), ((), ())),
                preferred_element_type=jnp.float32,
            ) * (DH ** (-0.5))
            for k in keys
        ]
        top = jnp.max(scores[0], axis=1, keepdims=True)
        for other in scores[1:]:
            top = jnp.maximum(top, jnp.max(other, axis=1, keepdims=True))
        top = top.astype(jnp.bfloat16).astype(jnp.float32)
        if held:
            before = held[0][rows, DH : DH + 1]
            top = jnp.maximum(top, before)
            scale = jnp.exp(before - top)
            part = held[0][rows, :DH] * scale
            total = held[0][rows, DH + 1 : DH + 2] * scale
        else:
            part = jnp.zeros((many, DH), jnp.float32)
            total = jnp.zeros((many, 1), jnp.float32)
        for score, v in zip(scores, values):
            weights = jnp.exp(score - top)
            total += jnp.sum(weights, axis=1, keepdims=True)
            part += jnp.dot(
                weights.astype(jnp.bfloat16), v[:, hs], preferred_element_type=jnp.float32
            )
        upper = total.astype(jnp.bfloat16).astype(jnp.float32)
        side = jnp.where(lane == 0, top, jnp.where(lane == 1, total, 0.0))
        side = jnp.where(lane == 2, upper, jnp.where(lane == 3, total - upper, side))
        out[rows] = jnp.concatenate([part, side], axis=1)


def global_parts(asking, blocks, held=()):
    n = len(blocks) // 2
    vmem = pl.BlockSpec(memory_space=pltpu.VMEM)
    rows = asking.shape[0] * asking.shape[1] // DH
    return pl.pallas_call(
        lambda *refs: global_kernel(n, *refs),
        out_shape=jax.ShapeDtypeStruct((rows, 2 * DH), jnp.float32),
        in_specs=[vmem] * (1 + len(blocks) + len(held)),
        out_specs=vmem,
        compiler_params=pltpu.CompilerParams(vmem_limit_bytes=32 * 2**20),
        cost_estimate=pl.CostEstimate(
            flops=4 * rows * DH * 768 * n, bytes_accessed=24 * 2**20, transcendentals=rows * 768 * n
        ),
        name="global_parts",
    )(asking, *blocks, *held)


def merge_rows(parts, first, out):
    peers = parts.shape[0]
    sums, side = slice(first, first + BLOCK), slice(first + BLOCK, first + 2 * BLOCK)
    tops = [parts[p, side, 0:1].astype(jnp.float32) for p in range(peers)]
    top = tops[0]
    for other in tops[1:]:
        top = jnp.maximum(top, other)
    part = jnp.zeros((BLOCK, DH), jnp.float32)
    total = jnp.zeros((BLOCK, 1), jnp.float32)
    for p, own in enumerate(tops):
        scale = jnp.exp(own - top)
        part += scale * parts[p, sums].astype(jnp.float32)
        upper = parts[p, side, 2:3].astype(jnp.float32)
        total += scale * (upper + parts[p, side, 3:4].astype(jnp.float32))
    whole = (part / total).astype(jnp.bfloat16)
    for p in range(peers):
        out[p] = whole


def times(pieces, weights):
    total = jnp.dot(pieces[0][...], weights[0][...], preferred_element_type=jnp.float32)
    for piece, weight in zip(pieces[1:], weights[1:]):
        total += jnp.dot(piece[...], weight[...], preferred_element_type=jnp.float32)
    return total.astype(jnp.bfloat16)


def upper_kernel(*refs):
    refs[8][...] = times(refs[:4], refs[4:8])


def lower_kernel(place, top, *refs):
    low, rows, weights, out = refs[:4], refs[4:8], refs[8:12], refs[12]
    half = top.shape[0]
    out[:half] = top[...]
    out[half:] = times(low, weights)
    replaced = times(rows, weights)
    for g in range(GLOBAL):

        @pl.when(place[2 + g] >= 0)
        def _():
            at_rows = pl.ds(pl.multiple_of(place[2 + g] * BLOCK, BLOCK), BLOCK)
            out[at_rows] = replaced[g * BLOCK : (g + 1) * BLOCK]


def product(pieces, weights, place=None, top=None, rows=()):
    features, width = weights[0].shape
    step = width // 4
    whole = [pl.BlockSpec(p.shape, lambda i: (0, 0)) for p in (*pieces, *rows)]
    sliced = [pl.BlockSpec((features, step), lambda i: (0, i))] * 4
    head = [] if top is None else [place, top]
    half = pieces[0].shape[0]
    tall = half if top is None else 2 * half
    specs = [] if top is None else [
        pl.BlockSpec(memory_space=pltpu.SMEM), pl.BlockSpec((half, step), lambda i: (0, i))
    ]
    return pl.pallas_call(
        upper_kernel if top is None else lower_kernel,
        out_shape=jax.ShapeDtypeStruct((tall, width), jnp.bfloat16),
        grid=(4,),
        in_specs=specs + whole + sliced,
        out_specs=pl.BlockSpec((tall, step), lambda i: (0, i)),
        compiler_params=pltpu.CompilerParams(vmem_limit_bytes=32 * 2**20),
        cost_estimate=pl.CostEstimate(
            flops=8 * half * features * width, bytes_accessed=8 * 2**20, transcendentals=0
        ),
        name="upper_product" if top is None else "lower_product",
    )(*head, *pieces, *rows, *weights)


def attend_kernel(counts, slots, place, q, k, v, before, after, *refs):
    n = len(counts)
    arrived, acc, stats, held, sems = refs[:n], refs[n], refs[n + 1], refs[n + 2], refs[n + 3]
    kpad, vpad = refs[n + 4], refs[n + 5]
    copies = []
    at = 0
    for part, count in enumerate(counts):
        copies.append(
            pltpu.make_async_copy(arrived[part], held.at[:, pl.ds(at, count)], sems.at[part])
        )
        copies[-1].start()
        at += count
    rows = q.shape[0]
    heads = q.shape[1] // DH
    blocks = rows // BLOCK
    for side, (pad, own) in enumerate(((kpad, k), (vpad, v))):
        pad[0:BLOCK] = before[side * BLOCK : (side + 1) * BLOCK]
        pad[BLOCK : BLOCK + rows] = own[...]
        pad[BLOCK + rows :] = after[side * BLOCK : (side + 1) * BLOCK]
    for copy in copies:
        copy.wait()
    scale = DH ** (-0.5)
    col = lax.broadcasted_iota(jnp.int32, (1, (3 + RANDOM + GLOBAL) * BLOCK), 1) // BLOCK
    lane = lax.broadcasted_iota(jnp.int32, (BLOCK, DH), 1)
    few = GLOBAL * 2 * BLOCK // INPLANE

    def one_block(b, carry):
        at_rows = pl.ds(pl.multiple_of(b * BLOCK, BLOCK), BLOCK)
        win_rows = pl.ds(pl.multiple_of(b * BLOCK, BLOCK), 3 * BLOCK)
        number = place[0] + b
        outside = jnp.where(number == 0, 0, -1), jnp.where(number == place[1] - 1, 2, -1)
        for pair in range(0, heads, 2):
            both = range(pair, pair + 2)
            found, scores = [], []
            for h in both:
                hs = slice(h * DH, (h + 1) * DH)
                picks = []
                bias = jnp.where((col == outside[0]) | (col == outside[1]), -jnp.inf, 0.0)
                for r in range(RANDOM):
                    slot = slots[(h * blocks + b) * RANDOM + r]
                    late = ((slot >> 2) & 7) == PLANES - 1
                    bias = jnp.where(col == jnp.where(late, 3 + r, -1), -jnp.inf, bias)
                    slot = jnp.where(late, 0, slot)
                    picks.append((slot >> 5, pl.multiple_of((slot & 31) * 2 * BLOCK, 2 * BLOCK)))
                found.append(picks)
                at = sum(counts) + (h - heads) * few
                keys = jnp.concatenate(
                    [kpad[win_rows, hs]]
                    + [held[p[0], pl.ds(p[1], BLOCK)] for p in picks]
                    + [held[4 * g + i, at : at + few] for g in range(GLOBAL) for i in range(2)],
                    axis=0,
                )
                scores.append(
                    lax.dot_general(
                        q[at_rows, hs], keys, (((1,), (1,)), ((), ())),
                        preferred_element_type=jnp.float32,
                    ) * scale + bias
                )
            peaks = [jnp.max(own, axis=1, keepdims=True) for own in scores]
            weights = [jnp.exp(own - peak) for own, peak in zip(scores, peaks)]
            totals = [jnp.sum(own, axis=1, keepdims=True) for own in weights]
            sums = []
            for h, picks, own in zip(both, found, weights):
                hs = slice(h * DH, (h + 1) * DH)
                at = sum(counts) + (h - heads) * few
                values = jnp.concatenate(
                    [vpad[win_rows, hs]]
                    + [held[p[0], pl.ds(p[1] + BLOCK, BLOCK)] for p in picks]
                    + [held[4 * g + 2 + i, at : at + few] for g in range(GLOBAL) for i in range(2)],
                    axis=0,
                )
                sums.append(
                    jnp.dot(own.astype(jnp.bfloat16), values, preferred_element_type=jnp.float32)
                )
            for h, own, peak, total in zip(both, sums, peaks, totals):
                acc[at_rows, h * DH : (h + 1) * DH] = own
                stats[h, at_rows] = jnp.where(lane < DH // 2, peak, total)
        return carry

    lax.fori_loop(0, blocks, one_block, 0)


def attended(slots, place, q, k, v, before, after, arrived):
    rows, features = q.shape
    counts = tuple(a.shape[1] for a in arrived)
    vmem = pl.BlockSpec(memory_space=pltpu.VMEM)
    smem = pl.BlockSpec(memory_space=pltpu.SMEM)
    return pl.pallas_call(
        lambda *refs: attend_kernel(counts, *refs),
        out_shape=(
            jax.ShapeDtypeStruct((rows, features), jnp.float32),
            jax.ShapeDtypeStruct((features // DH, rows, DH), jnp.float32),
        ),
        in_specs=[smem, smem] + [vmem] * 5 + [pl.BlockSpec(memory_space=pl.ANY)] * len(arrived),
        out_specs=(vmem, vmem),
        scratch_shapes=[
            pltpu.VMEM((INPLANE, sum(counts), DH), jnp.bfloat16),
            pltpu.SemaphoreType.DMA((len(arrived),)),
            pltpu.VMEM((rows + 2 * BLOCK, features), jnp.bfloat16),
            pltpu.VMEM((rows + 2 * BLOCK, features), jnp.bfloat16),
        ],
        compiler_params=pltpu.CompilerParams(vmem_limit_bytes=VMEM_LIMIT),
        cost_estimate=pl.CostEstimate(
            flops=4 * rows * features * 512, bytes_accessed=COST, transcendentals=rows * 4 * 512
        ),
        name="attend",
    )(slots, place, q, k, v, before, after, *arrived)


def finish_kernel(late, q, acc, stats, blocks_late, top, low, gout, summed, held):
    scale = DH ** (-0.5)
    lane = lax.broadcasted_iota(jnp.int32, (BLOCK, DH), 1)
    summed[...] = acc[...]
    held[...] = stats[...]

    def one_peer(peer, carry):
        found = []
        for rank in range(CAP):
            code = late[peer * CAP + rank]
            near = jnp.maximum(code, 0)
            at_rows = pl.ds(pl.multiple_of((near & 15) * BLOCK, BLOCK), BLOCK)
            cols = pl.ds(pl.multiple_of((near >> 4) * DH, DH), DH)
            scores = lax.dot_general(
                q[at_rows, cols], blocks_late[peer, 2 * rank * BLOCK : (2 * rank + 1) * BLOCK],
                (((1,), (1,)), ((), ())), preferred_element_type=jnp.float32,
            ) * scale
            found.append((code, near >> 4, at_rows, cols, scores))
        peaks = [jnp.max(own[-1], axis=1, keepdims=True) for own in found]
        weights = [jnp.exp(own[-1] - peak) for own, peak in zip(found, peaks)]
        totals = [jnp.sum(own, axis=1, keepdims=True) for own in weights]
        sums = [
            jnp.dot(
                own.astype(jnp.bfloat16),
                blocks_late[peer, (2 * rank + 1) * BLOCK : (2 * rank + 2) * BLOCK],
                preferred_element_type=jnp.float32,
            )
            for rank, own in enumerate(weights)
        ]
        for (code, h, at_rows, cols, _), peak, total, own in zip(found, peaks, totals, sums):

            @pl.when(code >= 0)
            def _():
                before = held[h, at_rows, 0:1]
                top = jnp.maximum(before, peak)
                less, more = jnp.exp(before - top), jnp.exp(peak - top)
                summed[at_rows, cols] = summed[at_rows, cols] * less + own * more
                both = held[h, at_rows, DH // 2 : DH // 2 + 1] * less + total * more
                held[h, at_rows] = jnp.where(lane < DH // 2, top, both)

        return carry

    lax.fori_loop(0, INPLANE, one_peer, 0)
    merge_rows(blocks_late, 2 * CAP * BLOCK, gout)
    half = top.shape[0]
    for side, out in enumerate((top, low)):

        def one_block(b, carry):
            to_rows = pl.ds(pl.multiple_of(b * BLOCK, BLOCK), BLOCK)
            at_rows = pl.ds(pl.multiple_of(b * BLOCK + side * half, BLOCK), BLOCK)
            for h in range(held.shape[0]):
                hs = slice(h * DH, (h + 1) * DH)
                total = held[h, at_rows, DH // 2 : DH // 2 + 1]
                out[to_rows, hs] = (summed[at_rows, hs] / total).astype(jnp.bfloat16)
            return carry

        lax.fori_loop(0, half // BLOCK, one_block, 0)


def finished(late, q, acc, stats, blocks_late):
    vmem = pl.BlockSpec(memory_space=pltpu.VMEM)
    rows, features = q.shape
    half = jax.ShapeDtypeStruct((rows // 2, features), jnp.bfloat16)
    return pl.pallas_call(
        finish_kernel,
        out_shape=(half, half, jax.ShapeDtypeStruct((INPLANE, BLOCK, DH), jnp.bfloat16)),
        in_specs=[pl.BlockSpec(memory_space=pltpu.SMEM)] + [vmem] * 4,
        out_specs=(vmem, vmem, vmem),
        scratch_shapes=[
            pltpu.VMEM(acc.shape, jnp.float32),
            pltpu.VMEM(stats.shape, jnp.float32),
        ],
        compiler_params=pltpu.CompilerParams(vmem_limit_bytes=32 * 2**20),
        name="late_blocks",
    )(late, q, acc, stats, blocks_late)


def on_device(queries, key_vectors, value_vectors, random_blocks, global_blocks, out_weight):
    shards = lax.axis_size(SEQ)
    my_index = lax.axis_index(SEQ)
    my_plane = lax.axis_index("seq_0")
    rows, features = queries.shape
    heads = features // DH
    blocks = rows // BLOCK
    requests = heads * blocks * RANDOM

    flat = random_blocks.reshape(requests)
    holders = flat // blocks
    number = jnp.arange(requests, dtype=jnp.int32)
    codes = (number // (blocks * RANDOM)) * 16 + flat % blocks
    earlier = (holders[:, None] == holders[None, :]) & (number[None, :] < number[:, None])
    rank = jnp.sum(earlier.astype(jnp.int32), axis=1)
    apart = (holders // INPLANE - my_plane) % PLANES
    order = jnp.where(apart <= PLANES // 2, jnp.minimum(2 * apart, PLANES - 1), 2 * PLANES - 1 - 2 * apart)
    slots = ((holders % INPLANE) * PLANES + order) * CAP + rank
    every = jnp.arange(INPLANE * PLANES * CAP, dtype=jnp.int32)
    asked = jnp.sum(jnp.where(slots[None, :] == every[:, None], codes[None, :], 0), axis=1)
    asker = number // RANDOM
    asker = (asker // blocks) * 16 + asker % blocks + 1
    late = jnp.sum(jnp.where(slots[None, :] == every[:, None], asker[None, :], 0), axis=1) - 1
    late = late.reshape(INPLANE, PLANES, CAP)[:, PLANES - 1].reshape(-1)
    asked = asked.astype(jnp.bfloat16).reshape(INPLANE, 1, PLANES * CAP)
    asked = jnp.pad(asked, ((0, 0), (0, 15), (0, features - PLANES * CAP)))

    holder = global_blocks // blocks
    spot = global_blocks % blocks
    mine = holder == my_index

    def cut(source, g):
        piece = lax.dynamic_slice_in_dim(source, spot[g] * BLOCK, BLOCK, axis=0)
        return jnp.where(mine[g], piece, jnp.zeros_like(piece))

    asking = jnp.concatenate([cut(queries, g) for g in range(GLOBAL)])
    shared = jnp.concatenate(
        [cut(source, g) for g in range(GLOBAL) for source in (key_vectors, value_vectors)]
    ).reshape(INPLANE, -1, features)
    asking = jnp.broadcast_to(asking[None], (INPLANE, *asking.shape))
    found = jnp.concatenate([asking, shared, asked], axis=1)
    up_k, down_v = ring_step(key_vectors, 1), ring_step(value_vectors, -1)
    up_v, down_k = ring_step(value_vectors, 1), ring_step(key_vectors, -1)
    me = lax.axis_index("heads")
    peers = lax.axis_size("heads")
    width = out_weight.shape[1] // peers
    weights = [
        lax.dynamic_slice_in_dim(out_weight, ((me + away) % peers) * width, width, axis=1)
        for away in (0, 1, -1, 2)
    ]
    ends = jnp.concatenate([key_vectors[rows - BLOCK :], value_vectors[rows - BLOCK :]])
    starts = jnp.concatenate([key_vectors[:BLOCK], value_vectors[:BLOCK]])
    found, ends, starts, weights, _, _ = lax.optimization_barrier(
        (found, ends, starts, weights, up_k, down_v)
    )
    found = over_plane(found)
    many = GLOBAL * BLOCK
    asking = found[:, :many].sum(axis=0)
    shared = found[:, many:-16].sum(axis=0)
    asked = found[:, -16, : PLANES * CAP].astype(jnp.int32).reshape(-1)

    picks, arrived = (), []
    ahead = [(i, i + 1) for i in range(shards - 1)]
    back = [(j, i) for i, j in ahead]

    def doubled(own, apart):
        return own + lax.ppermute(own, "seq_0", [(i, i ^ apart) for i in range(PLANES)])

    shared = doubled(shared, 1)
    first, parts = 0, ()
    beside = ()
    held = [key_vectors, up_k, down_k, value_vectors, up_v, down_v]
    first_pair = (up_v, down_k)
    for step in range(2, PLANES // 2 + 1):
        if step > 2:
            up_k, down_v, _ = lax.optimization_barrier((up_k, down_v, held if step == PLANES // 2 else first_pair))
        up_k = ring_step(up_k, 1)
        down_v = ring_step(down_v, -1)
        if step < PLANES // 2:
            up_v, down_k, _ = lax.optimization_barrier((up_v, down_k, picks))
        gate = (up_k, down_v) if step < PLANES // 2 else ()
        held, _, _, tied, parts, shared = lax.optimization_barrier(
            (held, gate, arrived[-1:], beside if step > 2 else (), parts, shared)
        )
        if step > 2:
            weights[turn] = tied[0]
        if step > 3:
            before, after = tied[1:]
        turn, away = ((3, 2), (1, 1), (2, -1))[step - 2]
        beside, _ = lax.optimization_barrier((weights[turn], held))
        beside = (across(beside, away),)
        if step == 3:
            ends, starts, _ = lax.optimization_barrier((ends, starts, held))
            beside += (lax.ppermute(ends, SEQ, ahead), lax.ppermute(starts, SEQ, back))
        if step < PLANES // 2:
            shared = doubled(shared, 2 * (step - 1))
        picks = picked(asked, first, held, (shared,) if step == PLANES // 2 else ())
        arrived.append(over_plane(picks))
        first += len(held) // 2
        parts = (global_parts(asking, held, parts),)
        if step < PLANES // 2:
            up_v = ring_step(up_v, 1)
            down_k = ring_step(down_k, -1)
            held = [up_k, down_k, up_v, down_v]
        else:
            held = [up_k, down_v]
    held, _, parts, beside = lax.optimization_barrier((held, picks, parts, beside))
    weights[turn] = beside[0]
    parts = (global_parts(asking, held, parts),)
    arrived.append(over_plane(picked(asked, first, held, parts)))
    place = jnp.concatenate(
        [
            jnp.stack([my_index * blocks, jnp.int32(shards * blocks)]).astype(jnp.int32),
            jnp.where(mine, spot, -1).astype(jnp.int32),
        ]
    )
    acc, stats = attended(
        slots, place, queries, key_vectors, value_vectors, before, after, arrived[:-1]
    )
    own_t, own_b, gout = finished(late, queries, acc, stats, arrived[-1])
    gout = over_plane(gout).reshape(heads, GLOBAL * BLOCK, DH)
    gout = gout.transpose(1, 0, 2).reshape(GLOBAL * BLOCK, features)
    right_t, left_t = across(own_t, 1), across(own_t, -1)
    right_b, left_b = across(own_b, 1), across(own_b, -1)
    near_t, near_b, gout, _ = lax.optimization_barrier((right_t, left_b, gout, (left_t, right_b)))
    rows_g = (gout, across(gout, 1), across(gout, -1), across(gout, 2))
    far_t, far_b = across(near_t, 1), across(near_b, -1)
    top = product((own_t, right_t, left_t, far_t), weights)
    return product((own_b, right_b, left_b, far_b), weights, place, top, rows_g)


def solution(mesh):
    torus = Mesh(
        mesh.devices.reshape(mesh.shape["heads"], 8, 4, 2), ("heads", "seq_0", "seq_1", "seq_2")
    )
    in_specs = (
        P(SEQ, "heads"),
        P(SEQ, "heads"),
        P(SEQ, "heads"),
        P("heads", SEQ, None),
        P(),
        P("heads", None),
    )
    out_specs = P(SEQ, "heads")
    return jax.shard_map(
        on_device, mesh=torus, in_specs=in_specs, out_specs=out_specs, check_vma=False
    )
```

```python
import jax
import jax.numpy as jnp
from jax import lax
from jax.experimental import pallas as pl
from jax.experimental.pallas import tpu as pltpu
from jax.sharding import Mesh
from jax.sharding import PartitionSpec as P

DH = 128
BLOCK = 64
RANDOM = 3
GLOBAL = 2
CAP = 4
PLANES = 8
INPLANE = 8
SEQ = ("seq_0", "seq_1", "seq_2")
PLANE = ("seq_1", "seq_2")
VMEM_LIMIT = 56 * 2**20
COST = 24 * 2**20


def ring_step(shard, step):
    peers = lax.axis_size("seq_0")
    return lax.ppermute(shard, "seq_0", [(i, (i + step) % peers) for i in range(peers)])


def across(shard, step):
    peers = lax.axis_size("heads")
    return lax.ppermute(shard, "heads", [(i, (i + step) % peers) for i in range(peers)])


def pick_kernel(n, first, codes, *refs):
    keys, values = refs[:n], refs[n : 2 * n]
    extra, out = refs[2 * n : -1], refs[-1]

    def one_peer(peer, carry):
        for run in range(n):
            for rank in range(CAP):
                code = codes[(peer * PLANES + first + run) * CAP + rank]
                rows = pl.ds(pl.multiple_of((code & 15) * BLOCK, BLOCK), BLOCK)
                cols = pl.ds(pl.multiple_of((code >> 4) * DH, DH), DH)
                at = (run * CAP + rank) * 2 * BLOCK
                out[peer, at : at + BLOCK] = keys[run][rows, cols]
                out[peer, at + BLOCK : at + 2 * BLOCK] = values[run][rows, cols]
        at = n * CAP * 2 * BLOCK
        if extra and extra[0].shape[0] < BLOCK:
            few = extra[0].shape[0]
            for h in range(extra[0].shape[1] // DH):
                out[peer, at + h * few : at + (h + 1) * few] = extra[0][:, h * DH : (h + 1) * DH]
        elif extra:
            own = extra[0][pl.ds(pl.multiple_of(peer * BLOCK, BLOCK), BLOCK)].astype(out.dtype)
            out[peer, at : at + BLOCK] = own[:, :DH]
            out[peer, at + BLOCK : at + 2 * BLOCK] = own[:, DH:]
        return carry

    lax.fori_loop(0, INPLANE, one_peer, 0)


def picked(codes, first, blocks, extra=()):
    n = len(blocks) // 2
    tail = sum(e.size if e.shape[0] < BLOCK else e.size // INPLANE for e in extra) // DH
    shape = (INPLANE, n * CAP * 2 * BLOCK + tail, DH)
    size = 2 * (sum(k.size for k in blocks) + INPLANE * n * CAP * 2 * BLOCK * DH)
    vmem = pl.BlockSpec(memory_space=pltpu.VMEM)
    return pl.pallas_call(
        lambda *refs: pick_kernel(n, first, *refs),
        out_shape=jax.ShapeDtypeStruct(shape, jnp.bfloat16),
        in_specs=[pl.BlockSpec(memory_space=pltpu.SMEM)] + [vmem] * (2 * n + len(extra)),
        out_specs=vmem,
        compiler_params=pltpu.CompilerParams(vmem_limit_bytes=32 * 2**20),
        cost_estimate=pl.CostEstimate(flops=0, bytes_accessed=24 * 2**20, transcendentals=0),
        name="pick_blocks",
    )(codes, *blocks, *extra)


def over_plane(parts):
    return lax.all_to_all(parts, PLANE, split_axis=0, concat_axis=0, tiled=True)


def global_kernel(n, asking, *refs):
    keys, values = refs[:n], refs[n : 2 * n]
    held, out = refs[2 * n : -1], refs[-1]
    heads = asking.shape[1] // DH
    many = GLOBAL * BLOCK
    lane = lax.broadcasted_iota(jnp.int32, (many, DH), 1)
    for h in range(heads):
        hs = slice(h * DH, (h + 1) * DH)
        rows = slice(h * many, (h + 1) * many)
        scores = [
            lax.dot_general(
                asking[:, hs], k[:, hs], (((1,), (1,)), ((), ())),
                preferred_element_type=jnp.float32,
            ) * (DH ** (-0.5))
            for k in keys
        ]
        top = jnp.max(scores[0], axis=1, keepdims=True)
        for other in scores[1:]:
            top = jnp.maximum(top, jnp.max(other, axis=1, keepdims=True))
        top = top.astype(jnp.bfloat16).astype(jnp.float32)
        if held:
            before = held[0][rows, DH : DH + 1]
            top = jnp.maximum(top, before)
            scale = jnp.exp(before - top)
            part = held[0][rows, :DH] * scale
            total = held[0][rows, DH + 1 : DH + 2] * scale
        else:
            part = jnp.zeros((many, DH), jnp.float32)
            total = jnp.zeros((many, 1), jnp.float32)
        for score, v in zip(scores, values):
            weights = jnp.exp(score - top)
            total += jnp.sum(weights, axis=1, keepdims=True)
            part += jnp.dot(
                weights.astype(jnp.bfloat16), v[:, hs], preferred_element_type=jnp.float32
            )
        upper = total.astype(jnp.bfloat16).astype(jnp.float32)
        side = jnp.where(lane == 0, top, jnp.where(lane == 1, total, 0.0))
        side = jnp.where(lane == 2, upper, jnp.where(lane == 3, total - upper, side))
        out[rows] = jnp.concatenate([part, side], axis=1)


def global_parts(asking, blocks, held=()):
    n = len(blocks) // 2
    vmem = pl.BlockSpec(memory_space=pltpu.VMEM)
    rows = asking.shape[0] * asking.shape[1] // DH
    return pl.pallas_call(
        lambda *refs: global_kernel(n, *refs),
        out_shape=jax.ShapeDtypeStruct((rows, 2 * DH), jnp.float32),
        in_specs=[vmem] * (1 + len(blocks) + len(held)),
        out_specs=vmem,
        compiler_params=pltpu.CompilerParams(vmem_limit_bytes=32 * 2**20),
        cost_estimate=pl.CostEstimate(
            flops=4 * rows * DH * 768 * n, bytes_accessed=24 * 2**20, transcendentals=rows * 768 * n
        ),
        name="global_parts",
    )(asking, *blocks, *held)


def merge_rows(parts, first, out):
    peers = parts.shape[0]
    sums, side = slice(first, first + BLOCK), slice(first + BLOCK, first + 2 * BLOCK)
    tops = [parts[p, side, 0:1].astype(jnp.float32) for p in range(peers)]
    top = tops[0]
    for other in tops[1:]:
        top = jnp.maximum(top, other)
    part = jnp.zeros((BLOCK, DH), jnp.float32)
    total = jnp.zeros((BLOCK, 1), jnp.float32)
    for p, own in enumerate(tops):
        scale = jnp.exp(own - top)
        part += scale * parts[p, sums].astype(jnp.float32)
        upper = parts[p, side, 2:3].astype(jnp.float32)
        total += scale * (upper + parts[p, side, 3:4].astype(jnp.float32))
    whole = (part / total).astype(jnp.bfloat16)
    for p in range(peers):
        out[p] = whole


def times(pieces, weights):
    total = jnp.dot(pieces[0][...], weights[0][...], preferred_element_type=jnp.float32)
    for piece, weight in zip(pieces[1:], weights[1:]):
        total += jnp.dot(piece[...], weight[...], preferred_element_type=jnp.float32)
    return total.astype(jnp.bfloat16)


def upper_kernel(*refs):
    refs[8][...] = times(refs[:4], refs[4:8])


def lower_kernel(place, top, *refs):
    low, rows, weights, out = refs[:4], refs[4:8], refs[8:12], refs[12]
    half = top.shape[0]
    out[:half] = top[...]
    out[half:] = times(low, weights)
    replaced = times(rows, weights)
    for g in range(GLOBAL):

        @pl.when(place[2 + g] >= 0)
        def _():
            at_rows = pl.ds(pl.multiple_of(place[2 + g] * BLOCK, BLOCK), BLOCK)
            out[at_rows] = replaced[g * BLOCK : (g + 1) * BLOCK]


def product(pieces, weights, place=None, top=None, rows=()):
    features, width = weights[0].shape
    step = width // 4
    whole = [pl.BlockSpec(p.shape, lambda i: (0, 0)) for p in (*pieces, *rows)]
    sliced = [pl.BlockSpec((features, step), lambda i: (0, i))] * 4
    head = [] if top is None else [place, top]
    half = pieces[0].shape[0]
    tall = half if top is None else 2 * half
    specs = [] if top is None else [
        pl.BlockSpec(memory_space=pltpu.SMEM), pl.BlockSpec((half, step), lambda i: (0, i))
    ]
    return pl.pallas_call(
        upper_kernel if top is None else lower_kernel,
        out_shape=jax.ShapeDtypeStruct((tall, width), jnp.bfloat16),
        grid=(4,),
        in_specs=specs + whole + sliced,
        out_specs=pl.BlockSpec((tall, step), lambda i: (0, i)),
        compiler_params=pltpu.CompilerParams(vmem_limit_bytes=32 * 2**20),
        cost_estimate=pl.CostEstimate(
            flops=8 * half * features * width, bytes_accessed=8 * 2**20, transcendentals=0
        ),
        name="upper_product" if top is None else "lower_product",
    )(*head, *pieces, *rows, *weights)


def attend_kernel(counts, slots, place, q, k, v, before, after, *refs):
    n = len(counts)
    arrived, acc, stats, held, sems = refs[:n], refs[n], refs[n + 1], refs[n + 2], refs[n + 3]
    kpad, vpad = refs[n + 4], refs[n + 5]
    copies = []
    at = 0
    for part, count in enumerate(counts):
        copies.append(
            pltpu.make_async_copy(arrived[part], held.at[:, pl.ds(at, count)], sems.at[part])
        )
        copies[-1].start()
        at += count
    rows = q.shape[0]
    heads = q.shape[1] // DH
    blocks = rows // BLOCK
    for side, (pad, own) in enumerate(((kpad, k), (vpad, v))):
        pad[0:BLOCK] = before[side * BLOCK : (side + 1) * BLOCK]
        pad[BLOCK : BLOCK + rows] = own[...]
        pad[BLOCK + rows :] = after[side * BLOCK : (side + 1) * BLOCK]
    for copy in copies:
        copy.wait()
    scale = DH ** (-0.5)
    col = lax.broadcasted_iota(jnp.int32, (1, (3 + RANDOM + GLOBAL) * BLOCK), 1) // BLOCK
    lane = lax.broadcasted_iota(jnp.int32, (BLOCK, DH), 1)
    few = GLOBAL * 2 * BLOCK // INPLANE

    def one_block(b, carry):
        at_rows = pl.ds(pl.multiple_of(b * BLOCK, BLOCK), BLOCK)
        win_rows = pl.ds(pl.multiple_of(b * BLOCK, BLOCK), 3 * BLOCK)
        number = place[0] + b
        outside = jnp.where(number == 0, 0, -1), jnp.where(number == place[1] - 1, 2, -1)
        for pair in range(0, heads, 2):
            both = range(pair, pair + 2)
            found, scores = [], []
            for h in both:
                hs = slice(h * DH, (h + 1) * DH)
                picks = []
                bias = jnp.where((col == outside[0]) | (col == outside[1]), -jnp.inf, 0.0)
                for r in range(RANDOM):
                    slot = slots[(h * blocks + b) * RANDOM + r]
                    late = ((slot >> 2) & 7) == PLANES - 1
                    bias = jnp.where(col == jnp.where(late, 3 + r, -1), -jnp.inf, bias)
                    slot = jnp.where(late, 0, slot)
                    picks.append((slot >> 5, pl.multiple_of((slot & 31) * 2 * BLOCK, 2 * BLOCK)))
                found.append(picks)
                at = sum(counts) + (h - heads) * few
                keys = jnp.concatenate(
                    [kpad[win_rows, hs]]
                    + [held[p[0], pl.ds(p[1], BLOCK)] for p in picks]
                    + [held[4 * g + i, at : at + few] for g in range(GLOBAL) for i in range(2)],
                    axis=0,
                )
                scores.append(
                    lax.dot_general(
                        q[at_rows, hs], keys, (((1,), (1,)), ((), ())),
                        preferred_element_type=jnp.float32,
                    ) * scale + bias
                )
            peaks = [jnp.max(own, axis=1, keepdims=True) for own in scores]
            weights = [jnp.exp(own - peak) for own, peak in zip(scores, peaks)]
            totals = [jnp.sum(own, axis=1, keepdims=True) for own in weights]
            sums = []
            for h, picks, own in zip(both, found, weights):
                hs = slice(h * DH, (h + 1) * DH)
                at = sum(counts) + (h - heads) * few
                values = jnp.concatenate(
                    [vpad[win_rows, hs]]
                    + [held[p[0], pl.ds(p[1] + BLOCK, BLOCK)] for p in picks]
                    + [held[4 * g + 2 + i, at : at + few] for g in range(GLOBAL) for i in range(2)],
                    axis=0,
                )
                sums.append(
                    jnp.dot(own.astype(jnp.bfloat16), values, preferred_element_type=jnp.float32)
                )
            for h, own, peak, total in zip(both, sums, peaks, totals):
                acc[at_rows, h * DH : (h + 1) * DH] = own
                stats[h, at_rows] = jnp.where(lane < DH // 2, peak, total)
        return carry

    lax.fori_loop(0, blocks, one_block, 0)


def attended(slots, place, q, k, v, before, after, arrived):
    rows, features = q.shape
    counts = tuple(a.shape[1] for a in arrived)
    vmem = pl.BlockSpec(memory_space=pltpu.VMEM)
    smem = pl.BlockSpec(memory_space=pltpu.SMEM)
    return pl.pallas_call(
        lambda *refs: attend_kernel(counts, *refs),
        out_shape=(
            jax.ShapeDtypeStruct((rows, features), jnp.float32),
            jax.ShapeDtypeStruct((features // DH, rows, DH), jnp.float32),
        ),
        in_specs=[smem, smem] + [vmem] * 5 + [pl.BlockSpec(memory_space=pl.ANY)] * len(arrived),
        out_specs=(vmem, vmem),
        scratch_shapes=[
            pltpu.VMEM((INPLANE, sum(counts), DH), jnp.bfloat16),
            pltpu.SemaphoreType.DMA((len(arrived),)),
            pltpu.VMEM((rows + 2 * BLOCK, features), jnp.bfloat16),
            pltpu.VMEM((rows + 2 * BLOCK, features), jnp.bfloat16),
        ],
        compiler_params=pltpu.CompilerParams(vmem_limit_bytes=VMEM_LIMIT),
        cost_estimate=pl.CostEstimate(
            flops=4 * rows * features * 512, bytes_accessed=COST, transcendentals=rows * 4 * 512
        ),
        name="attend",
    )(slots, place, q, k, v, before, after, *arrived)


def finish_kernel(late, q, acc, stats, blocks_late, top, low, gout, summed, held):
    scale = DH ** (-0.5)
    lane = lax.broadcasted_iota(jnp.int32, (BLOCK, DH), 1)
    summed[...] = acc[...]
    held[...] = stats[...]

    def one_peer(peer, carry):
        found = []
        for rank in range(CAP):
            code = late[peer * CAP + rank]
            near = jnp.maximum(code, 0)
            at_rows = pl.ds(pl.multiple_of((near & 15) * BLOCK, BLOCK), BLOCK)
            cols = pl.ds(pl.multiple_of((near >> 4) * DH, DH), DH)
            scores = lax.dot_general(
                q[at_rows, cols], blocks_late[peer, 2 * rank * BLOCK : (2 * rank + 1) * BLOCK],
                (((1,), (1,)), ((), ())), preferred_element_type=jnp.float32,
            ) * scale
            found.append((code, near >> 4, at_rows, cols, scores))
        peaks = [jnp.max(own[-1], axis=1, keepdims=True) for own in found]
        weights = [jnp.exp(own[-1] - peak) for own, peak in zip(found, peaks)]
        totals = [jnp.sum(own, axis=1, keepdims=True) for own in weights]
        sums = [
            jnp.dot(
                own.astype(jnp.bfloat16),
                blocks_late[peer, (2 * rank + 1) * BLOCK : (2 * rank + 2) * BLOCK],
                preferred_element_type=jnp.float32,
            )
            for rank, own in enumerate(weights)
        ]
        for (code, h, at_rows, cols, _), peak, total, own in zip(found, peaks, totals, sums):

            @pl.when(code >= 0)
            def _():
                before = held[h, at_rows, 0:1]
                top = jnp.maximum(before, peak)
                less, more = jnp.exp(before - top), jnp.exp(peak - top)
                summed[at_rows, cols] = summed[at_rows, cols] * less + own * more
                both = held[h, at_rows, DH // 2 : DH // 2 + 1] * less + total * more
                held[h, at_rows] = jnp.where(lane < DH // 2, top, both)

        return carry

    lax.fori_loop(0, INPLANE, one_peer, 0)
    merge_rows(blocks_late, 2 * CAP * BLOCK, gout)
    half = top.shape[0]
    for side, out in enumerate((top, low)):

        def one_block(b, carry):
            to_rows = pl.ds(pl.multiple_of(b * BLOCK, BLOCK), BLOCK)
            at_rows = pl.ds(pl.multiple_of(b * BLOCK + side * half, BLOCK), BLOCK)
            for h in range(held.shape[0]):
                hs = slice(h * DH, (h + 1) * DH)
                total = held[h, at_rows, DH // 2 : DH // 2 + 1]
                out[to_rows, hs] = (summed[at_rows, hs] / total).astype(jnp.bfloat16)
            return carry

        lax.fori_loop(0, half // BLOCK, one_block, 0)


def finished(late, q, acc, stats, blocks_late):
    vmem = pl.BlockSpec(memory_space=pltpu.VMEM)
    rows, features = q.shape
    half = jax.ShapeDtypeStruct((rows // 2, features), jnp.bfloat16)
    return pl.pallas_call(
        finish_kernel,
        out_shape=(half, half, jax.ShapeDtypeStruct((INPLANE, BLOCK, DH), jnp.bfloat16)),
        in_specs=[pl.BlockSpec(memory_space=pltpu.SMEM)] + [vmem] * 4,
        out_specs=(vmem, vmem, vmem),
        scratch_shapes=[
            pltpu.VMEM(acc.shape, jnp.float32),
            pltpu.VMEM(stats.shape, jnp.float32),
        ],
        compiler_params=pltpu.CompilerParams(vmem_limit_bytes=32 * 2**20),
        name="late_blocks",
    )(late, q, acc, stats, blocks_late)


def on_device(queries, key_vectors, value_vectors, random_blocks, global_blocks, out_weight):
    shards = lax.axis_size(SEQ)
    my_index = lax.axis_index(SEQ)
    my_plane = lax.axis_index("seq_0")
    rows, features = queries.shape
    heads = features // DH
    blocks = rows // BLOCK
    requests = heads * blocks * RANDOM

    flat = random_blocks.reshape(requests)
    holders = flat // blocks
    number = jnp.arange(requests, dtype=jnp.int32)
    codes = (number // (blocks * RANDOM)) * 16 + flat % blocks
    earlier = (holders[:, None] == holders[None, :]) & (number[None, :] < number[:, None])
    rank = jnp.sum(earlier.astype(jnp.int32), axis=1)
    apart = (holders // INPLANE - my_plane) % PLANES
    order = jnp.where(apart <= PLANES // 2, jnp.minimum(2 * apart, PLANES - 1), 2 * PLANES - 1 - 2 * apart)
    slots = ((holders % INPLANE) * PLANES + order) * CAP + rank
    every = jnp.arange(INPLANE * PLANES * CAP, dtype=jnp.int32)
    asked = jnp.sum(jnp.where(slots[None, :] == every[:, None], codes[None, :], 0), axis=1)
    asker = number // RANDOM
    asker = (asker // blocks) * 16 + asker % blocks + 1
    late = jnp.sum(jnp.where(slots[None, :] == every[:, None], asker[None, :], 0), axis=1) - 1
    late = late.reshape(INPLANE, PLANES, CAP)[:, PLANES - 1].reshape(-1)
    asked = asked.astype(jnp.bfloat16).reshape(INPLANE, 1, PLANES * CAP)
    asked = jnp.pad(asked, ((0, 0), (0, 15), (0, features - PLANES * CAP)))

    holder = global_blocks // blocks
    spot = global_blocks % blocks
    mine = holder == my_index

    def cut(source, g):
        piece = lax.dynamic_slice_in_dim(source, spot[g] * BLOCK, BLOCK, axis=0)
        return jnp.where(mine[g], piece, jnp.zeros_like(piece))

    asking = jnp.concatenate([cut(queries, g) for g in range(GLOBAL)])
    shared = jnp.concatenate(
        [cut(source, g) for g in range(GLOBAL) for source in (key_vectors, value_vectors)]
    ).reshape(INPLANE, -1, features)
    asking = jnp.broadcast_to(asking[None], (INPLANE, *asking.shape))
    found = jnp.concatenate([asking, shared, asked], axis=1)
    up_k, down_v = ring_step(key_vectors, 1), ring_step(value_vectors, -1)
    up_v, down_k = ring_step(value_vectors, 1), ring_step(key_vectors, -1)
    me = lax.axis_index("heads")
    peers = lax.axis_size("heads")
    width = out_weight.shape[1] // peers
    weights = [
        lax.dynamic_slice_in_dim(out_weight, ((me + away) % peers) * width, width, axis=1)
        for away in (0, 1, -1, 2)
    ]
    ends = jnp.concatenate([key_vectors[rows - BLOCK :], value_vectors[rows - BLOCK :]])
    starts = jnp.concatenate([key_vectors[:BLOCK], value_vectors[:BLOCK]])
    found, ends, starts, weights, _, _ = lax.optimization_barrier(
        (found, ends, starts, weights, up_k, down_v)
    )
    found = over_plane(found)
    many = GLOBAL * BLOCK
    asking = found[:, :many].sum(axis=0)
    shared = found[:, many:-16].sum(axis=0)
    asked = found[:, -16, : PLANES * CAP].astype(jnp.int32).reshape(-1)

    picks, arrived = (), []
    ahead = [(i, i + 1) for i in range(shards - 1)]
    back = [(j, i) for i, j in ahead]

    def doubled(own, apart):
        return own + lax.ppermute(own, "seq_0", [(i, i ^ apart) for i in range(PLANES)])

    shared = doubled(shared, 1)
    first, parts = 0, ()
    beside = ()
    held = [key_vectors, up_k, down_k, value_vectors, up_v, down_v]
    first_pair = (up_v, down_k)
    for step in range(2, PLANES // 2 + 1):
        if step > 2:
            up_k, down_v, _ = lax.optimization_barrier((up_k, down_v, held if step == PLANES // 2 else first_pair))
        up_k = ring_step(up_k, 1)
        down_v = ring_step(down_v, -1)
        if step < PLANES // 2:
            up_v, down_k, _ = lax.optimization_barrier((up_v, down_k, picks))
        gate = (up_k, down_v) if step < PLANES // 2 else ()
        held, _, _, tied, early, shared = lax.optimization_barrier(
            (held, gate, arrived[-1:], beside if step > 2 else (), parts if step < 4 else (), shared)
        )
        parts = early if step < 4 else parts
        if step > 2:
            weights[turn] = tied[0]
        if step > 3:
            before, after = tied[1:]
        turn, away = ((3, 2), (1, 1), (2, -1))[step - 2]
        beside, _ = lax.optimization_barrier((weights[turn], held))
        beside = (across(beside, away),)
        if step == 3:
            ends, starts, _ = lax.optimization_barrier((ends, starts, held))
            beside += (lax.ppermute(ends, SEQ, ahead), lax.ppermute(starts, SEQ, back))
        if step == 3:
            shared, _ = lax.optimization_barrier((shared, held))
            shared = doubled(doubled(shared, 2), 4)
        picks = picked(asked, first, held, (shared,) if step == PLANES // 2 else ())
        arrived.append(over_plane(picks))
        first += len(held) // 2
        parts = (global_parts(asking, held, parts),)
        if step < PLANES // 2:
            up_v = ring_step(up_v, 1)
            down_k = ring_step(down_k, -1)
            held = [up_k, down_k, up_v, down_v]
        else:
            held = [up_k, down_v]
    held, _, parts, beside = lax.optimization_barrier((held, picks, parts, beside))
    weights[turn] = beside[0]
    parts = (global_parts(asking, held, parts),)
    arrived.append(over_plane(picked(asked, first, held, parts)))
    place = jnp.concatenate(
        [
            jnp.stack([my_index * blocks, jnp.int32(shards * blocks)]).astype(jnp.int32),
            jnp.where(mine, spot, -1).astype(jnp.int32),
        ]
    )
    acc, stats = attended(
        slots, place, queries, key_vectors, value_vectors, before, after, arrived[:-1]
    )
    own_t, own_b, gout = finished(late, queries, acc, stats, arrived[-1])
    right_t, left_t = across(own_t, 1), across(own_t, -1)
    right_b, left_b = across(own_b, 1), across(own_b, -1)
    far_t, far_b = across(right_t, 1), across(left_b, -1)
    gout = over_plane(gout).reshape(heads, GLOBAL * BLOCK, DH)
    gout = gout.transpose(1, 0, 2).reshape(GLOBAL * BLOCK, features)
    rows_g = (gout, across(gout, 1), across(gout, -1), across(gout, 2))
    top = product((own_t, right_t, left_t, far_t), weights)
    return product((own_b, right_b, left_b, far_b), weights, place, top, rows_g)


def solution(mesh):
    torus = Mesh(
        mesh.devices.reshape(mesh.shape["heads"], 8, 4, 2), ("heads", "seq_0", "seq_1", "seq_2")
    )
    in_specs = (
        P(SEQ, "heads"),
        P(SEQ, "heads"),
        P(SEQ, "heads"),
        P("heads", SEQ, None),
        P(),
        P("heads", None),
    )
    out_specs = P(SEQ, "heads")
    return jax.shard_map(
        on_device, mesh=torus, in_specs=in_specs, out_specs=out_specs, check_vma=False
    )
```
